128 devices in a mesh: dp: 2 (over z_lo), ty: 8 (over x, core), tz: 8 (over y, z_hi).
Axes of the slice: x: 4, y: 4, z: 4 (z_hi: 2, z_lo: 2; z = z_hi * 2 + z_lo), core: 2. Of those that a mesh axis runs over, the one named last changes fastest.
Arguments:
- fine_input: bfloat16 [2, 16, 2, 512, 1024], P('dp', None, None, 'ty', 'tz'), may hold values from -6 to 6
- fine_cotangent: bfloat16 [2, 16, 2, 512, 1024], P('dp', None, None, 'ty', 'tz'), may hold values from -6 to 6
- first_weight: bfloat16 [27, 16, 16], replicated, may hold values from -0.3125 to 0.3125
- second_weight: bfloat16 [27, 16, 16], replicated, may hold values from -0.3125 to 0.3125
- coarse_input: bfloat16 [2, 16, 64, 64, 128], P('dp', None, 'ty', 'tz'), may hold values from -6 to 6
- coarse_cotangent: bfloat16 [2, 16, 64, 64, 128], P('dp', None, 'ty', 'tz'), may hold values from -6 to 6
- coarse_weight: bfloat16 [27, 128, 128], replicated, may hold values from -0.109375 to 0.109375
Outputs:
- grad_fine_input: bfloat16 [2, 16, 2, 512, 1024], P('dp', None, None, 'ty', 'tz')
- grad_first: float32 [27, 16, 16], replicated
- grad_second: float32 [27, 16, 16], replicated
- grad_coarse_input: bfloat16 [2, 16, 64, 64, 128], P('dp', None, 'ty', 'tz')
- grad_coarse: float32 [128, 27, 128], P(('ty', 'tz'))
The draws below stay inside these ranges and needn't reach their ends.
All inputs are finite; a program needn't handle non-finite values.
Results may differ from the reference program's by a relative error of at most 0.0049.
Values may be sent and summed in bfloat16 or wider, within the bound.
A program may use at most 320 MiB of HBM per device.

```python
import jax
import jax.numpy as jnp
from jax import lax

CF = 16
CB = 128
SX = 2
BX = 16
BATCH = 2
NY = 512
NZ = 1024
BY = 64
BZ = 64


def spiked(result, key, source, target, blocks, factor):
    def block_of(position):
        return (jnp.arange(result.shape[position]) // (result.shape[position] // blocks)).reshape((-1,) + (1,) * (result.ndim - 1 - position))

    one_side = jax.random.permutation(key, blocks)[block_of(target)]
    second = (block_of(target) + blocks // 2) % blocks
    return jnp.where((block_of(source) == one_side) | (block_of(source) == second), factor * result, result)


def steps_of(key, dims, cuts, least, high):
    gain = 1.0
    for position, blocks in cuts:
        steps = jax.random.uniform(jax.random.fold_in(jax.random.fold_in(key, 6), position), (blocks,), jnp.float32, least / len(cuts), high / len(cuts))
        gain = gain * jnp.repeat(jnp.exp(steps), dims[position] // blocks).reshape((-1,) + (1,) * (len(dims) - 1 - position))
    return gain


def normal_values(stream_key, dims, scale, reach, shards=(), dtype=jnp.bfloat16):
    result = scale * jax.random.normal(stream_key, dims, jnp.float32)
    if shards:
        result = result * steps_of(stream_key, dims, shards, -0.22, 0.18)
    return jnp.clip(result, -reach, reach).astype(dtype)


def noise_with(key, dims, spread, reach, pieces, heavy, kind=jnp.bfloat16):
    result = spread * jax.random.normal(key, dims, jnp.float32)
    if pieces:
        result = result * steps_of(key, dims, pieces, -0.22, 0.18)
    return jnp.clip(spiked(result, jax.random.fold_in(key, 3), *heavy), -reach, reach).astype(kind)


def setup_inputs(seed: int = 0) -> dict:
    seeds = jax.random.split(jax.random.key(seed), 8)
    return {
        "fine_input": normal_values(seeds[0], (BATCH, CF, SX, NY, NZ), 1.0, 6.0, ((0, 2), (3, 8), (4, 8))),
        "fine_cotangent": normal_values(seeds[1], (BATCH, CF, SX, NY, NZ), 1.0, 6.0, ((0, 2), (3, 8), (4, 8))),
        "first_weight": normal_values(seeds[2], (27, CF, CF), (27 * CF) ** -0.5, 0.3125),
        "second_weight": normal_values(seeds[3], (27, CF, CF), (27 * CF) ** -0.5, 0.3125),
        "coarse_input": normal_values(seeds[4], (BATCH, BX, BY, BZ, CB), 1.0, 6.0, ((0, 2), (2, 8), (3, 8))),
        "coarse_cotangent": noise_with(seeds[5], (BATCH, BX, BY, BZ, CB), 1.0, 6.0, ((0, 2), (2, 8), (3, 8)), (2, 4, 8, 2.0)),
        "coarse_weight": normal_values(seeds[6], (27, CB, CB), (27 * CB) ** -0.5, 0.109375),
    }


def offsets():
    return [(kk // 9, kk // 3 % 3, kk % 3) for kk in range(27)]

def pad_first(values):
    return jnp.pad(values, ((0, 0), (1, 1), (1, 1), (1, 1)))

def forward_conv(source, weight):
    depth, height, width = (source.shape[1] - 2, source.shape[2] - 2, source.shape[3] - 2)
    summed = None
    for sx, sy, sz in offsets():
        window = source[:, sx:sx + depth, sy:sy + height, sz:sz + width].astype(jnp.float32)
        contrib = jnp.einsum('oc,cxyz->oxyz', weight[9 * sx + 3 * sy + sz].astype(jnp.float32), window)
        summed = contrib if summed is None else summed + contrib
    return summed

def transposed_conv(source, weight):
    depth, height, width = (source.shape[1] - 2, source.shape[2] - 2, source.shape[3] - 2)
    summed = None
    for sx, sy, sz in offsets():
        window = source[:, 2 - sx:2 - sx + depth, 2 - sy:2 - sy + height, 2 - sz:2 - sz + width].astype(jnp.float32)
        contrib = jnp.einsum('oc,oxyz->cxyz', weight[9 * sx + 3 * sy + sz].astype(jnp.float32), window)
        summed = contrib if summed is None else summed + contrib
    return summed

def weight_grad(cotangent, source):
    depth, height, width = (cotangent.shape[1], cotangent.shape[2], cotangent.shape[3])
    parts = []
    for sx, sy, sz in offsets():
        window = source[:, sx:sx + depth, sy:sy + height, sz:sz + width].astype(jnp.float32)
        parts.append(jnp.einsum('oxyz,cxyz->oc', cotangent.astype(jnp.float32), window))
    return jnp.stack(parts, 0)

def pad_last(values):
    return jnp.pad(values, ((1, 1), (1, 1), (1, 1), (0, 0)))

def transposed_last(source, weight):
    depth, height, width = (source.shape[0] - 2, source.shape[1] - 2, source.shape[2] - 2)
    summed = None
    for sx, sy, sz in offsets():
        window = source[2 - sx:2 - sx + depth, 2 - sy:2 - sy + height, 2 - sz:2 - sz + width].astype(jnp.float32)
        contrib = jnp.einsum('xyzo,oc->xyzc', window, weight[9 * sx + 3 * sy + sz].astype(jnp.float32))
        summed = contrib if summed is None else summed + contrib
    return summed

def weight_grad_last(cotangent, source):
    depth, height, width = (cotangent.shape[0], cotangent.shape[1], cotangent.shape[2])
    parts = []
    for sx, sy, sz in offsets():
        window = source[sx:sx + depth, sy:sy + height, sz:sz + width].astype(jnp.float32)
        parts.append(jnp.einsum('xyzo,xyzc->oc', cotangent.astype(jnp.float32), window))
    return jnp.stack(parts, 1)

def fine_sample(pair, first_weight, second_weight):
    source, cotangent = pair
    pre = forward_conv(pad_first(source), first_weight)
    act = jax.nn.gelu(pre).astype(jnp.bfloat16)
    dact = transposed_conv(pad_first(cotangent), second_weight)
    grad_two = weight_grad(cotangent, pad_first(act))
    dpre = jax.vjp(jax.nn.gelu, pre)[1](dact)[0].astype(jnp.bfloat16)
    grad_one = weight_grad(dpre, pad_first(source))
    grad_in = transposed_conv(pad_first(dpre), first_weight).astype(jnp.bfloat16)
    return (grad_in, grad_one, grad_two)

def coarse_sample(pair, coarse_weight):
    source, cotangent = pair
    grad_in = transposed_last(pad_last(cotangent), coarse_weight).astype(jnp.bfloat16)
    return (grad_in, weight_grad_last(cotangent, pad_last(source)))

def reference(fine_input, fine_cotangent, first_weight, second_weight, coarse_input, coarse_cotangent, coarse_weight):
    grad_fine_input, grads_one, grads_two = lax.map(lambda pair: fine_sample(pair, first_weight, second_weight), (fine_input, fine_cotangent))
    grad_coarse_input, grads_coarse = lax.map(lambda pair: coarse_sample(pair, coarse_weight), (coarse_input, coarse_cotangent))
    return (grad_fine_input, lax.optimization_barrier(jnp.sum(grads_one, 0)), lax.optimization_barrier(jnp.sum(grads_two, 0)), grad_coarse_input, lax.optimization_barrier(jnp.sum(grads_coarse, 0)))
```

```python
import functools

import jax
import jax.numpy as jnp
from jax import lax
from jax.experimental import pallas as pl
from jax.experimental.pallas import tpu as pltpu
from jax.sharding import PartitionSpec as P

MESH = pl.DeviceIdType.MESH
BF = jnp.bfloat16
F32 = jnp.float32
NN = (((1,), (0,)), ((), ()))
NT = (((1,), (1,)), ((), ()))
TN = (((0,), (0,)), ((), ()))
ROWS = 34 * 32
C0 = 0.7978845608028654
C1 = 0.044715


def mm(a, b, dims=NN):
    return lax.dot_general(a, b, dims, preferred_element_type=F32)


def iota(shape, dim):
    return lax.broadcasted_iota(jnp.int32, shape, dim)


def one_hot(cond):
    return jnp.where(cond, 1.0, 0.0).astype(BF)


def kernel(
    sizes,
    fin,
    fcot,
    w1,
    w1t,
    w2t,
    cin,
    ccot,
    wc,
    o_gfi,
    o_gf,
    o_gs,
    o_gci,
    o_gc,
    perm,
    shifts,
    xin,
    xcot,
    xdp,
    act,
    bands,
    ysend,
    yrecv,
    zsend,
    zrecv,
    dsend,
    drecv,
    ysend2,
    yrecv2,
    zsend2,
    zrecv2,
    cflat,
    cplus,
    cminus,
    vmat,
    inp3,
    rsend,
    rs1,
    qf,
    qb,
    rs2,
    acc1,
    acc2,
    fpart,
    ar1,
    fsum1,
    ar2,
    fsum2,
    gath,
    hs,
    hr,
    gs,
    gr,
    r1s,
    r1r,
    r2s,
    r2r,
    a1s,
    a1r,
    a2s,
    a2r,
    a3s,
    a3r,
):
    ndp, nty, ntz = sizes
    dp, ty, tz = lax.axis_index("dp"), lax.axis_index("ty"), lax.axis_index("tz")
    zgroup = ndp * ntz
    me = dp * ntz + tz

    def at(dy, dz):
        return (dp, lax.rem(ty + dy + nty, nty), lax.rem(tz + dz + ntz, ntz))

    def ty_peer(j):
        t = lax.rem(ty + j, nty)
        return t, (dp, t, tz)

    def z_peer(j):
        g = lax.rem(me + j, zgroup)
        z = lax.rem(g, ntz)
        return g, z, (lax.div(g, ntz), ty, z)

    def remote(src, dst, ssem, rsem, dev):
        return pltpu.make_async_remote_copy(
            src_ref=src,
            dst_ref=dst,
            send_sem=ssem,
            recv_sem=rsem,
            device_id=dev,
            device_id_type=MESH,
        )

    up = (ty > 0, ty < nty - 1)
    side = (tz > 0, tz < ntz - 1)

    barrier = pltpu.get_barrier_semaphore()
    partners = [at(dy, dz) for dy in (-1, 1) for dz in (-1, 1)]
    partners += [ty_peer(j)[1] for j in range(1, nty)]
    partners += [z_peer(j)[2] for j in range(1, zgroup)]
    for dev in partners:
        pl.semaphore_signal(barrier, inc=1, device_id=dev, device_id_type=MESH)

    r, c = iota((512, 512), 0), iota((512, 512), 1)
    perm[...] = one_hot(c == (r % 16) * 32 + ((r // 16) % 2) * 16 + r // 32)
    r, c = iota((128, 256), 0), iota((128, 256), 1)
    shifts[0] = one_hot(((r == c + 1) & (c < 127)) | ((r + 1 == c - 128) & (c > 128)))
    shifts[1] = one_hot((r == 0) & (c == 127))
    shifts[2] = one_hot((r == 127) & (c == 128))

    def relayout(src, dst):
        for j in range(2):
            left = src[:, 16 * j : 16 * j + 16, :].reshape(512, 128)
            right = src[:, 32 + 16 * j : 48 + 16 * j, :].reshape(512, 128)
            both = jnp.concatenate([left, right], 1)
            dst[0, 32 + 512 * j : 544 + 512 * j, :] = mm(perm[...], both).astype(BF)

    relayout(fin, xin)
    relayout(fcot, xcot)

    def pick(first):
        r, c = iota((16, 128), 0), iota((16, 128), 1)
        return one_hot(((r == first) & (c == 0)) | ((r == first + 1) & (c == 127)))

    for h in range(2):
        lanes = slice(128 * h, 128 * h + 128)
        edge = mm(pick(0), xin[0, 32:1056, lanes], NT) + mm(pick(2), xcot[0, 32:1056, lanes], NT)
        edge = edge.astype(BF)
        for j in range(8):
            rows = slice((8 * h + j) * 16, (8 * h + j) * 16 + 16)
            tile = edge[:, 128 * j : 128 * j + 128]
            zsend[0, rows, :] = tile
            zsend[1, rows, :] = tile

    for x in range(16):
        cflat[80 * x + 8 : 80 * x + 72, :] = ccot[64 * x : 64 * x + 64, :].astype(F32)

    def column(y, z):
        return cflat[pl.ds(8 * y + z, 16, stride=80), :]

    for y in range(8):
        zsend[0, 256 + 16 * y : 272 + 16 * y, :] = column(y + 1, 0).astype(BF)
        zsend[1, 256 + 16 * y : 272 + 16 * y, :] = column(y + 1, 7).astype(BF)
    for s in range(2):
        own = (slice(32, 64), slice(0, 128)) if s == 0 else (slice(1024, 1056), slice(128, 256))
        e_in, e_cot = xin[(0, *own)], xcot[(0, *own)]
        ysend[s, 0:32, :] = e_in
        ysend[s, 32:64, :] = e_cot
        first = 8 if s == 0 else 64
        for x in range(0, 16, 2):
            pair = [cflat[80 * (x + q) + first : 80 * (x + q) + first + 8, :] for q in range(2)]
            ysend[s, 64 + 8 * x : 80 + 8 * x, :] = jnp.concatenate(pair, 0).astype(BF)
        for t in range(2):
            dsend[s, t, 0:32, :] = e_in
            dsend[s, t, 32:64, :] = e_cot
            dsend[s, t, 64:80, :] = column(1 if s == 0 else 8, 0 if t == 0 else 7).astype(BF)

    pl.semaphore_wait(barrier, len(partners))

    step = (-1, 1)
    halo = []
    for s in range(2):
        halo.append(remote(ysend.at[s], yrecv.at[s], hs.at[s], hr.at[s], at(step[s], 0)))
        halo.append(remote(zsend.at[s], zrecv.at[s], hs.at[2 + s], hr.at[2 + s], at(0, step[s])))
        for t in range(2):
            q = 4 + 2 * s + t
            halo.append(
                remote(dsend.at[s, t], drecv.at[s, t], hs.at[q], hr.at[q], at(step[s], step[t]))
            )
    for copy in halo:
        copy.start()

    rl = one_hot(iota((16, 256), 1) % 16 == iota((16, 256), 0))
    lane = iota((16, 256), 1)
    for n, w in enumerate((w1, w2t, w1t)):
        wide = mm(w[...], rl)
        for cc in range(3):
            for xo in range(2):
                strip = jnp.zeros((16, 256), F32)
                for b in range(3):
                    for xi in range(2):
                        k = 9 * (xi - xo + 1) + 3 * b + cc
                        strip = jnp.where(
                            lane // 16 == 2 * b + xi, wide[16 * k : 16 * k + 16, :], strip
                        )
                for yo in range(4):
                    moved = strip if yo == 0 else pltpu.roll(strip, 32 * yo, 1)
                    first = 32 * yo + 16 * xo
                    bands[n, cc, first : first + 16, :] = moved.astype(BF)

    inp3[...] = jnp.zeros_like(inp3)
    for a in range(3):
        inp3[64 * (2 - a) : 64 * (2 - a) + 1024, 128 * a : 128 * a + 128] = cin[...]
    vmat[0] = jnp.zeros((64, 1152), BF)
    vmat[17] = jnp.zeros((64, 1152), BF)
    qf[...] = jnp.zeros_like(qf)

    for copy in halo:
        copy.wait()

    def valid(cond, value):
        return jnp.where(cond, value, jnp.zeros_like(value))

    for x in range(16):
        rows = slice(64 + 8 * (x // 2 * 2), 80 + 8 * (x // 2 * 2))
        half = slice(8 * (x % 2), 8 * (x % 2) + 8)
        cflat[80 * x : 80 * x + 8, :] = valid(up[0], yrecv[1, rows, :].astype(F32)[half])
        cflat[80 * x + 72 : 80 * x + 80, :] = valid(up[1], yrecv[0, rows, :].astype(F32)[half])
    cplus[...] = pltpu.roll(cflat[...], 1279, 0)
    cminus[...] = pltpu.roll(cflat[...], 1, 0)
    for y in range(10):
        for ref, z, t, ok in ((cplus, 7, 0, side[1]), (cminus, 0, 1, side[0])):
            if y == 0:
                part, ok = drecv[1, t, 64:80, :], ok & up[0]
            elif y == 9:
                part, ok = drecv[0, t, 64:80, :], ok & up[1]
            else:
                part = zrecv[t, 256 + 16 * (y - 1) : 272 + 16 * (y - 1), :]
            ref[pl.ds(8 * y + z, 16, stride=80), :] = valid(ok, part.astype(F32))

    def spread(x, carry):
        for b in range(3):
            for cc, ref in enumerate((cplus, cflat, cminus)):
                rows = ref[pl.ds(pl.multiple_of(x * 80 + 8 * (2 - b), 8), 64), :]
                q = 3 * b + cc
                vmat[x + 1, :, 128 * q : 128 * q + 128] = rows.astype(BF)
        return carry

    lax.fori_loop(0, 16, spread, 0)

    for b in range(3):
        left = vmat[:, :, 384 * b : 384 * b + 384].reshape(1152, 384)
        g = mm(left, inp3[...], TN)
        for cc in range(3):
            for a in range(3):
                rsend[9 * a + 3 * b + cc] = g[
                    128 * cc : 128 * cc + 128, 128 * a : 128 * a + 128
                ].astype(BF)
    wide_o = 128 // nty

    def part1(t):
        return rsend.at[:, pl.ds(pl.multiple_of(t * wide_o, 16), wide_o), :]

    hop1 = []
    for j in range(1, nty):
        t, dev = ty_peer(j)
        hop1.append(remote(part1(t), rs1.at[ty], r1s.at[j], r1r.at[nty - j], dev))
    for copy in hop1:
        copy.start()

    def fill(dst, first, get_y, get_d, get_z):
        pieces, halves = [], []
        for s in (1, 0):
            ok = up[0] if s == 1 else up[1]
            mid = valid(ok, get_y(s))
            after, before = valid(ok & side[1], get_d(s, 0)), valid(ok & side[0], get_d(s, 1))
            out = mm(mid, shifts[0]) + mm(after, shifts[1]) + mm(before, shifts[2])
            rows, lanes = (slice(0, 32), slice(0, 128)) if s == 1 else (slice(1056, 1088), slice(128, 256))
            dst[0, rows, lanes] = mid
            dst[2, rows, lanes] = out[:, :128].astype(BF)
            dst[1, rows, lanes] = out[:, 128:].astype(BF)
        r, c = iota((32, 256), 0), iota((32, 256), 1)
        place = one_hot(
            ((r == first) & (c == 127) & side[1]) | ((r == 17 + first) & (c == 128) & side[0])
        )
        for h in range(2):
            lanes = slice(128 * h, 128 * h + 128)
            for j in range(8):
                rows = slice(32 + 128 * j, 160 + 128 * j)
                got = slice((8 * h + j) * 16, (8 * h + j) * 16 + 16)
                edge = jnp.concatenate([get_z(0, got), get_z(1, got)], 0)
                out = mm(dst[0, rows, lanes], shifts[0]) + mm(edge, place, TN)
                dst[2, rows, lanes] = out[:, :128].astype(BF)
                dst[1, rows, lanes] = out[:, 128:].astype(BF)
        for v in range(3):
            dst[v, 0:32, 128:256] = dst[v, 1024:1056, 0:128]
            dst[v, 1056:1088, 0:128] = dst[v, 32:64, 128:256]

    for n, dst in enumerate((xin, xcot)):
        rows = slice(32 * n, 32 * n + 32)
        fill(
            dst,
            2 * n,
            lambda s, rows=rows: yrecv[s, rows, :],
            lambda s, t, rows=rows: drecv[s, t, rows, :],
            lambda t, got: zrecv[t, got, :],
        )

    version = (1, 0, 2)

    def conv(n, src, g):
        rows = pl.ds(pl.multiple_of(g * 128, 128), 192)
        out = None
        for cc in range(3):
            term = mm(bands[n, cc, :, 0:192], src[version[cc], rows, :])
            out = term if out is None else out + term
        return out

    def forward(g, carry):
        pre = conv(0, xin, g)
        dact = conv(1, xcot, g)
        square = pre * pre
        t = jnp.tanh(C0 * pre * (1.0 + C1 * square))
        half = 0.5 + 0.5 * t
        slope = half + 0.5 * pre * (1.0 - t * t) * (C0 * (1.0 + (3.0 * C1) * square))
        act[pl.ds(pl.multiple_of(g * 128, 128), 128), :] = (pre * half).astype(BF)
        xdp[0, pl.ds(pl.multiple_of(g * 128 + 32, 32), 128), :] = (dact * slope).astype(BF)
        return carry

    lax.fori_loop(0, 8, forward, 0)

    for h in range(2):
        lanes = slice(128 * h, 128 * h + 128)
        edge = mm(pick(0), xdp[0, 32:1056, lanes], NT).astype(BF)
        for j in range(8):
            rows = slice((8 * h + j) * 16, (8 * h + j) * 16 + 16)
            zsend2[rows, :] = edge[:, 128 * j : 128 * j + 128]
    ysend2[0] = xdp[0, 32:64, 0:128]
    ysend2[1] = xdp[0, 1024:1056, 128:256]
    halo2 = []
    for s in range(2):
        halo2.append(remote(ysend2.at[s], yrecv2.at[s, 0], gs.at[s], gr.at[s], at(step[s], 0)))
        halo2.append(remote(zsend2, zrecv2.at[s], gs.at[2 + s], gr.at[2 + s], at(0, step[s])))
        for t in range(2):
            q = 4 + 2 * s + t
            halo2.append(
                remote(ysend2.at[s], yrecv2.at[s, 1 + t], gs.at[q], gr.at[q], at(step[s], step[t]))
            )
    for copy in halo2:
        copy.start()

    acc1[...] = jnp.zeros_like(acc1)
    acc2[...] = jnp.zeros_like(acc2)

    def gram(g, carry):
        rows = pl.ds(pl.multiple_of(g * 128, 128), 192)
        own = xdp[0, pl.ds(pl.multiple_of(g * 128 + 32, 32), 128), :]
        a_own = act[pl.ds(pl.multiple_of(g * 128, 128), 128), :]
        for cc in range(3):
            acc1[cc, :, 0:192] += mm(own, xin[version[cc], rows, :], NT)
            acc2[cc] += mm(xcot[version[cc], rows, :], a_own, NT)
        return carry

    lax.fori_loop(0, 8, gram, 0)
    for cc in range(3):
        total = None
        for yo in range(4):
            part = acc1[cc, 32 * yo : 32 * yo + 32, :]
            part = part if yo == 0 else pltpu.roll(part, 256 - 32 * yo, 1)
            total = part if total is None else total + part
        fpart[32 * cc : 32 * cc + 32, :] = total[:, 0:128]
    total = jnp.zeros((96, 128), F32)
    lane = iota((96, 128), 1)
    for cc in range(3):
        band = None
        for yo in range(4):
            part = acc2[cc, 32 * yo : 32 * yo + 96, :]
            turn = (32 * cc - 32 * yo) % 128
            part = part if turn == 0 else pltpu.roll(part, turn, 1)
            band = part if band is None else band + part
        total = jnp.where(lane // 32 == cc, band, total)
    fpart[96:192, :] = total

    slab = 192 // nty
    hop_a = []
    for j in range(1, nty):
        t, dev = ty_peer(j)
        src = fpart.at[pl.ds(pl.multiple_of(t * slab, 8), slab), :]
        hop_a.append(remote(src, ar1.at[ty], a1s.at[j], a1r.at[nty - j], dev))
    for copy in hop_a:
        copy.start()
    ar1[ty] = fpart[pl.ds(pl.multiple_of(ty * slab, 8), slab), :]

    rs1[ty] = rsend[:, pl.ds(pl.multiple_of(ty * wide_o, 16), wide_o), :]
    for copy in hop1:
        copy.wait()

    def sum1(k, carry):
        total = rs1[0, k].astype(F32)
        for t in range(1, nty):
            total = total + rs1[t, k].astype(F32)
        qf[pl.ds(k, wide_o, stride=32), :] = total
        return carry

    lax.fori_loop(0, 27, sum1, 0)
    qb[...] = qf[...].astype(BF)
    deep = 32 * wide_o // ntz

    hop2 = []
    for j in range(1, zgroup):
        g, z, dev = z_peer(j)
        src = qb.at[pl.ds(pl.multiple_of(z * deep, 16), deep), :]
        hop2.append(remote(src, rs2.at[me], r2s.at[j], r2r.at[zgroup - j], dev))
    for copy in hop2:
        copy.start()
    rs2[me] = qb[pl.ds(pl.multiple_of(tz * deep, 16), deep), :]

    for copy in hop_a:
        copy.wait()
    total = ar1[0]
    for t in range(1, nty):
        total = total + ar1[t]
    fsum1[...] = total
    hop_b = []
    for j in range(1, zgroup):
        g, z, dev = z_peer(j)
        hop_b.append(remote(fsum1, ar2.at[me], a2s.at[j], a2r.at[zgroup - j], dev))
    for copy in hop_b:
        copy.start()
    ar2[me] = fsum1[...]

    def coarse(q, carry):
        out = None
        for a in range(3):
            left = vmat[pl.ds(q * 4 + 2 - a, 4)].reshape(256, 1152)
            term = mm(left, wc[1152 * a : 1152 * a + 1152, :])
            out = term if out is None else out + term
        o_gci[pl.ds(pl.multiple_of(q * 256, 256), 256), :] = out.astype(BF)
        return carry

    lax.fori_loop(0, 4, coarse, 0)

    for copy in hop_b:
        copy.wait()
    total = ar2[0]
    for t in range(1, zgroup):
        total = total + ar2[t]
    fsum2[...] = total
    hop_c = []
    for j in range(1, nty):
        t, dev = ty_peer(j)
        hop_c.append(remote(fsum2, gath.at[ty], a3s.at[j], a3r.at[nty - j], dev))
    for copy in hop_c:
        copy.start()
    gath[ty] = fsum2[...]

    for copy in halo2:
        copy.wait()
    fill(
        xdp,
        0,
        lambda s: yrecv2[s, 0],
        lambda s, t: yrecv2[s, 1 + t],
        lambda t, got: zrecv2[t, got, :],
    )

    def last(j, carry):
        parts = [conv(2, xdp, 4 * j + q).astype(BF) for q in range(4)]
        out = mm(perm[...], jnp.concatenate(parts, 0)).astype(BF)
        first = pl.multiple_of(16 * j, 16)
        o_gfi[:, pl.ds(first, 16), :] = out[:, :128].reshape(32, 16, 128)
        o_gfi[:, pl.ds(first + 32, 16), :] = out[:, 128:].reshape(32, 16, 128)
        return carry

    lax.fori_loop(0, 2, last, 0)

    for copy in hop2:
        copy.wait()
    total = rs2[0].astype(F32)
    for t in range(1, zgroup):
        total = total + rs2[t].astype(F32)
    for o in range(wide_o // ntz):
        o_gc[o] = total[32 * o : 32 * o + 27, :]

    for copy in hop_c:
        copy.wait()
    fpart[...] = gath[...].reshape(192, 128)
    for a in range(3):
        planes = [(xo, xo + a - 1) for xo in range(2) if 0 <= xo + a - 1 < 2]
        for b in range(3):
            for cc in range(3):
                k = 9 * a + 3 * b + cc
                one, two = None, None
                for xo, xi in planes:
                    first = 32 * cc + 16 * xo
                    lanes = slice(32 * b + 16 * xi, 32 * b + 16 * xi + 16)
                    part = fpart[first : first + 16, lanes]
                    one = part if one is None else one + part
                    first = 96 + 32 * b + 16 * xi
                    lanes = slice(32 * cc + 16 * xo, 32 * cc + 16 * xo + 16)
                    part = fpart[first : first + 16, lanes]
                    two = part if two is None else two + part
                o_gf[k] = one
                o_gs[26 - k] = two


def solution(mesh):
    sizes = tuple(mesh.shape[a] for a in ("dp", "ty", "tz"))
    ndp, nty, ntz = sizes
    zgroup = ndp * ntz
    wide_o = 128 // nty
    slab = 192 // nty

    def per_device(fine_input, fine_cotangent, first_weight, second_weight, coarse_input, coarse_cotangent, coarse_weight):
        def turned(w):
            return w[::-1].transpose(0, 2, 1).reshape(432, 16)

        dma = pltpu.SemaphoreType.DMA
        scratch = [
            pltpu.VMEM((512, 512), BF),
            pltpu.VMEM((3, 128, 256), BF),
            pltpu.VMEM((3, ROWS, 256), BF),
            pltpu.VMEM((3, ROWS, 256), BF),
            pltpu.VMEM((3, ROWS, 256), BF),
            pltpu.VMEM((1024, 256), BF),
            pltpu.VMEM((3, 3, 128, 256), BF),
            pltpu.VMEM((2, 192, 128), BF),
            pltpu.VMEM((2, 192, 128), BF),
            pltpu.VMEM((2, 384, 128), BF),
            pltpu.VMEM((2, 384, 128), BF),
            pltpu.VMEM((2, 2, 80, 128), BF),
            pltpu.VMEM((2, 2, 80, 128), BF),
            pltpu.VMEM((2, 32, 128), BF),
            pltpu.VMEM((2, 3, 32, 128), BF),
            pltpu.VMEM((256, 128), BF),
            pltpu.VMEM((2, 256, 128), BF),
            pltpu.VMEM((1280, 128), F32),
            pltpu.VMEM((1280, 128), F32),
            pltpu.VMEM((1280, 128), F32),
            pltpu.VMEM((18, 64, 1152), BF),
            pltpu.VMEM((1152, 384), BF),
            pltpu.VMEM((27, 128, 128), BF),
            pltpu.VMEM((nty, 27, wide_o, 128), BF),
            pltpu.VMEM((32 * wide_o, 128), F32),
            pltpu.VMEM((32 * wide_o, 128), BF),
            pltpu.VMEM((zgroup, 32 * wide_o // ntz, 128), BF),
            pltpu.VMEM((3, 128, 256), F32),
            pltpu.VMEM((3, 192, 128), F32),
            pltpu.VMEM((192, 128), F32),
            pltpu.VMEM((nty, slab, 128), F32),
            pltpu.VMEM((slab, 128), F32),
            pltpu.VMEM((zgroup, slab, 128), F32),
            pltpu.VMEM((slab, 128), F32),
            pltpu.VMEM((nty, slab, 128), F32),
            dma((8,)),
            dma((8,)),
            dma((8,)),
            dma((8,)),
            dma((nty,)),
            dma((nty,)),
            dma((zgroup,)),
            dma((zgroup,)),
            dma((nty,)),
            dma((nty,)),
            dma((zgroup,)),
            dma((zgroup,)),
            dma((nty,)),
            dma((nty,)),
        ]
        vmem = pl.BlockSpec(memory_space=pltpu.VMEM)
        outs = pl.pallas_call(
            functools.partial(kernel, sizes),
            out_shape=(
                jax.ShapeDtypeStruct((32, 64, 128), BF),
                jax.ShapeDtypeStruct((27, 16, 16), F32),
                jax.ShapeDtypeStruct((27, 16, 16), F32),
                jax.ShapeDtypeStruct((1024, 128), BF),
                jax.ShapeDtypeStruct((wide_o // ntz, 27, 128), F32),
            ),
            in_specs=[vmem] * 8,
            out_specs=(vmem,) * 5,
            scratch_shapes=scratch,
            compiler_params=pltpu.CompilerParams(
                collective_id=0, has_side_effects=True, vmem_limit_bytes=48 * 1024 * 1024
            ),
        )(
            fine_input.reshape(32, 64, 128),
            fine_cotangent.reshape(32, 64, 128),
            first_weight.reshape(432, 16),
            turned(first_weight),
            turned(second_weight),
            coarse_input.reshape(1024, 128),
            coarse_cotangent.reshape(1024, 128),
            coarse_weight.reshape(3456, 128),
        )
        return (
            outs[0].reshape(fine_input.shape),
            outs[1],
            outs[2],
            outs[3].reshape(coarse_input.shape),
            outs[4],
        )

    fine = P("dp", None, None, "ty", "tz")
    wide = P("dp", None, "ty", "tz", None)
    return jax.shard_map(
        per_device,
        mesh=mesh,
        in_specs=(fine, fine, P(), P(), wide, wide, P()),
        out_specs=(fine, P(), P(), wide, P(("ty", "tz"), None, None)),
        check_vma=False,
    )
```

```python
import functools

import jax
import jax.numpy as jnp
from jax import lax
from jax.experimental import pallas as pl
from jax.experimental.pallas import tpu as pltpu
from jax.sharding import PartitionSpec as P

MESH = pl.DeviceIdType.MESH
BF = jnp.bfloat16
F32 = jnp.float32
NN = (((1,), (0,)), ((), ()))
NT = (((1,), (1,)), ((), ()))
TN = (((0,), (0,)), ((), ()))
ROWS = 34 * 32
C0 = 0.7978845608028654
C1 = 0.044715


def mm(a, b, dims=NN):
    return lax.dot_general(a, b, dims, preferred_element_type=F32)


def iota(shape, dim):
    return lax.broadcasted_iota(jnp.int32, shape, dim)


def one_hot(cond):
    return jnp.where(cond, 1.0, 0.0).astype(BF)


def kernel(
    sizes,
    h_fin,
    h_fcot,
    h_w1,
    h_w2,
    h_cin,
    h_ccot,
    h_wc,
    o_gfi,
    o_gf,
    o_gs,
    o_gci,
    o_gc,
    fin,
    fcot,
    w1,
    w2,
    cin,
    ccot,
    wc,
    perm,
    shifts,
    xin,
    xcot,
    xdp,
    act,
    bands,
    ysend,
    yrecv,
    zsend,
    zrecv,
    dsend,
    drecv,
    ysend2,
    yrecv2,
    zsend2,
    zrecv2,
    drecv2,
    cflat,
    cplus,
    cminus,
    vmat,
    inp3,
    rsend,
    rpair,
    psum,
    rs1,
    qf,
    qb,
    rs2,
    acc1,
    acc2,
    fpart,
    ar1,
    fsum1,
    ar2,
    fsum2,
    gath,
    ls,
    hs,
    hr,
    ps,
    pr,
    gs,
    gr,
    r1s,
    r1r,
    r2s,
    r2r,
    a1s,
    a1r,
    a2s,
    a2r,
    a3s,
    a3r,
):
    ndp, nty, ntz = sizes
    dp, ty, tz = lax.axis_index("dp"), lax.axis_index("ty"), lax.axis_index("tz")
    zgroup = ndp * ntz
    me = dp * ntz + tz

    def at(dy, dz):
        return (dp, lax.rem(ty + dy + nty, nty), lax.rem(tz + dz + ntz, ntz))

    def ty_peer(j):
        t = lax.rem(ty + j, nty)
        return t, (dp, t, tz)

    def z_peer(j):
        g = lax.rem(me + j, zgroup)
        z = lax.rem(g, ntz)
        return g, z, (lax.div(g, ntz), ty, z)

    def remote(src, dst, ssem, rsem, dev):
        return pltpu.make_async_remote_copy(
            src_ref=src,
            dst_ref=dst,
            send_sem=ssem,
            recv_sem=rsem,
            device_id=dev,
            device_id_type=MESH,
        )

    loads = []
    pairs = ((h_ccot, ccot), (h_fin, fin), (h_fcot, fcot), (h_w1, w1), (h_w2, w2), (h_cin, cin), (h_wc, wc))
    for n, (src, dst) in enumerate(pairs):
        loads.append(pltpu.make_async_copy(src, dst, ls.at[n]))
        loads[n].start()

    up = (ty > 0, ty < nty - 1)
    side = (tz > 0, tz < ntz - 1)

    barrier = pltpu.get_barrier_semaphore()
    partners = [at(dy, dz) for dy in (-1, 1) for dz in (-1, 1)]
    partners += [ty_peer(j)[1] for j in range(1, nty)]
    partners += [z_peer(j)[2] for j in range(1, zgroup)]
    for dev in partners:
        pl.semaphore_signal(barrier, inc=1, device_id=dev, device_id_type=MESH)

    r, c = iota((512, 512), 0), iota((512, 512), 1)
    perm[...] = one_hot(c == (r % 16) * 32 + ((r // 16) % 2) * 16 + r // 32)
    r, c = iota((128, 256), 0), iota((128, 256), 1)
    shifts[...] = one_hot(((r == c + 1) & (c < 127)) | ((r + 1 == c - 128) & (c > 128)))

    def relayout(src, dst):
        for j in range(2):
            left = src[:, 16 * j : 16 * j + 16, :].reshape(512, 128)
            right = src[:, 32 + 16 * j : 48 + 16 * j, :].reshape(512, 128)
            both = jnp.concatenate([left, right], 1)
            dst[0, 32 + 512 * j : 544 + 512 * j, :] = mm(perm[...], both).astype(BF)

    def extract(src):
        r, c = iota((32, 256), 0), iota((32, 256), 1)
        total = None
        for j in range(8):
            sel = one_hot((r % 16 == 8 * (c // 128) + j) & (c % 128 == 127 * (r // 16)))
            part = mm(sel, src[0, 32 + 128 * j : 160 + 128 * j, :], NT)
            total = part if total is None else total + part
        return total.astype(BF)

    loads[1].wait()
    relayout(fin, xin)
    loads[2].wait()
    relayout(fcot, xcot)
    for n, src in enumerate((xin, xcot)):
        columns = extract(src)
        for t in range(2):
            tile = columns[16 * t : 16 * t + 16, :]
            zsend[t, 16 * n : 16 * n + 16, :] = tile
            for q in range(2):
                dsend[q, t, 16 * n : 16 * n + 16, :] = tile

    loads[0].wait()
    for x in range(16):
        cflat[80 * x + 8 : 80 * x + 72, :] = ccot[64 * x : 64 * x + 64, :].astype(F32)

    def column(y, z):
        return cflat[pl.ds(8 * y + z, 16, stride=80), :]

    for y in range(8):
        zsend[0, 32 + 16 * y : 48 + 16 * y, :] = column(y + 1, 0).astype(BF)
        zsend[1, 32 + 16 * y : 48 + 16 * y, :] = column(y + 1, 7).astype(BF)
    for s in range(2):
        own = (slice(32, 64), slice(0, 128)) if s == 0 else (slice(1024, 1056), slice(128, 256))
        ysend[s, 0:32, :] = xin[(0, *own)]
        ysend[s, 32:64, :] = xcot[(0, *own)]
        first = 8 if s == 0 else 64
        for x in range(0, 16, 2):
            pair = [cflat[80 * (x + q) + first : 80 * (x + q) + first + 8, :] for q in range(2)]
            ysend[s, 64 + 8 * x : 80 + 8 * x, :] = jnp.concatenate(pair, 0).astype(BF)
        for t in range(2):
            dsend[s, t, 32:48, :] = column(1 if s == 0 else 8, 0 if t == 0 else 7).astype(BF)

    pl.semaphore_wait(barrier, len(partners))

    step = (-1, 1)
    halo = []
    for s in range(2):
        halo.append(remote(ysend.at[s], yrecv.at[s], hs.at[s], hr.at[s], at(step[s], 0)))
        halo.append(remote(zsend.at[s], zrecv.at[s], hs.at[2 + s], hr.at[2 + s], at(0, step[s])))
        for t in range(2):
            q = 4 + 2 * s + t
            halo.append(
                remote(dsend.at[s, t], drecv.at[s, t], hs.at[q], hr.at[q], at(step[s], step[t]))
            )
    for copy in halo:
        copy.start()

    lane = iota((32, 768), 1)
    q, m = lane // 128, lane % 128
    k = 9 * ((m // 16) % 2 - q % 2 + 1) + 3 * (m // 32) + q // 2
    wanted = (m < 96, iota((32, 768), 0))
    straight = one_hot(wanted[0] & (wanted[1] == k))[:27]
    flipped = one_hot(wanted[0] & (wanted[1] == 26 - k))[:27]
    r, c = iota((256, 768), 0), iota((256, 768), 1)
    to_in, to_out = r % 16 == c % 16, r // 16 == c % 16
    r, c = iota((16, 256), 0), iota((16, 256), 1)
    by_out, by_in = one_hot(c // 16 == r), one_hot(c % 16 == r)
    loads[3].wait()
    loads[4].wait()
    for n, (w, pick, mask, rows) in enumerate(
        (
            (w1, straight, to_in, by_out),
            (w2, flipped, to_out, by_in),
            (w1, flipped, to_out, by_in),
        )
    ):
        wide = jnp.where(mask, mm(w[...], pick), 0.0).astype(BF)
        strips = mm(rows, wide)
        for cc in range(3):
            for xo in range(2):
                first = 128 * (2 * cc + xo)
                strip = strips[:, first : first + 128]
                strip = jnp.concatenate([strip, jnp.zeros_like(strip)], 1)
                for yo in range(4):
                    moved = strip if yo == 0 else pltpu.roll(strip, 32 * yo, 1)
                    first = 32 * yo + 16 * xo
                    bands[n, cc, first : first + 16, :] = moved.astype(BF)

    inp3[...] = jnp.zeros_like(inp3)
    loads[5].wait()
    for a in range(3):
        inp3[64 * (2 - a) : 64 * (2 - a) + 1024, 128 * a : 128 * a + 128] = cin[...]
    vmat[0] = jnp.zeros((64, 1152), BF)
    vmat[17] = jnp.zeros((64, 1152), BF)
    qf[...] = jnp.zeros_like(qf)

    for copy in halo:
        copy.wait()

    def valid(cond, value):
        return jnp.where(cond, value, jnp.zeros_like(value))

    for x in range(16):
        rows = slice(64 + 8 * (x // 2 * 2), 80 + 8 * (x // 2 * 2))
        half = slice(8 * (x % 2), 8 * (x % 2) + 8)
        cflat[80 * x : 80 * x + 8, :] = valid(up[0], yrecv[1, rows, :].astype(F32)[half])
        cflat[80 * x + 72 : 80 * x + 80, :] = valid(up[1], yrecv[0, rows, :].astype(F32)[half])
    cplus[...] = pltpu.roll(cflat[...], 1279, 0)
    cminus[...] = pltpu.roll(cflat[...], 1, 0)
    for y in range(10):
        for ref, z, t, ok in ((cplus, 7, 0, side[1]), (cminus, 0, 1, side[0])):
            if y == 0:
                part, ok = drecv[1, t, 32:48, :], ok & up[0]
            elif y == 9:
                part, ok = drecv[0, t, 32:48, :], ok & up[1]
            else:
                part = zrecv[t, 32 + 16 * (y - 1) : 48 + 16 * (y - 1), :]
            ref[pl.ds(8 * y + z, 16, stride=80), :] = valid(ok, part.astype(F32))

    def spread(x, carry):
        for b in range(3):
            for cc, ref in enumerate((cplus, cflat, cminus)):
                rows = ref[pl.ds(pl.multiple_of(x * 80 + 8 * (2 - b), 8), 64), :]
                q = 3 * b + cc
                vmat[x + 1, :, 128 * q : 128 * q + 128] = rows.astype(BF)
        return carry

    lax.fori_loop(0, 16, spread, 0)

    wide_o, nx = 128 // nty, nty // 2
    core, xme = lax.rem(ty, 2), lax.div(ty, 2)
    other = (dp, ty + 1 - 2 * core, tz)
    hop0 = []
    for b in range(3):
        left = vmat[:, :, 384 * b : 384 * b + 384].reshape(1152, 384)
        g = mm(left, inp3[...], TN)
        for a in range(3):
            for cc in range(3):
                part = g[128 * cc : 128 * cc + 128, 128 * a : 128 * a + 128]
                rsend[9 * b + 3 * a + cc] = part.astype(BF).reshape(nx, 2, wide_o, 128)
        src = rsend.at[pl.ds(9 * b, 9), :, 1 - core]
        hop0.append(remote(src, rpair.at[pl.ds(9 * b, 9)], ps.at[b], pr.at[b], other))
        hop0[b].start()
    hop1 = []
    for b in range(3):
        hop0[b].wait()
        for q in range(9 * b, 9 * b + 9):
            psum[q] = (rsend[q, :, core].astype(F32) + rpair[q].astype(F32)).astype(BF)
        for j in range(1, nx):
            x = lax.rem(xme + j, nx)
            src, dst = psum.at[pl.ds(9 * b, 9), x], rs1.at[xme, pl.ds(9 * b, 9)]
            dev = (dp, 2 * x + core, tz)
            hop1.append(remote(src, dst, r1s.at[b, j], r1r.at[b, nx - j], dev))
            hop1[-1].start()

    def turned(after, before):
        return jnp.concatenate([after, before], 0).astype(F32).T.astype(BF)

    def fill(dst, get_y, get_d, get_z):
        r, c = iota((32, 256), 0), iota((32, 256), 1)

        def place(row, ok):
            after = (r == row) & (c == 127) & side[1] & ok
            return one_hot(after | ((r == 16 + row) & (c == 128) & side[0] & ok))

        for s in (1, 0):
            ok = up[0] if s == 1 else up[1]
            mid = valid(ok, get_y(s))
            corner = turned(get_d(s, 0), get_d(s, 1))
            corner = corner[96:128] if s == 1 else corner[0:32]
            out = mm(mid, shifts[...]) + mm(corner, place(15 if s == 1 else 0, ok))
            rows, lanes = (slice(0, 32), slice(0, 128)) if s == 1 else (slice(1056, 1088), slice(128, 256))
            dst[0, rows, lanes] = mid
            dst[2, rows, lanes] = out[:, :128].astype(BF)
            dst[1, rows, lanes] = out[:, 128:].astype(BF)
        edge = turned(get_z(0), get_z(1))
        for h in range(2):
            lanes = slice(128 * h, 128 * h + 128)
            for j in range(8):
                rows = slice(32 + 128 * j, 160 + 128 * j)
                out = mm(dst[0, rows, lanes], shifts[...]) + mm(edge, place(8 * h + j, True))
                dst[2, rows, lanes] = out[:, :128].astype(BF)
                dst[1, rows, lanes] = out[:, 128:].astype(BF)
        for v in range(3):
            dst[v, 0:32, 128:256] = dst[v, 1024:1056, 0:128]
            dst[v, 1056:1088, 0:128] = dst[v, 32:64, 128:256]

    for n, dst in enumerate((xin, xcot)):
        rows, tile = slice(32 * n, 32 * n + 32), slice(16 * n, 16 * n + 16)
        fill(
            dst,
            lambda s, rows=rows: yrecv[s, rows, :],
            lambda s, t, tile=tile: drecv[s, t, tile, :],
            lambda t, tile=tile: zrecv[t, tile, :],
        )

    version = (1, 0, 2)

    def conv(n, src, g):
        rows = pl.ds(pl.multiple_of(g * 128, 128), 192)
        out = None
        for cc in range(3):
            term = mm(bands[n, cc, :, 0:192], src[version[cc], rows, :])
            out = term if out is None else out + term
        return out

    def forward(g, carry):
        pre = conv(0, xin, g)
        dact = conv(1, xcot, g)
        square = pre * pre
        t = jnp.tanh(C0 * pre * (1.0 + C1 * square))
        half = 0.5 + 0.5 * t
        slope = half + 0.5 * pre * (1.0 - t * t) * (C0 * (1.0 + (3.0 * C1) * square))
        act[pl.ds(pl.multiple_of(g * 128, 128), 128), :] = (pre * half).astype(BF)
        xdp[0, pl.ds(pl.multiple_of(g * 128 + 32, 32), 128), :] = (dact * slope).astype(BF)
        return carry

    lax.fori_loop(0, 8, forward, 0)

    columns = extract(xdp)
    zsend2[0] = columns[0:16]
    zsend2[1] = columns[16:32]
    ysend2[0] = xdp[0, 32:64, 0:128]
    ysend2[1] = xdp[0, 1024:1056, 128:256]
    halo2 = []
    for s in range(2):
        halo2.append(remote(ysend2.at[s], yrecv2.at[s], gs.at[s], gr.at[s], at(step[s], 0)))
        halo2.append(remote(zsend2.at[s], zrecv2.at[s], gs.at[2 + s], gr.at[2 + s], at(0, step[s])))
        for t in range(2):
            q = 4 + 2 * s + t
            dev = at(step[s], step[t])
            halo2.append(remote(zsend2.at[t], drecv2.at[s, t], gs.at[q], gr.at[q], dev))
    for copy in halo2:
        copy.start()

    acc1[...] = jnp.zeros_like(acc1)
    acc2[...] = jnp.zeros_like(acc2)

    def gram(g, carry):
        rows = pl.ds(pl.multiple_of(g * 128, 128), 192)
        own = xdp[0, pl.ds(pl.multiple_of(g * 128 + 32, 32), 128), :]
        a_own = act[pl.ds(pl.multiple_of(g * 128, 128), 128), :]
        for cc in range(3):
            acc1[cc, :, 0:192] += mm(own, xin[version[cc], rows, :], NT)
            acc2[cc] += mm(xcot[version[cc], rows, :], a_own, NT)
        return carry

    lax.fori_loop(0, 8, gram, 0)
    for cc in range(3):
        total = None
        for yo in range(4):
            part = acc1[cc, 32 * yo : 32 * yo + 32, :]
            part = part if yo == 0 else pltpu.roll(part, 256 - 32 * yo, 1)
            total = part if total is None else total + part
        fpart[32 * cc : 32 * cc + 32, :] = total[:, 0:128]
    total = jnp.zeros((96, 128), F32)
    lane = iota((96, 128), 1)
    for cc in range(3):
        band = None
        for yo in range(4):
            part = acc2[cc, 32 * yo : 32 * yo + 96, :]
            turn = (32 * cc - 32 * yo) % 128
            part = part if turn == 0 else pltpu.roll(part, turn, 1)
            band = part if band is None else band + part
        total = jnp.where(lane // 32 == cc, band, total)
    fpart[96:192, :] = total

    slab = 192 // nty
    hop_a = []
    for j in range(1, nty):
        t, dev = ty_peer(j)
        src = fpart.at[pl.ds(pl.multiple_of(t * slab, 8), slab), :]
        hop_a.append(remote(src, ar1.at[ty], a1s.at[j], a1r.at[nty - j], dev))
    for copy in hop_a:
        copy.start()
    ar1[ty] = fpart[pl.ds(pl.multiple_of(ty * slab, 8), slab), :]

    rs1[xme] = psum[:, xme]
    for copy in hop1:
        copy.wait()

    def sum1(q, carry):
        total = rs1[0, q].astype(F32)
        for t in range(1, nx):
            total = total + rs1[t, q].astype(F32)
        k = 9 * (lax.div(q, 3) % 3) + 3 * lax.div(q, 9) + q % 3
        qf[pl.ds(k, wide_o, stride=32), :] = total
        return carry

    lax.fori_loop(0, 27, sum1, 0)
    qb[...] = qf[...].astype(BF)
    deep = 32 * wide_o // ntz

    hop2 = []
    for j in range(1, zgroup):
        g, z, dev = z_peer(j)
        src = qb.at[pl.ds(pl.multiple_of(z * deep, 16), deep), :]
        hop2.append(remote(src, rs2.at[me], r2s.at[j], r2r.at[zgroup - j], dev))
    for copy in hop2:
        copy.start()
    rs2[me] = qb[pl.ds(pl.multiple_of(tz * deep, 16), deep), :]

    for copy in hop_a:
        copy.wait()
    total = ar1[0]
    for t in range(1, nty):
        total = total + ar1[t]
    fsum1[...] = total
    hop_b = []
    for j in range(1, zgroup):
        g, z, dev = z_peer(j)
        hop_b.append(remote(fsum1, ar2.at[me], a2s.at[j], a2r.at[zgroup - j], dev))
    for copy in hop_b:
        copy.start()
    ar2[me] = fsum1[...]

    loads[6].wait()

    def coarse(q, carry):
        out = None
        for a in range(3):
            left = vmat[pl.ds(q * 4 + 2 - a, 4)].reshape(256, 1152)
            term = mm(left, wc[1152 * a : 1152 * a + 1152, :])
            out = term if out is None else out + term
        o_gci[pl.ds(pl.multiple_of(q * 256, 256), 256), :] = out.astype(BF)
        return carry

    lax.fori_loop(0, 4, coarse, 0)

    for copy in hop_b:
        copy.wait()
    total = ar2[0]
    for t in range(1, zgroup):
        total = total + ar2[t]
    fsum2[...] = total
    hop_c = []
    for j in range(1, nty):
        t, dev = ty_peer(j)
        hop_c.append(remote(fsum2, gath.at[ty], a3s.at[j], a3r.at[nty - j], dev))
    for copy in hop_c:
        copy.start()
    gath[ty] = fsum2[...]

    for copy in halo2:
        copy.wait()
    fill(
        xdp,
        lambda s: yrecv2[s],
        lambda s, t: drecv2[s, t],
        lambda t: zrecv2[t],
    )

    def last(j, carry):
        parts = [conv(2, xdp, 4 * j + q).astype(BF) for q in range(4)]
        out = mm(perm[...], jnp.concatenate(parts, 0)).astype(BF)
        first = pl.multiple_of(16 * j, 16)
        o_gfi[:, pl.ds(first, 16), :] = out[:, :128].reshape(32, 16, 128)
        o_gfi[:, pl.ds(first + 32, 16), :] = out[:, 128:].reshape(32, 16, 128)
        return carry

    lax.fori_loop(0, 2, last, 0)

    for copy in hop2:
        copy.wait()
    total = rs2[0].astype(F32)
    for t in range(1, zgroup):
        total = total + rs2[t].astype(F32)
    for o in range(wide_o // ntz):
        o_gc[o] = total[32 * o : 32 * o + 27, :]

    for copy in hop_c:
        copy.wait()
    fpart[...] = gath[...].reshape(192, 128)
    for a in range(3):
        planes = [(xo, xo + a - 1) for xo in range(2) if 0 <= xo + a - 1 < 2]
        for b in range(3):
            for cc in range(3):
                k = 9 * a + 3 * b + cc
                one, two = None, None
                for xo, xi in planes:
                    first = 32 * cc + 16 * xo
                    lanes = slice(32 * b + 16 * xi, 32 * b + 16 * xi + 16)
                    part = fpart[first : first + 16, lanes]
                    one = part if one is None else one + part
                    first = 96 + 32 * b + 16 * xi
                    lanes = slice(32 * cc + 16 * xo, 32 * cc + 16 * xo + 16)
                    part = fpart[first : first + 16, lanes]
                    two = part if two is None else two + part
                o_gf[k] = one
                o_gs[26 - k] = two


def solution(mesh):
    sizes = tuple(mesh.shape[a] for a in ("dp", "ty", "tz"))
    ndp, nty, ntz = sizes
    zgroup = ndp * ntz
    wide_o, nx = 128 // nty, nty // 2
    slab = 192 // nty

    def per_device(fine_input, fine_cotangent, first_weight, second_weight, coarse_input, coarse_cotangent, coarse_weight):
        def by_offset(w):
            return w.transpose(1, 2, 0).reshape(256, 27)

        dma = pltpu.SemaphoreType.DMA
        scratch = [
            pltpu.VMEM((32, 64, 128), BF),
            pltpu.VMEM((32, 64, 128), BF),
            pltpu.VMEM((256, 27), BF),
            pltpu.VMEM((256, 27), BF),
            pltpu.VMEM((1024, 128), BF),
            pltpu.VMEM((1024, 128), BF),
            pltpu.VMEM((3456, 128), BF),
            pltpu.VMEM((512, 512), BF),
            pltpu.VMEM((128, 256), BF),
            pltpu.VMEM((3, ROWS, 256), BF),
            pltpu.VMEM((3, ROWS, 256), BF),
            pltpu.VMEM((3, ROWS, 256), BF),
            pltpu.VMEM((1024, 256), BF),
            pltpu.VMEM((3, 3, 128, 256), BF),
            pltpu.VMEM((2, 192, 128), BF),
            pltpu.VMEM((2, 192, 128), BF),
            pltpu.VMEM((2, 160, 128), BF),
            pltpu.VMEM((2, 160, 128), BF),
            pltpu.VMEM((2, 2, 48, 128), BF),
            pltpu.VMEM((2, 2, 48, 128), BF),
            pltpu.VMEM((2, 32, 128), BF),
            pltpu.VMEM((2, 32, 128), BF),
            pltpu.VMEM((2, 16, 128), BF),
            pltpu.VMEM((2, 16, 128), BF),
            pltpu.VMEM((2, 2, 16, 128), BF),
            pltpu.VMEM((1280, 128), F32),
            pltpu.VMEM((1280, 128), F32),
            pltpu.VMEM((1280, 128), F32),
            pltpu.VMEM((18, 64, 1152), BF),
            pltpu.VMEM((1152, 384), BF),
            pltpu.VMEM((27, nx, 2, wide_o, 128), BF),
            pltpu.VMEM((27, nx, wide_o, 128), BF),
            pltpu.VMEM((27, nx, wide_o, 128), BF),
            pltpu.VMEM((nx, 27, wide_o, 128), BF),
            pltpu.VMEM((32 * wide_o, 128), F32),
            pltpu.VMEM((32 * wide_o, 128), BF),
            pltpu.VMEM((zgroup, 32 * wide_o // ntz, 128), BF),
            pltpu.VMEM((3, 128, 256), F32),
            pltpu.VMEM((3, 192, 128), F32),
            pltpu.VMEM((192, 128), F32),
            pltpu.VMEM((nty, slab, 128), F32),
            pltpu.VMEM((slab, 128), F32),
            pltpu.VMEM((zgroup, slab, 128), F32),
            pltpu.VMEM((slab, 128), F32),
            pltpu.VMEM((nty, slab, 128), F32),
            dma((7,)),
            dma((8,)),
            dma((8,)),
            dma((3,)),
            dma((3,)),
            dma((8,)),
            dma((8,)),
            dma((3, nx)),
            dma((3, nx)),
            dma((zgroup,)),
            dma((zgroup,)),
            dma((nty,)),
            dma((nty,)),
            dma((zgroup,)),
            dma((zgroup,)),
            dma((nty,)),
            dma((nty,)),
        ]
        vmem = pl.BlockSpec(memory_space=pltpu.VMEM)
        outs = pl.pallas_call(
            functools.partial(kernel, sizes),
            out_shape=(
                jax.ShapeDtypeStruct((32, 64, 128), BF),
                jax.ShapeDtypeStruct((27, 16, 16), F32),
                jax.ShapeDtypeStruct((27, 16, 16), F32),
                jax.ShapeDtypeStruct((1024, 128), BF),
                jax.ShapeDtypeStruct((wide_o // ntz, 27, 128), F32),
            ),
            in_specs=[pl.BlockSpec(memory_space=pltpu.HBM)] * 7,
            out_specs=(vmem,) * 5,
            scratch_shapes=scratch,
            compiler_params=pltpu.CompilerParams(
                collective_id=0, has_side_effects=True, vmem_limit_bytes=48 * 1024 * 1024
            ),
        )(
            fine_input.reshape(32, 64, 128),
            fine_cotangent.reshape(32, 64, 128),
            by_offset(first_weight),
            by_offset(second_weight),
            coarse_input.reshape(1024, 128),
            coarse_cotangent.reshape(1024, 128),
            coarse_weight.reshape(3456, 128),
        )
        return (
            outs[0].reshape(fine_input.shape),
            outs[1],
            outs[2],
            outs[3].reshape(coarse_input.shape),
            outs[4],
        )

    fine = P("dp", None, None, "ty", "tz")
    wide = P("dp", None, "ty", "tz", None)
    return jax.shard_map(
        per_device,
        mesh=mesh,
        in_specs=(fine, fine, P(), P(), wide, wide, P()),
        out_specs=(fine, P(), P(), wide, P(("ty", "tz"), None, None)),
        check_vma=False,
    )
```

```python
import functools

import jax
import jax.numpy as jnp
from jax import lax
from jax.experimental import pallas as pl
from jax.experimental.pallas import tpu as pltpu
from jax.sharding import PartitionSpec as P

MESH = pl.DeviceIdType.MESH
BF = jnp.bfloat16
F32 = jnp.float32
NN = (((1,), (0,)), ((), ()))
NT = (((1,), (1,)), ((), ()))
TN = (((0,), (0,)), ((), ()))
ROWS = 34 * 32
C0 = 0.7978845608028654
C1 = 0.044715


def mm(a, b, dims=NN):
    return lax.dot_general(a, b, dims, preferred_element_type=F32)


def iota(shape, dim):
    return lax.broadcasted_iota(jnp.int32, shape, dim)


def one_hot(cond):
    return jnp.where(cond, 1.0, 0.0).astype(BF)


def kernel(
    sizes,
    h_fin,
    h_fcot,
    h_w1,
    h_w2,
    h_cin,
    h_ccot,
    h_wc,
    o_gfi,
    o_gf,
    o_gs,
    o_gci,
    o_gc,
    fin,
    fcot,
    w1,
    w2,
    cin,
    ccot,
    wc,
    perm,
    shifts,
    xin,
    xcot,
    xdp,
    act,
    bands,
    ysend,
    yrecv,
    zsend,
    zrecv,
    dsend,
    drecv,
    ysend2,
    yrecv2,
    zsend2,
    zrecv2,
    drecv2,
    cflat,
    cplus,
    cminus,
    vmat,
    inp3,
    rsend,
    rpair,
    psum,
    rs1,
    qf,
    qb,
    rs2,
    acc1,
    acc2,
    fpart,
    ar1,
    fsum1,
    ar2,
    fsum2,
    gath,
    ls,
    hs,
    hr,
    ps,
    pr,
    gs,
    gr,
    r1s,
    r1r,
    r2s,
    r2r,
    a1s,
    a1r,
    a2s,
    a2r,
    a3s,
    a3r,
):
    ndp, nty, ntz = sizes
    dp, ty, tz = lax.axis_index("dp"), lax.axis_index("ty"), lax.axis_index("tz")
    zgroup = ndp * ntz
    me = dp * ntz + tz

    def at(dy, dz):
        return (dp, lax.rem(ty + dy + nty, nty), lax.rem(tz + dz + ntz, ntz))

    def ty_peer(j):
        t = lax.rem(ty + j, nty)
        return t, (dp, t, tz)

    def z_peer(j):
        g = lax.rem(me + j, zgroup)
        z = lax.rem(g, ntz)
        return g, z, (lax.div(g, ntz), ty, z)

    def remote(src, dst, ssem, rsem, dev):
        return pltpu.make_async_remote_copy(
            src_ref=src,
            dst_ref=dst,
            send_sem=ssem,
            recv_sem=rsem,
            device_id=dev,
            device_id_type=MESH,
        )

    loads = []
    pairs = ((h_ccot, ccot), (h_fin, fin), (h_fcot, fcot), (h_w1, w1), (h_w2, w2), (h_cin, cin), (h_wc, wc))
    for n, (src, dst) in enumerate(pairs):
        loads.append(pltpu.make_async_copy(src, dst, ls.at[n]))
        loads[n].start()

    up = (ty > 0, ty < nty - 1)
    side = (tz > 0, tz < ntz - 1)

    barrier = pltpu.get_barrier_semaphore()
    partners = [at(dy, dz) for dy in (-1, 1) for dz in (-1, 1)]
    partners += [ty_peer(j)[1] for j in range(1, nty)]
    partners += [z_peer(j)[2] for j in range(1, zgroup)]
    for dev in partners:
        pl.semaphore_signal(barrier, inc=1, device_id=dev, device_id_type=MESH)

    r, c = iota((512, 512), 0), iota((512, 512), 1)
    perm[...] = one_hot(c == (r % 16) * 32 + ((r // 16) % 2) * 16 + r // 32)
    r, c = iota((128, 256), 0), iota((128, 256), 1)
    shifts[...] = one_hot(((r == c + 1) & (c < 127)) | ((r + 1 == c - 128) & (c > 128)))

    def relayout(src, dst):
        for j in range(2):
            left = src[:, 16 * j : 16 * j + 16, :].reshape(512, 128)
            right = src[:, 32 + 16 * j : 48 + 16 * j, :].reshape(512, 128)
            both = jnp.concatenate([left, right], 1)
            dst[0, 32 + 512 * j : 544 + 512 * j, :] = mm(perm[...], both).astype(BF)

    def extract(src):
        r, c = iota((32, 256), 0), iota((32, 256), 1)
        total = None
        for j in range(8):
            sel = one_hot((r % 16 == 8 * (c // 128) + j) & (c % 128 == 127 * (r // 16)))
            part = mm(sel, src[0, 32 + 128 * j : 160 + 128 * j, :], NT)
            total = part if total is None else total + part
        return total.astype(BF)

    loads[1].wait()
    relayout(fin, xin)
    loads[2].wait()
    relayout(fcot, xcot)
    for n, src in enumerate((xin, xcot)):
        columns = extract(src)
        for t in range(2):
            tile = columns[16 * t : 16 * t + 16, :]
            zsend[t, 16 * n : 16 * n + 16, :] = tile
            for q in range(2):
                dsend[q, t, 16 * n : 16 * n + 16, :] = tile

    loads[0].wait()
    for x in range(16):
        cflat[80 * x + 8 : 80 * x + 72, :] = ccot[64 * x : 64 * x + 64, :].astype(F32)

    def column(y, z):
        return cflat[pl.ds(8 * y + z, 16, stride=80), :]

    for y in range(8):
        zsend[0, 32 + 16 * y : 48 + 16 * y, :] = column(y + 1, 0).astype(BF)
        zsend[1, 32 + 16 * y : 48 + 16 * y, :] = column(y + 1, 7).astype(BF)
    for s in range(2):
        own = (slice(32, 64), slice(0, 128)) if s == 0 else (slice(1024, 1056), slice(128, 256))
        ysend[s, 0:32, :] = xin[(0, *own)]
        ysend[s, 32:64, :] = xcot[(0, *own)]
        first = 8 if s == 0 else 64
        for x in range(0, 16, 2):
            pair = [cflat[80 * (x + q) + first : 80 * (x + q) + first + 8, :] for q in range(2)]
            ysend[s, 64 + 8 * x : 80 + 8 * x, :] = jnp.concatenate(pair, 0).astype(BF)
        for t in range(2):
            dsend[s, t, 32:48, :] = column(1 if s == 0 else 8, 0 if t == 0 else 7).astype(BF)

    pl.semaphore_wait(barrier, len(partners))

    step = (-1, 1)
    halo = []
    for s in range(2):
        halo.append(remote(ysend.at[s], yrecv.at[s], hs.at[s], hr.at[s], at(step[s], 0)))
        halo.append(remote(zsend.at[s], zrecv.at[s], hs.at[2 + s], hr.at[2 + s], at(0, step[s])))
        for t in range(2):
            q = 4 + 2 * s + t
            halo.append(
                remote(dsend.at[s, t], drecv.at[s, t], hs.at[q], hr.at[q], at(step[s], step[t]))
            )
    for copy in halo:
        copy.start()

    lane = iota((32, 768), 1)
    q, m = lane // 128, lane % 128
    k = 9 * ((m // 16) % 2 - q % 2 + 1) + 3 * (m // 32) + q // 2
    wanted = (m < 96, iota((32, 768), 0))
    straight = one_hot(wanted[0] & (wanted[1] == k))[:27]
    flipped = one_hot(wanted[0] & (wanted[1] == 26 - k))[:27]
    r, c = iota((256, 768), 0), iota((256, 768), 1)
    to_in, to_out = r % 16 == c % 16, r // 16 == c % 16
    r, c = iota((16, 256), 0), iota((16, 256), 1)
    by_out, by_in = one_hot(c // 16 == r), one_hot(c % 16 == r)
    loads[3].wait()
    loads[4].wait()
    for n, (w, pick, mask, rows) in enumerate(
        (
            (w1, straight, to_in, by_out),
            (w2, flipped, to_out, by_in),
            (w1, flipped, to_out, by_in),
        )
    ):
        wide = jnp.where(mask, mm(w[...], pick), 0.0).astype(BF)
        strips = mm(rows, wide)
        for cc in range(3):
            for xo in range(2):
                first = 128 * (2 * cc + xo)
                strip = strips[:, first : first + 128]
                strip = jnp.concatenate([strip, jnp.zeros_like(strip)], 1)
                for yo in range(4):
                    moved = strip if yo == 0 else pltpu.roll(strip, 32 * yo, 1)
                    first = 32 * yo + 16 * xo
                    bands[n, cc, first : first + 16, :] = moved.astype(BF)

    inp3[...] = jnp.zeros_like(inp3)
    loads[5].wait()
    for a in range(3):
        inp3[64 * (2 - a) : 64 * (2 - a) + 1024, 128 * a : 128 * a + 128] = cin[...]
    vmat[0] = jnp.zeros((64, 1152), BF)
    vmat[17] = jnp.zeros((64, 1152), BF)
    qf[...] = jnp.zeros_like(qf)

    for copy in halo:
        copy.wait()

    def valid(cond, value):
        return jnp.where(cond, value, jnp.zeros_like(value))

    for x in range(16):
        rows = slice(64 + 8 * (x // 2 * 2), 80 + 8 * (x // 2 * 2))
        half = slice(8 * (x % 2), 8 * (x % 2) + 8)
        cflat[80 * x : 80 * x + 8, :] = valid(up[0], yrecv[1, rows, :].astype(F32)[half])
        cflat[80 * x + 72 : 80 * x + 80, :] = valid(up[1], yrecv[0, rows, :].astype(F32)[half])
    cplus[...] = pltpu.roll(cflat[...], 1279, 0)
    cminus[...] = pltpu.roll(cflat[...], 1, 0)
    for y in range(10):
        for ref, z, t, ok in ((cplus, 7, 0, side[1]), (cminus, 0, 1, side[0])):
            if y == 0:
                part, ok = drecv[1, t, 32:48, :], ok & up[0]
            elif y == 9:
                part, ok = drecv[0, t, 32:48, :], ok & up[1]
            else:
                part = zrecv[t, 32 + 16 * (y - 1) : 48 + 16 * (y - 1), :]
            ref[pl.ds(8 * y + z, 16, stride=80), :] = valid(ok, part.astype(F32))

    def spread(x, carry):
        for b in range(3):
            for cc, ref in enumerate((cplus, cflat, cminus)):
                rows = ref[pl.ds(pl.multiple_of(x * 80 + 8 * (2 - b), 8), 64), :]
                q = 3 * b + cc
                vmat[x + 1, :, 128 * q : 128 * q + 128] = rows.astype(BF)
        return carry

    lax.fori_loop(0, 16, spread, 0)

    wide_o, nx = 128 // nty, nty // 2
    core, xme = lax.rem(ty, 2), lax.div(ty, 2)
    other = (dp, ty + 1 - 2 * core, tz)
    hop0 = []
    for b in range(3):
        left = vmat[:, :, 384 * b : 384 * b + 384].reshape(1152, 384)
        g = mm(left, inp3[...], TN)
        for a in range(3):
            for cc in range(3):
                part = g[128 * cc : 128 * cc + 128, 128 * a : 128 * a + 128]
                rsend[9 * b + 3 * a + cc] = part.astype(BF).reshape(nx, 2, wide_o, 128)
        src = rsend.at[pl.ds(9 * b, 9), :, 1 - core]
        hop0.append(remote(src, rpair.at[pl.ds(9 * b, 9)], ps.at[b], pr.at[b], other))
        hop0[b].start()
    hop1 = []
    for b in range(3):
        hop0[b].wait()
        for q in range(9 * b, 9 * b + 9):
            psum[q] = (rsend[q, :, core].astype(F32) + rpair[q].astype(F32)).astype(BF)
        for j in range(1, nx):
            x = lax.rem(xme + j, nx)
            src, dst = psum.at[pl.ds(9 * b, 9), x], rs1.at[xme, pl.ds(9 * b, 9)]
            dev = (dp, 2 * x + core, tz)
            hop1.append(remote(src, dst, r1s.at[b, j], r1r.at[b, nx - j], dev))
            hop1[-1].start()

    def turned(after, before):
        return jnp.concatenate([after, before], 0).astype(F32).T.astype(BF)

    def fill(dst, get_y, get_d, get_z):
        r, c = iota((32, 256), 0), iota((32, 256), 1)

        def place(row, ok):
            after = (r == row) & (c == 127) & side[1] & ok
            return one_hot(after | ((r == 16 + row) & (c == 128) & side[0] & ok))

        for s in (1, 0):
            ok = up[0] if s == 1 else up[1]
            mid = valid(ok, get_y(s))
            corner = turned(get_d(s, 0), get_d(s, 1))
            corner = corner[96:128] if s == 1 else corner[0:32]
            out = mm(mid, shifts[...]) + mm(corner, place(15 if s == 1 else 0, ok))
            rows, lanes = (slice(0, 32), slice(0, 128)) if s == 1 else (slice(1056, 1088), slice(128, 256))
            dst[0, rows, lanes] = mid
            dst[2, rows, lanes] = out[:, :128].astype(BF)
            dst[1, rows, lanes] = out[:, 128:].astype(BF)
        edge = turned(get_z(0), get_z(1))
        for h in range(2):
            lanes = slice(128 * h, 128 * h + 128)
            for j in range(8):
                rows = slice(32 + 128 * j, 160 + 128 * j)
                out = mm(dst[0, rows, lanes], shifts[...]) + mm(edge, place(8 * h + j, True))
                dst[2, rows, lanes] = out[:, :128].astype(BF)
                dst[1, rows, lanes] = out[:, 128:].astype(BF)
        for v in range(3):
            dst[v, 0:32, 128:256] = dst[v, 1024:1056, 0:128]
            dst[v, 1056:1088, 0:128] = dst[v, 32:64, 128:256]

    for n, dst in enumerate((xin, xcot)):
        rows, tile = slice(32 * n, 32 * n + 32), slice(16 * n, 16 * n + 16)
        fill(
            dst,
            lambda s, rows=rows: yrecv[s, rows, :],
            lambda s, t, tile=tile: drecv[s, t, tile, :],
            lambda t, tile=tile: zrecv[t, tile, :],
        )

    version = (1, 0, 2)

    def conv(n, src, g):
        rows = pl.ds(pl.multiple_of(g * 128, 128), 192)
        out = None
        for cc in range(3):
            term = mm(bands[n, cc, :, 0:192], src[version[cc], rows, :])
            out = term if out is None else out + term
        return out

    def forward(g, carry):
        pre = conv(0, xin, g)
        dact = conv(1, xcot, g)
        square = pre * pre
        t = jnp.tanh(C0 * pre * (1.0 + C1 * square))
        half = 0.5 + 0.5 * t
        slope = half + 0.5 * pre * (1.0 - t * t) * (C0 * (1.0 + (3.0 * C1) * square))
        act[pl.ds(pl.multiple_of(g * 128, 128), 128), :] = (pre * half).astype(BF)
        xdp[0, pl.ds(pl.multiple_of(g * 128 + 32, 32), 128), :] = (dact * slope).astype(BF)
        return carry

    lax.fori_loop(0, 8, forward, 0)

    columns = extract(xdp)
    zsend2[0] = columns[0:16]
    zsend2[1] = columns[16:32]
    ysend2[0] = xdp[0, 32:64, 0:128]
    ysend2[1] = xdp[0, 1024:1056, 128:256]
    halo2 = []
    for s in range(2):
        halo2.append(remote(ysend2.at[s], yrecv2.at[s], gs.at[s], gr.at[s], at(step[s], 0)))
        halo2.append(remote(zsend2.at[s], zrecv2.at[s], gs.at[2 + s], gr.at[2 + s], at(0, step[s])))
        for t in range(2):
            q = 4 + 2 * s + t
            dev = at(step[s], step[t])
            halo2.append(remote(zsend2.at[t], drecv2.at[s, t], gs.at[q], gr.at[q], dev))
    for copy in halo2:
        copy.start()

    acc1[...] = jnp.zeros_like(acc1)
    acc2[...] = jnp.zeros_like(acc2)

    def gram(g, carry):
        rows = pl.ds(pl.multiple_of(g * 128, 128), 192)
        own = xdp[0, pl.ds(pl.multiple_of(g * 128 + 32, 32), 128), :]
        a_own = act[pl.ds(pl.multiple_of(g * 128, 128), 128), :]
        for cc in range(3):
            acc1[cc, :, 0:192] += mm(own, xin[version[cc], rows, :], NT)
            acc2[cc] += mm(xcot[version[cc], rows, :], a_own, NT)
        return carry

    lax.fori_loop(0, 8, gram, 0)
    for cc in range(3):
        total = None
        for yo in range(4):
            part = acc1[cc, 32 * yo : 32 * yo + 32, :]
            part = part if yo == 0 else pltpu.roll(part, 256 - 32 * yo, 1)
            total = part if total is None else total + part
        fpart[32 * cc : 32 * cc + 32, :] = total[:, 0:128]
    total = jnp.zeros((96, 128), F32)
    lane = iota((96, 128), 1)
    for cc in range(3):
        band = None
        for yo in range(4):
            part = acc2[cc, 32 * yo : 32 * yo + 96, :]
            turn = (32 * cc - 32 * yo) % 128
            part = part if turn == 0 else pltpu.roll(part, turn, 1)
            band = part if band is None else band + part
        total = jnp.where(lane // 32 == cc, band, total)
    fpart[96:192, :] = total

    slab = 192 // nty
    hop_a = []
    for j in range(1, nty):
        t, dev = ty_peer(j)
        src = fpart.at[pl.ds(pl.multiple_of(t * slab, 8), slab), :]
        hop_a.append(remote(src, ar1.at[ty], a1s.at[j], a1r.at[nty - j], dev))
    for copy in hop_a:
        copy.start()
    ar1[ty] = fpart[pl.ds(pl.multiple_of(ty * slab, 8), slab), :]

    rs1[xme] = psum[:, xme]
    for copy in hop1:
        copy.wait()

    def sum1(q, carry):
        total = rs1[0, q].astype(F32)
        for t in range(1, nx):
            total = total + rs1[t, q].astype(F32)
        k = 9 * (lax.div(q, 3) % 3) + 3 * lax.div(q, 9) + q % 3
        qf[pl.ds(k, wide_o, stride=32), :] = total
        return carry

    lax.fori_loop(0, 27, sum1, 0)
    qb[...] = qf[...].astype(BF)
    deep = 32 * wide_o // ntz

    hop2 = []
    for j in range(1, zgroup):
        g, z, dev = z_peer(j)
        src = qb.at[pl.ds(pl.multiple_of(z * deep, 16), deep), :]
        hop2.append(remote(src, rs2.at[me], r2s.at[j], r2r.at[zgroup - j], dev))
    for copy in hop2:
        copy.start()
    rs2[me] = qb[pl.ds(pl.multiple_of(tz * deep, 16), deep), :]

    for copy in hop_a:
        copy.wait()
    total = ar1[0]
    for t in range(1, nty):
        total = total + ar1[t]
    fsum1[...] = total
    hop_b = []
    for j in range(1, zgroup):
        g, z, dev = z_peer(j)
        hop_b.append(remote(fsum1, ar2.at[me], a2s.at[j], a2r.at[zgroup - j], dev))
    for copy in hop_b:
        copy.start()
    ar2[me] = fsum1[...]

    loads[6].wait()

    def coarse(q, carry):
        out = None
        for a in range(3):
            left = vmat[pl.ds(q * 4 + 2 - a, 4)].reshape(256, 1152)
            term = mm(left, wc[1152 * a : 1152 * a + 1152, :])
            out = term if out is None else out + term
        o_gci[pl.ds(pl.multiple_of(q * 256, 256), 256), :] = out.astype(BF)
        return carry

    lax.fori_loop(0, 4, coarse, 0)

    for copy in hop_b:
        copy.wait()
    total = ar2[0]
    for t in range(1, zgroup):
        total = total + ar2[t]
    fsum2[...] = total
    hop_c = []
    for j in range(1, nty):
        t, dev = ty_peer(j)
        hop_c.append(remote(fsum2, gath.at[ty], a3s.at[j], a3r.at[nty - j], dev))
    for copy in hop_c:
        copy.start()
    gath[ty] = fsum2[...]

    for copy in halo2:
        copy.wait()
    fill(
        xdp,
        lambda s: yrecv2[s],
        lambda s, t: drecv2[s, t],
        lambda t: zrecv2[t],
    )

    def last(j, carry):
        parts = [conv(2, xdp, 4 * j + q).astype(BF) for q in range(4)]
        out = mm(perm[...], jnp.concatenate(parts, 0)).astype(BF)
        first = pl.multiple_of(16 * j, 16)
        o_gfi[:, pl.ds(first, 16), :] = out[:, :128].reshape(32, 16, 128)
        o_gfi[:, pl.ds(first + 32, 16), :] = out[:, 128:].reshape(32, 16, 128)
        return carry

    lax.fori_loop(0, 2, last, 0)

    for copy in hop2:
        copy.wait()
    total = rs2[0].astype(F32)
    for t in range(1, zgroup):
        total = total + rs2[t].astype(F32)
    for o in range(wide_o // ntz):
        o_gc[:, o, :] = total[32 * o : 32 * o + 27, :]

    for copy in hop_c:
        copy.wait()
    fpart[...] = gath[...].reshape(192, 128)
    for a in range(3):
        planes = [(xo, xo + a - 1) for xo in range(2) if 0 <= xo + a - 1 < 2]
        for b in range(3):
            for cc in range(3):
                k = 9 * a + 3 * b + cc
                one, two = None, None
                for xo, xi in planes:
                    first = 32 * cc + 16 * xo
                    lanes = slice(32 * b + 16 * xi, 32 * b + 16 * xi + 16)
                    part = fpart[first : first + 16, lanes]
                    one = part if one is None else one + part
                    first = 96 + 32 * b + 16 * xi
                    lanes = slice(32 * cc + 16 * xo, 32 * cc + 16 * xo + 16)
                    part = fpart[first : first + 16, lanes]
                    two = part if two is None else two + part
                o_gf[k] = one
                o_gs[26 - k] = two


def finish(gfi, gf, gs, gci, gc, o_gfi, o_gf, o_gs, o_gci, o_gc, sems):
    copies = [
        pltpu.make_async_copy(src, dst, sems.at[n])
        for n, (src, dst) in enumerate(((gfi, o_gfi), (gci, o_gci), (gc, o_gc)))
    ]
    for copy in copies:
        copy.start()
    for src, dst in ((gf, o_gf), (gs, o_gs)):
        for o in range(16):
            dst[o] = src[:, o, :].T
    for copy in copies:
        copy.wait()


def solution(mesh):
    sizes = tuple(mesh.shape[a] for a in ("dp", "ty", "tz"))
    ndp, nty, ntz = sizes
    zgroup = ndp * ntz
    wide_o, nx = 128 // nty, nty // 2
    slab = 192 // nty

    def per_device(fine_input, fine_cotangent, first_weight, second_weight, coarse_input, coarse_cotangent, coarse_weight):
        def by_offset(w):
            return w.transpose(1, 2, 0).reshape(256, 27)

        dma = pltpu.SemaphoreType.DMA
        scratch = [
            pltpu.VMEM((32, 64, 128), BF),
            pltpu.VMEM((32, 64, 128), BF),
            pltpu.VMEM((256, 27), BF),
            pltpu.VMEM((256, 27), BF),
            pltpu.VMEM((1024, 128), BF),
            pltpu.VMEM((1024, 128), BF),
            pltpu.VMEM((3456, 128), BF),
            pltpu.VMEM((512, 512), BF),
            pltpu.VMEM((128, 256), BF),
            pltpu.VMEM((3, ROWS, 256), BF),
            pltpu.VMEM((3, ROWS, 256), BF),
            pltpu.VMEM((3, ROWS, 256), BF),
            pltpu.VMEM((1024, 256), BF),
            pltpu.VMEM((3, 3, 128, 256), BF),
            pltpu.VMEM((2, 192, 128), BF),
            pltpu.VMEM((2, 192, 128), BF),
            pltpu.VMEM((2, 160, 128), BF),
            pltpu.VMEM((2, 160, 128), BF),
            pltpu.VMEM((2, 2, 48, 128), BF),
            pltpu.VMEM((2, 2, 48, 128), BF),
            pltpu.VMEM((2, 32, 128), BF),
            pltpu.VMEM((2, 32, 128), BF),
            pltpu.VMEM((2, 16, 128), BF),
            pltpu.VMEM((2, 16, 128), BF),
            pltpu.VMEM((2, 2, 16, 128), BF),
            pltpu.VMEM((1280, 128), F32),
            pltpu.VMEM((1280, 128), F32),
            pltpu.VMEM((1280, 128), F32),
            pltpu.VMEM((18, 64, 1152), BF),
            pltpu.VMEM((1152, 384), BF),
            pltpu.VMEM((27, nx, 2, wide_o, 128), BF),
            pltpu.VMEM((27, nx, wide_o, 128), BF),
            pltpu.VMEM((27, nx, wide_o, 128), BF),
            pltpu.VMEM((nx, 27, wide_o, 128), BF),
            pltpu.VMEM((32 * wide_o, 128), F32),
            pltpu.VMEM((32 * wide_o, 128), BF),
            pltpu.VMEM((zgroup, 32 * wide_o // ntz, 128), BF),
            pltpu.VMEM((3, 128, 256), F32),
            pltpu.VMEM((3, 192, 128), F32),
            pltpu.VMEM((192, 128), F32),
            pltpu.VMEM((nty, slab, 128), F32),
            pltpu.VMEM((slab, 128), F32),
            pltpu.VMEM((zgroup, slab, 128), F32),
            pltpu.VMEM((slab, 128), F32),
            pltpu.VMEM((nty, slab, 128), F32),
            dma((7,)),
            dma((8,)),
            dma((8,)),
            dma((3,)),
            dma((3,)),
            dma((8,)),
            dma((8,)),
            dma((3, nx)),
            dma((3, nx)),
            dma((zgroup,)),
            dma((zgroup,)),
            dma((nty,)),
            dma((nty,)),
            dma((zgroup,)),
            dma((zgroup,)),
            dma((nty,)),
            dma((nty,)),
        ]
        vmem = pl.BlockSpec(memory_space=pltpu.VMEM)
        outs = pl.pallas_call(
            functools.partial(kernel, sizes),
            out_shape=(
                jax.ShapeDtypeStruct((32, 64, 128), BF),
                jax.ShapeDtypeStruct((27, 16, 16), F32),
                jax.ShapeDtypeStruct((27, 16, 16), F32),
                jax.ShapeDtypeStruct((1024, 128), BF),
                jax.ShapeDtypeStruct((27, wide_o // ntz, 128), F32),
            ),
            in_specs=[pl.BlockSpec(memory_space=pl.ANY)] * 7,
            out_specs=(vmem,) * 5,
            scratch_shapes=scratch,
            compiler_params=pltpu.CompilerParams(
                collective_id=0, has_side_effects=True, vmem_limit_bytes=60 * 1024 * 1024
            ),
        )(
            fine_input.reshape(32, 64, 128),
            fine_cotangent.reshape(32, 64, 128),
            by_offset(first_weight),
            by_offset(second_weight),
            coarse_input.reshape(1024, 128),
            coarse_cotangent.reshape(1024, 128),
            coarse_weight.reshape(3456, 128),
        )
        far = pl.BlockSpec(memory_space=pl.ANY)
        outs = pl.pallas_call(
            finish,
            out_shape=(
                jax.ShapeDtypeStruct((32, 64, 128), BF),
                jax.ShapeDtypeStruct((16, 16, 27), F32),
                jax.ShapeDtypeStruct((16, 16, 27), F32),
                jax.ShapeDtypeStruct((1024, 128), BF),
                jax.ShapeDtypeStruct((27, wide_o // ntz, 128), F32),
            ),
            in_specs=[far, vmem, vmem, far, far],
            out_specs=(far, vmem, vmem, far, far),
            scratch_shapes=[dma((3,))],
            compiler_params=pltpu.CompilerParams(vmem_limit_bytes=60 * 1024 * 1024),
        )(*outs)
        return (
            outs[0].reshape(fine_input.shape),
            outs[1].transpose(2, 0, 1),
            outs[2].transpose(2, 0, 1),
            outs[3].reshape(coarse_input.shape),
            outs[4].transpose(1, 0, 2),
        )

    fine = P("dp", None, None, "ty", "tz")
    wide = P("dp", None, "ty", "tz", None)
    return jax.shard_map(
        per_device,
        mesh=mesh,
        in_specs=(fine, fine, P(), P(), wide, wide, P()),
        out_specs=(fine, P(), P(), wide, P(("ty", "tz"), None, None)),
        check_vma=False,
    )
```

```python
import functools

import jax
import jax.numpy as jnp
from jax import lax
from jax.experimental import pallas as pl
from jax.experimental.pallas import tpu as pltpu
from jax.sharding import PartitionSpec as P

MESH = pl.DeviceIdType.MESH
BF = jnp.bfloat16
F32 = jnp.float32
NN = (((1,), (0,)), ((), ()))
NT = (((1,), (1,)), ((), ()))
TN = (((0,), (0,)), ((), ()))
ROWS = 34 * 32
C0 = 0.7978845608028654
C1 = 0.044715


def mm(a, b, dims=NN):
    return lax.dot_general(a, b, dims, preferred_element_type=F32)


def iota(shape, dim):
    return lax.broadcasted_iota(jnp.int32, shape, dim)


def one_hot(cond):
    return jnp.where(cond, 1.0, 0.0).astype(BF)


def kernel(
    sizes,
    h_fin,
    h_fcot,
    h_w1,
    h_w2,
    h_cin,
    h_ccot,
    h_wc,
    o_gfi,
    o_gf,
    o_gs,
    o_gci,
    o_gc,
    fin,
    fcot,
    w1,
    w2,
    cin,
    ccot,
    wc,
    perm,
    shifts,
    xin,
    xcot,
    xdp,
    act,
    bands,
    ysend,
    yrecv,
    zsend,
    zrecv,
    dsend,
    drecv,
    ysend2,
    yrecv2,
    zsend2,
    zrecv2,
    drecv2,
    cflat,
    cplus,
    cminus,
    vmat,
    inp3,
    rsend,
    rpair,
    psum,
    rs1,
    qf,
    qb,
    rs2,
    acc1,
    acc2,
    fpart,
    ar1,
    fsum1,
    ar2,
    fsum2,
    gath,
    ls,
    hs,
    hr,
    ps,
    pr,
    gs,
    gr,
    r1s,
    r1r,
    r2s,
    r2r,
    a1s,
    a1r,
    a2s,
    a2r,
    a3s,
    a3r,
):
    ndp, nty, ntz = sizes
    dp, ty, tz = lax.axis_index("dp"), lax.axis_index("ty"), lax.axis_index("tz")
    zgroup = ndp * ntz
    me = dp * ntz + tz

    def at(dy, dz):
        return (dp, lax.rem(ty + dy + nty, nty), lax.rem(tz + dz + ntz, ntz))

    def ty_peer(j):
        t = lax.rem(ty + j, nty)
        return t, (dp, t, tz)

    def z_peer(j):
        g = lax.rem(me + j, zgroup)
        z = lax.rem(g, ntz)
        return g, z, (lax.div(g, ntz), ty, z)

    def remote(src, dst, ssem, rsem, dev):
        return pltpu.make_async_remote_copy(
            src_ref=src,
            dst_ref=dst,
            send_sem=ssem,
            recv_sem=rsem,
            device_id=dev,
            device_id_type=MESH,
        )

    loads = []
    pairs = ((h_ccot, ccot), (h_fin, fin), (h_fcot, fcot), (h_w1, w1), (h_w2, w2), (h_cin, cin), (h_wc, wc))
    for n, (src, dst) in enumerate(pairs):
        loads.append(pltpu.make_async_copy(src, dst, ls.at[n]))
        loads[n].start()

    up = (ty > 0, ty < nty - 1)
    side = (tz > 0, tz < ntz - 1)

    barrier = pltpu.get_barrier_semaphore()
    partners = [at(dy, dz) for dy in (-1, 1) for dz in (-1, 1)]
    partners += [ty_peer(j)[1] for j in range(1, nty)]
    partners += [z_peer(j)[2] for j in range(1, zgroup)]
    for dev in partners:
        pl.semaphore_signal(barrier, inc=1, device_id=dev, device_id_type=MESH)

    r, c = iota((512, 512), 0), iota((512, 512), 1)
    perm[...] = one_hot(c == (r % 16) * 32 + ((r // 16) % 2) * 16 + r // 32)
    r, c = iota((128, 256), 0), iota((128, 256), 1)
    shifts[...] = one_hot(((r == c + 1) & (c < 127)) | ((r + 1 == c - 128) & (c > 128)))

    def relayout(src, dst):
        for j in range(2):
            left = src[:, 16 * j : 16 * j + 16, :].reshape(512, 128)
            right = src[:, 32 + 16 * j : 48 + 16 * j, :].reshape(512, 128)
            both = jnp.concatenate([left, right], 1)
            dst[0, 32 + 512 * j : 544 + 512 * j, :] = mm(perm[...], both).astype(BF)

    def extract(src):
        r, c = iota((32, 256), 0), iota((32, 256), 1)
        total = None
        for j in range(8):
            sel = one_hot((r % 16 == 8 * (c // 128) + j) & (c % 128 == 127 * (r // 16)))
            part = mm(sel, src[0, 32 + 128 * j : 160 + 128 * j, :], NT)
            total = part if total is None else total + part
        return total.astype(BF)

    loads[1].wait()
    relayout(fin, xin)
    loads[2].wait()
    relayout(fcot, xcot)
    for n, src in enumerate((xin, xcot)):
        columns = extract(src)
        for t in range(2):
            tile = columns[16 * t : 16 * t + 16, :]
            zsend[t, 16 * n : 16 * n + 16, :] = tile
            for q in range(2):
                dsend[q, t, 16 * n : 16 * n + 16, :] = tile

    loads[0].wait()
    for x in range(16):
        cflat[80 * x + 8 : 80 * x + 72, :] = ccot[64 * x : 64 * x + 64, :].astype(F32)

    def column(y, z):
        return cflat[pl.ds(8 * y + z, 16, stride=80), :]

    for y in range(8):
        zsend[0, 32 + 16 * y : 48 + 16 * y, :] = column(y + 1, 0).astype(BF)
        zsend[1, 32 + 16 * y : 48 + 16 * y, :] = column(y + 1, 7).astype(BF)
    for s in range(2):
        own = (slice(32, 64), slice(0, 128)) if s == 0 else (slice(1024, 1056), slice(128, 256))
        ysend[s, 0:32, :] = xin[(0, *own)]
        ysend[s, 32:64, :] = xcot[(0, *own)]
        first = 8 if s == 0 else 64
        for x in range(0, 16, 2):
            pair = [cflat[80 * (x + q) + first : 80 * (x + q) + first + 8, :] for q in range(2)]
            ysend[s, 64 + 8 * x : 80 + 8 * x, :] = jnp.concatenate(pair, 0).astype(BF)
        for t in range(2):
            dsend[s, t, 32:48, :] = column(1 if s == 0 else 8, 0 if t == 0 else 7).astype(BF)

    pl.semaphore_wait(barrier, len(partners))

    step = (-1, 1)
    halo = []
    for s in range(2):
        halo.append(remote(ysend.at[s], yrecv.at[s], hs.at[s], hr.at[s], at(step[s], 0)))
        halo.append(remote(zsend.at[s], zrecv.at[s], hs.at[2 + s], hr.at[2 + s], at(0, step[s])))
        for t in range(2):
            q = 4 + 2 * s + t
            halo.append(
                remote(dsend.at[s, t], drecv.at[s, t], hs.at[q], hr.at[q], at(step[s], step[t]))
            )
    for copy in halo:
        copy.start()

    lane = iota((32, 768), 1)
    q, m = lane // 128, lane % 128
    k = 9 * ((m // 16) % 2 - q % 2 + 1) + 3 * (m // 32) + q // 2
    wanted = (m < 96, iota((32, 768), 0))
    straight = one_hot(wanted[0] & (wanted[1] == k))[:27]
    flipped = one_hot(wanted[0] & (wanted[1] == 26 - k))[:27]
    r, c = iota((256, 768), 0), iota((256, 768), 1)
    to_in, to_out = r % 16 == c % 16, r // 16 == c % 16
    r, c = iota((16, 256), 0), iota((16, 256), 1)
    by_out, by_in = one_hot(c // 16 == r), one_hot(c % 16 == r)
    loads[3].wait()
    loads[4].wait()
    for n, (w, pick, mask, rows) in enumerate(
        (
            (w1, straight, to_in, by_out),
            (w2, flipped, to_out, by_in),
            (w1, flipped, to_out, by_in),
        )
    ):
        wide = jnp.where(mask, mm(w[...], pick), 0.0).astype(BF)
        strips = mm(rows, wide)
        for cc in range(3):
            for xo in range(2):
                first = 128 * (2 * cc + xo)
                strip = strips[:, first : first + 128]
                strip = jnp.concatenate([strip, jnp.zeros_like(strip)], 1)
                for yo in range(4):
                    moved = strip if yo == 0 else pltpu.roll(strip, 32 * yo, 1)
                    first = 32 * yo + 16 * xo
                    bands[n, cc, first : first + 16, :] = moved.astype(BF)

    inp3[...] = jnp.zeros_like(inp3)
    loads[5].wait()
    for a in range(3):
        inp3[64 * (2 - a) : 64 * (2 - a) + 1024, 128 * a : 128 * a + 128] = cin[...]
    vmat[0] = jnp.zeros((64, 1152), BF)
    vmat[17] = jnp.zeros((64, 1152), BF)
    qf[...] = jnp.zeros_like(qf)

    for copy in halo:
        copy.wait()

    def valid(cond, value):
        return jnp.where(cond, value, jnp.zeros_like(value))

    for x in range(16):
        rows = slice(64 + 8 * (x // 2 * 2), 80 + 8 * (x // 2 * 2))
        half = slice(8 * (x % 2), 8 * (x % 2) + 8)
        cflat[80 * x : 80 * x + 8, :] = valid(up[0], yrecv[1, rows, :].astype(F32)[half])
        cflat[80 * x + 72 : 80 * x + 80, :] = valid(up[1], yrecv[0, rows, :].astype(F32)[half])
    cplus[...] = pltpu.roll(cflat[...], 1279, 0)
    cminus[...] = pltpu.roll(cflat[...], 1, 0)
    for y in range(10):
        for ref, z, t, ok in ((cplus, 7, 0, side[1]), (cminus, 0, 1, side[0])):
            if y == 0:
                part, ok = drecv[1, t, 32:48, :], ok & up[0]
            elif y == 9:
                part, ok = drecv[0, t, 32:48, :], ok & up[1]
            else:
                part = zrecv[t, 32 + 16 * (y - 1) : 48 + 16 * (y - 1), :]
            ref[pl.ds(8 * y + z, 16, stride=80), :] = valid(ok, part.astype(F32))

    def spread(x, carry):
        for b in range(3):
            for cc, ref in enumerate((cplus, cflat, cminus)):
                rows = ref[pl.ds(pl.multiple_of(x * 80 + 8 * (2 - b), 8), 64), :]
                q = 3 * b + cc
                vmat[x + 1, :, 128 * q : 128 * q + 128] = rows.astype(BF)
        return carry

    lax.fori_loop(0, 16, spread, 0)

    wide_o, nx = 128 // nty, nty // 2
    core, xme = lax.rem(ty, 2), lax.div(ty, 2)
    other = (dp, ty + 1 - 2 * core, tz)
    hop0 = []
    for b in range(3):
        left = vmat[:, :, 384 * b : 384 * b + 384].reshape(1152, 384)
        g = mm(left, inp3[...], TN)
        for a in range(3):
            for cc in range(3):
                part = g[128 * cc : 128 * cc + 128, 128 * a : 128 * a + 128]
                rsend[9 * b + 3 * a + cc] = part.astype(BF).reshape(nx, 2, wide_o, 128)
        src = rsend.at[pl.ds(9 * b, 9), :, 1 - core]
        hop0.append(remote(src, rpair.at[pl.ds(9 * b, 9)], ps.at[b], pr.at[b], other))
        hop0[b].start()
    hop1 = []
    for b in range(3):
        hop0[b].wait()
        for q in range(9 * b, 9 * b + 9):
            psum[q] = (rsend[q, :, core].astype(F32) + rpair[q].astype(F32)).astype(BF)
        for j in range(1, nx):
            x = lax.rem(xme + j, nx)
            src, dst = psum.at[pl.ds(9 * b, 9), x], rs1.at[xme, pl.ds(9 * b, 9)]
            dev = (dp, 2 * x + core, tz)
            hop1.append(remote(src, dst, r1s.at[b, j], r1r.at[b, nx - j], dev))
            hop1[-1].start()

    def turned(after, before):
        return jnp.concatenate([after, before], 0).astype(F32).T.astype(BF)

    def fill(dst, get_y, get_d, get_z):
        r, c = iota((32, 256), 0), iota((32, 256), 1)

        def place(row, ok):
            after = (r == row) & (c == 127) & side[1] & ok
            return one_hot(after | ((r == 16 + row) & (c == 128) & side[0] & ok))

        for s in (1, 0):
            ok = up[0] if s == 1 else up[1]
            mid = valid(ok, get_y(s))
            corner = turned(get_d(s, 0), get_d(s, 1))
            corner = corner[96:128] if s == 1 else corner[0:32]
            out = mm(mid, shifts[...]) + mm(corner, place(15 if s == 1 else 0, ok))
            rows, lanes = (slice(0, 32), slice(0, 128)) if s == 1 else (slice(1056, 1088), slice(128, 256))
            dst[0, rows, lanes] = mid
            dst[2, rows, lanes] = out[:, :128].astype(BF)
            dst[1, rows, lanes] = out[:, 128:].astype(BF)
        edge = turned(get_z(0), get_z(1))
        for h in range(2):
            lanes = slice(128 * h, 128 * h + 128)
            for j in range(8):
                rows = slice(32 + 128 * j, 160 + 128 * j)
                out = mm(dst[0, rows, lanes], shifts[...]) + mm(edge, place(8 * h + j, True))
                dst[2, rows, lanes] = out[:, :128].astype(BF)
                dst[1, rows, lanes] = out[:, 128:].astype(BF)
        for v in range(3):
            dst[v, 0:32, 128:256] = dst[v, 1024:1056, 0:128]
            dst[v, 1056:1088, 0:128] = dst[v, 32:64, 128:256]

    for n, dst in enumerate((xin, xcot)):
        rows, tile = slice(32 * n, 32 * n + 32), slice(16 * n, 16 * n + 16)
        fill(
            dst,
            lambda s, rows=rows: yrecv[s, rows, :],
            lambda s, t, tile=tile: drecv[s, t, tile, :],
            lambda t, tile=tile: zrecv[t, tile, :],
        )

    version = (1, 0, 2)

    def conv(n, src, g):
        rows = pl.ds(pl.multiple_of(g * 128, 128), 192)
        out = None
        for cc in range(3):
            term = mm(bands[n, cc, :, 0:192], src[version[cc], rows, :])
            out = term if out is None else out + term
        return out

    def forward(g, carry):
        pre = conv(0, xin, g)
        dact = conv(1, xcot, g)
        square = pre * pre
        t = jnp.tanh(C0 * pre * (1.0 + C1 * square))
        half = 0.5 + 0.5 * t
        slope = half + 0.5 * pre * (1.0 - t * t) * (C0 * (1.0 + (3.0 * C1) * square))
        act[pl.ds(pl.multiple_of(g * 128, 128), 128), :] = (pre * half).astype(BF)
        xdp[0, pl.ds(pl.multiple_of(g * 128 + 32, 32), 128), :] = (dact * slope).astype(BF)
        return carry

    lax.fori_loop(0, 8, forward, 0)

    columns = extract(xdp)
    zsend2[0] = columns[0:16]
    zsend2[1] = columns[16:32]
    ysend2[0] = xdp[0, 32:64, 0:128]
    ysend2[1] = xdp[0, 1024:1056, 128:256]
    halo2 = []
    for s in range(2):
        halo2.append(remote(ysend2.at[s], yrecv2.at[s], gs.at[s], gr.at[s], at(step[s], 0)))
        halo2.append(remote(zsend2.at[s], zrecv2.at[s], gs.at[2 + s], gr.at[2 + s], at(0, step[s])))
        for t in range(2):
            q = 4 + 2 * s + t
            dev = at(step[s], step[t])
            halo2.append(remote(zsend2.at[t], drecv2.at[s, t], gs.at[q], gr.at[q], dev))
    for copy in halo2:
        copy.start()

    acc1[...] = jnp.zeros_like(acc1)
    acc2[...] = jnp.zeros_like(acc2)

    def gram(g, carry):
        rows = pl.ds(pl.multiple_of(g * 128, 128), 192)
        own = xdp[0, pl.ds(pl.multiple_of(g * 128 + 32, 32), 128), :]
        a_own = act[pl.ds(pl.multiple_of(g * 128, 128), 128), :]
        for cc in range(3):
            acc1[cc, :, 0:192] += mm(own, xin[version[cc], rows, :], NT)
            acc2[cc] += mm(xcot[version[cc], rows, :], a_own, NT)
        return carry

    lax.fori_loop(0, 8, gram, 0)
    for cc in range(3):
        total = None
        for yo in range(4):
            part = acc1[cc, 32 * yo : 32 * yo + 32, :]
            part = part if yo == 0 else pltpu.roll(part, 256 - 32 * yo, 1)
            total = part if total is None else total + part
        fpart[32 * cc : 32 * cc + 32, :] = total[:, 0:128]
    total = jnp.zeros((96, 128), F32)
    lane = iota((96, 128), 1)
    for cc in range(3):
        band = None
        for yo in range(4):
            part = acc2[cc, 32 * yo : 32 * yo + 96, :]
            turn = (32 * cc - 32 * yo) % 128
            part = part if turn == 0 else pltpu.roll(part, turn, 1)
            band = part if band is None else band + part
        total = jnp.where(lane // 32 == cc, band, total)
    fpart[96:192, :] = total

    slab = 192 // nty
    hop_a = []
    for j in range(1, nty):
        t, dev = ty_peer(j)
        src = fpart.at[pl.ds(pl.multiple_of(t * slab, 8), slab), :]
        hop_a.append(remote(src, ar1.at[ty], a1s.at[j], a1r.at[nty - j], dev))
    for copy in hop_a:
        copy.start()
    ar1[ty] = fpart[pl.ds(pl.multiple_of(ty * slab, 8), slab), :]

    rs1[xme] = psum[:, xme]
    for copy in hop1:
        copy.wait()

    def sum1(q, carry):
        total = rs1[0, q].astype(F32)
        for t in range(1, nx):
            total = total + rs1[t, q].astype(F32)
        k = 9 * (lax.div(q, 3) % 3) + 3 * lax.div(q, 9) + q % 3
        qf[pl.ds(k, wide_o, stride=32), :] = total
        return carry

    lax.fori_loop(0, 27, sum1, 0)
    qb[...] = qf[...].astype(BF)
    deep = 32 * wide_o // ntz

    hop2 = []
    for j in range(1, zgroup):
        g, z, dev = z_peer(j)
        src = qb.at[pl.ds(pl.multiple_of(z * deep, 16), deep), :]
        hop2.append(remote(src, rs2.at[me], r2s.at[j], r2r.at[zgroup - j], dev))
    for copy in hop2:
        copy.start()
    rs2[me] = qb[pl.ds(pl.multiple_of(tz * deep, 16), deep), :]

    for copy in hop_a:
        copy.wait()
    total = ar1[0]
    for t in range(1, nty):
        total = total + ar1[t]
    fsum1[...] = total
    hop_b = []
    for j in range(1, zgroup):
        g, z, dev = z_peer(j)
        hop_b.append(remote(fsum1, ar2.at[me], a2s.at[j], a2r.at[zgroup - j], dev))
    for copy in hop_b:
        copy.start()
    ar2[me] = fsum1[...]

    loads[6].wait()

    def coarse(q, carry):
        out = None
        for a in range(3):
            left = vmat[pl.ds(q * 4 + 2 - a, 4)].reshape(256, 1152)
            term = mm(left, wc[1152 * a : 1152 * a + 1152, :])
            out = term if out is None else out + term
        o_gci[pl.ds(pl.multiple_of(q * 256, 256), 256), :] = out.astype(BF)
        return carry

    lax.fori_loop(0, 4, coarse, 0)

    for copy in hop_b:
        copy.wait()
    total = ar2[0]
    for t in range(1, zgroup):
        total = total + ar2[t]
    fsum2[...] = total
    hop_c = []
    for j in range(1, nty):
        t, dev = ty_peer(j)
        hop_c.append(remote(fsum2, gath.at[ty], a3s.at[j], a3r.at[nty - j], dev))
    for copy in hop_c:
        copy.start()
    gath[ty] = fsum2[...]

    for copy in halo2:
        copy.wait()
    fill(
        xdp,
        lambda s: yrecv2[s],
        lambda s, t: drecv2[s, t],
        lambda t: zrecv2[t],
    )

    def last(j, carry):
        parts = [conv(2, xdp, 4 * j + q).astype(BF) for q in range(4)]
        out = mm(perm[...], jnp.concatenate(parts, 0)).astype(BF)
        first = pl.multiple_of(16 * j, 16)
        o_gfi[:, pl.ds(first, 16), :] = out[:, :128].reshape(32, 16, 128)
        o_gfi[:, pl.ds(first + 32, 16), :] = out[:, 128:].reshape(32, 16, 128)
        return carry

    lax.fori_loop(0, 2, last, 0)

    for copy in hop2:
        copy.wait()
    total = rs2[0].astype(F32)
    for t in range(1, zgroup):
        total = total + rs2[t].astype(F32)
    for o in range(wide_o // ntz):
        o_gc[:, o, :] = total[32 * o : 32 * o + 27, :]

    for copy in hop_c:
        copy.wait()
    fpart[...] = gath[...].reshape(192, 128)
    for a in range(3):
        planes = [(xo, xo + a - 1) for xo in range(2) if 0 <= xo + a - 1 < 2]
        for b in range(3):
            for cc in range(3):
                k = 9 * a + 3 * b + cc
                one, two = None, None
                for xo, xi in planes:
                    first = 32 * cc + 16 * xo
                    lanes = slice(32 * b + 16 * xi, 32 * b + 16 * xi + 16)
                    part = fpart[first : first + 16, lanes]
                    one = part if one is None else one + part
                    first = 96 + 32 * b + 16 * xi
                    lanes = slice(32 * cc + 16 * xo, 32 * cc + 16 * xo + 16)
                    part = fpart[first : first + 16, lanes]
                    two = part if two is None else two + part
                o_gf[k] = one
                o_gs[26 - k] = two


def finish(gfi, gf, gs, gci, gc, o_gfi, o_gf, o_gs, o_gci, o_gc, v_gfi, v_gci, v_gc, sems):
    moves = ((gfi, v_gfi, o_gfi), (gci, v_gci, o_gci), (gc, v_gc, o_gc))
    into = [pltpu.make_async_copy(src, mid, sems.at[n]) for n, (src, mid, _) in enumerate(moves)]
    out = [pltpu.make_async_copy(mid, dst, sems.at[3 + n]) for n, (_, mid, dst) in enumerate(moves)]
    for copy in into:
        copy.start()
    for n in range(3):
        into[n].wait()
        out[n].start()
    for src, dst in ((gf, o_gf), (gs, o_gs)):
        for o in range(16):
            dst[o] = src[:, o, :].T
    for copy in out:
        copy.wait()


def solution(mesh):
    sizes = tuple(mesh.shape[a] for a in ("dp", "ty", "tz"))
    ndp, nty, ntz = sizes
    zgroup = ndp * ntz
    wide_o, nx = 128 // nty, nty // 2
    slab = 192 // nty

    def per_device(fine_input, fine_cotangent, first_weight, second_weight, coarse_input, coarse_cotangent, coarse_weight):
        def by_offset(w):
            return w.transpose(1, 2, 0).reshape(256, 27)

        dma = pltpu.SemaphoreType.DMA
        scratch = [
            pltpu.VMEM((32, 64, 128), BF),
            pltpu.VMEM((32, 64, 128), BF),
            pltpu.VMEM((256, 27), BF),
            pltpu.VMEM((256, 27), BF),
            pltpu.VMEM((1024, 128), BF),
            pltpu.VMEM((1024, 128), BF),
            pltpu.VMEM((3456, 128), BF),
            pltpu.VMEM((512, 512), BF),
            pltpu.VMEM((128, 256), BF),
            pltpu.VMEM((3, ROWS, 256), BF),
            pltpu.VMEM((3, ROWS, 256), BF),
            pltpu.VMEM((3, ROWS, 256), BF),
            pltpu.VMEM((1024, 256), BF),
            pltpu.VMEM((3, 3, 128, 256), BF),
            pltpu.VMEM((2, 192, 128), BF),
            pltpu.VMEM((2, 192, 128), BF),
            pltpu.VMEM((2, 160, 128), BF),
            pltpu.VMEM((2, 160, 128), BF),
            pltpu.VMEM((2, 2, 48, 128), BF),
            pltpu.VMEM((2, 2, 48, 128), BF),
            pltpu.VMEM((2, 32, 128), BF),
            pltpu.VMEM((2, 32, 128), BF),
            pltpu.VMEM((2, 16, 128), BF),
            pltpu.VMEM((2, 16, 128), BF),
            pltpu.VMEM((2, 2, 16, 128), BF),
            pltpu.VMEM((1280, 128), F32),
            pltpu.VMEM((1280, 128), F32),
            pltpu.VMEM((1280, 128), F32),
            pltpu.VMEM((18, 64, 1152), BF),
            pltpu.VMEM((1152, 384), BF),
            pltpu.VMEM((27, nx, 2, wide_o, 128), BF),
            pltpu.VMEM((27, nx, wide_o, 128), BF),
            pltpu.VMEM((27, nx, wide_o, 128), BF),
            pltpu.VMEM((nx, 27, wide_o, 128), BF),
            pltpu.VMEM((32 * wide_o, 128), F32),
            pltpu.VMEM((32 * wide_o, 128), BF),
            pltpu.VMEM((zgroup, 32 * wide_o // ntz, 128), BF),
            pltpu.VMEM((3, 128, 256), F32),
            pltpu.VMEM((3, 192, 128), F32),
            pltpu.VMEM((192, 128), F32),
            pltpu.VMEM((nty, slab, 128), F32),
            pltpu.VMEM((slab, 128), F32),
            pltpu.VMEM((zgroup, slab, 128), F32),
            pltpu.VMEM((slab, 128), F32),
            pltpu.VMEM((nty, slab, 128), F32),
            dma((7,)),
            dma((8,)),
            dma((8,)),
            dma((3,)),
            dma((3,)),
            dma((8,)),
            dma((8,)),
            dma((3, nx)),
            dma((3, nx)),
            dma((zgroup,)),
            dma((zgroup,)),
            dma((nty,)),
            dma((nty,)),
            dma((zgroup,)),
            dma((zgroup,)),
            dma((nty,)),
            dma((nty,)),
        ]
        vmem = pl.BlockSpec(memory_space=pltpu.VMEM)
        outs = pl.pallas_call(
            functools.partial(kernel, sizes),
            out_shape=(
                jax.ShapeDtypeStruct((32, 64, 128), BF),
                jax.ShapeDtypeStruct((27, 16, 16), F32),
                jax.ShapeDtypeStruct((27, 16, 16), F32),
                jax.ShapeDtypeStruct((1024, 128), BF),
                jax.ShapeDtypeStruct((27, wide_o // ntz, 128), F32),
            ),
            in_specs=[pl.BlockSpec(memory_space=pl.ANY)] * 7,
            out_specs=(vmem,) * 5,
            scratch_shapes=scratch,
            compiler_params=pltpu.CompilerParams(
                collective_id=0, has_side_effects=True, vmem_limit_bytes=60 * 1024 * 1024
            ),
        )(
            fine_input.reshape(32, 64, 128),
            fine_cotangent.reshape(32, 64, 128),
            by_offset(first_weight),
            by_offset(second_weight),
            coarse_input.reshape(1024, 128),
            coarse_cotangent.reshape(1024, 128),
            coarse_weight.reshape(3456, 128),
        )
        far = pl.BlockSpec(memory_space=pl.ANY)
        outs = pl.pallas_call(
            finish,
            out_shape=(
                jax.ShapeDtypeStruct((32, 64, 128), BF),
                jax.ShapeDtypeStruct((16, 16, 27), F32),
                jax.ShapeDtypeStruct((16, 16, 27), F32),
                jax.ShapeDtypeStruct((1024, 128), BF),
                jax.ShapeDtypeStruct((27, wide_o // ntz, 128), F32),
            ),
            in_specs=[far, vmem, vmem, far, far],
            out_specs=(far, vmem, vmem, far, far),
            scratch_shapes=[
                pltpu.VMEM((32, 64, 128), BF),
                pltpu.VMEM((1024, 128), BF),
                pltpu.VMEM((27, wide_o // ntz, 128), F32),
                dma((6,)),
            ],
            compiler_params=pltpu.CompilerParams(vmem_limit_bytes=60 * 1024 * 1024),
        )(*outs)
        return (
            outs[0].reshape(fine_input.shape),
            outs[1].transpose(2, 0, 1),
            outs[2].transpose(2, 0, 1),
            outs[3].reshape(coarse_input.shape),
            outs[4].transpose(1, 0, 2),
        )

    fine = P("dp", None, None, "ty", "tz")
    wide = P("dp", None, "ty", "tz", None)
    return jax.shard_map(
        per_device,
        mesh=mesh,
        in_specs=(fine, fine, P(), P(), wide, wide, P()),
        out_specs=(fine, P(), P(), wide, P(("ty", "tz"), None, None)),
        check_vma=False,
    )
```

```python
import functools

import jax
import jax.numpy as jnp
from jax import lax
from jax.experimental import pallas as pl
from jax.experimental.pallas import tpu as pltpu
from jax.sharding import PartitionSpec as P

MESH = pl.DeviceIdType.MESH
BF = jnp.bfloat16
F32 = jnp.float32
NN = (((1,), (0,)), ((), ()))
NT = (((1,), (1,)), ((), ()))
TN = (((0,), (0,)), ((), ()))
ROWS = 34 * 32
C0 = 0.7978845608028654
C1 = 0.044715


def mm(a, b, dims=NN):
    return lax.dot_general(a, b, dims, preferred_element_type=F32)


def iota(shape, dim):
    return lax.broadcasted_iota(jnp.int32, shape, dim)


def one_hot(cond):
    return jnp.where(cond, 1.0, 0.0).astype(BF)


def kernel(
    sizes,
    h_fin,
    h_fcot,
    h_w1,
    h_w2,
    h_cin,
    h_ccot,
    h_wc,
    o_gfi,
    o_gf,
    o_gs,
    o_gci,
    o_gc,
    fin,
    fcot,
    w1,
    w2,
    cin,
    ccot,
    wc,
    perm,
    shifts,
    xin,
    xcot,
    xdp,
    act,
    bands,
    ysend,
    yrecv,
    zsend,
    zrecv,
    drecv,
    ycs,
    ycr,
    zcs,
    zcr,
    dcs,
    dcr,
    ysend2,
    yrecv2,
    zsend2,
    zrecv2,
    drecv2,
    cflat,
    cplus,
    cminus,
    vmat,
    inp3,
    rsend,
    rpair,
    psum,
    rs1,
    qf,
    qb,
    rs2,
    g_gci,
    g_gfi,
    g_gf,
    g_gs,
    t_gf,
    t_gs,
    g_gc,
    acc1,
    acc2,
    fpart,
    ar1,
    fsum1,
    ar2,
    fsum2,
    gath,
    ls,
    hs,
    hr,
    cs,
    cr,
    ps,
    pr,
    gs,
    gr,
    r1s,
    r1r,
    r2s,
    r2r,
    a1s,
    a1r,
    a2s,
    a2r,
    a3s,
    a3r,
    ws,
):
    ndp, nty, ntz = sizes
    dp, ty, tz = lax.axis_index("dp"), lax.axis_index("ty"), lax.axis_index("tz")
    zgroup = ndp * ntz
    me = dp * ntz + tz

    def at(dy, dz):
        return (dp, lax.rem(ty + dy + nty, nty), lax.rem(tz + dz + ntz, ntz))

    def ty_peer(j):
        t = lax.rem(ty + j, nty)
        return t, (dp, t, tz)

    def z_peer(j):
        g = lax.rem(me + j, zgroup)
        z = lax.rem(g, ntz)
        return g, z, (lax.div(g, ntz), ty, z)

    def remote(src, dst, ssem, rsem, dev):
        return pltpu.make_async_remote_copy(
            src_ref=src,
            dst_ref=dst,
            send_sem=ssem,
            recv_sem=rsem,
            device_id=dev,
            device_id_type=MESH,
        )

    loads = []
    pairs = ((h_ccot, ccot), (h_fin, fin), (h_fcot, fcot), (h_w1, w1), (h_w2, w2), (h_cin, cin), (h_wc, wc))
    for n, (src, dst) in enumerate(pairs):
        loads.append(pltpu.make_async_copy(src, dst, ls.at[n]))
        loads[n].start()

    up = (ty > 0, ty < nty - 1)
    side = (tz > 0, tz < ntz - 1)

    barrier = pltpu.get_barrier_semaphore()
    partners = [at(dy, dz) for dy in (-1, 1) for dz in (-1, 1)]
    partners += [ty_peer(j)[1] for j in range(1, nty)]
    partners += [z_peer(j)[2] for j in range(1, zgroup)]
    for dev in partners:
        pl.semaphore_signal(barrier, inc=1, device_id=dev, device_id_type=MESH)

    r, c = iota((512, 512), 0), iota((512, 512), 1)
    perm[...] = one_hot(c == (r % 16) * 32 + ((r // 16) % 2) * 16 + r // 32)
    r, c = iota((128, 256), 0), iota((128, 256), 1)
    shifts[...] = one_hot(((r == c + 1) & (c < 127)) | ((r + 1 == c - 128) & (c > 128)))

    def relayout(src, dst):
        for j in range(2):
            left = src[:, 16 * j : 16 * j + 16, :].reshape(512, 128)
            right = src[:, 32 + 16 * j : 48 + 16 * j, :].reshape(512, 128)
            both = jnp.concatenate([left, right], 1)
            dst[0, 32 + 512 * j : 544 + 512 * j, :] = mm(perm[...], both).astype(BF)

    def extract(src):
        r, c = iota((32, 256), 0), iota((32, 256), 1)
        total = None
        for j in range(8):
            sel = one_hot((r % 16 == 8 * (c // 128) + j) & (c % 128 == 127 * (r // 16)))
            part = mm(sel, src[0, 32 + 128 * j : 160 + 128 * j, :], NT)
            total = part if total is None else total + part
        return total.astype(BF)

    loads[1].wait()
    relayout(fin, xin)
    loads[2].wait()
    relayout(fcot, xcot)
    for n, src in enumerate((xin, xcot)):
        columns = extract(src)
        for t in range(2):
            tile = columns[16 * t : 16 * t + 16, :]
            zsend[t, 16 * n : 16 * n + 16, :] = tile

    loads[0].wait()
    for x in range(16):
        cflat[80 * x + 8 : 80 * x + 72, :] = ccot[64 * x : 64 * x + 64, :].astype(F32)

    def column(y, z):
        return cflat[pl.ds(8 * y + z, 16, stride=80), :]

    for y in range(8):
        zcs[0, 16 * y : 16 * y + 16, :] = column(y + 1, 0).astype(BF)
        zcs[1, 16 * y : 16 * y + 16, :] = column(y + 1, 7).astype(BF)
    for s in range(2):
        own = (slice(32, 64), slice(0, 128)) if s == 0 else (slice(1024, 1056), slice(128, 256))
        ysend[s, 0:32, :] = xin[(0, *own)]
        ysend[s, 32:64, :] = xcot[(0, *own)]
        first = 8 if s == 0 else 64
        for x in range(0, 16, 2):
            pair = [cflat[80 * (x + q) + first : 80 * (x + q) + first + 8, :] for q in range(2)]
            ycs[s, 8 * x : 8 * x + 16, :] = jnp.concatenate(pair, 0).astype(BF)
        for t in range(2):
            dcs[s, t] = column(1 if s == 0 else 8, 0 if t == 0 else 7).astype(BF)

    pl.semaphore_wait(barrier, len(partners))

    step = (-1, 1)
    halo, halo_c = [], []
    for s in range(2):
        for t in range(2):
            q, dev = 4 + 2 * s + t, at(step[s], step[t])
            halo.append(remote(zsend.at[t], drecv.at[s, t], hs.at[q], hr.at[q], dev))
            halo_c.append(remote(dcs.at[s, t], dcr.at[s, t], cs.at[q], cr.at[q], dev))
        y, z, q = at(step[s], 0), at(0, step[s]), 2 + s
        halo.append(remote(zsend.at[s], zrecv.at[s], hs.at[q], hr.at[q], z))
        halo.append(remote(ysend.at[s], yrecv.at[s], hs.at[s], hr.at[s], y))
        halo_c.append(remote(zcs.at[s], zcr.at[s], cs.at[q], cr.at[q], z))
        halo_c.append(remote(ycs.at[s], ycr.at[s], cs.at[s], cr.at[s], y))
    for copy in halo + halo_c:
        copy.start()

    lane = iota((32, 768), 1)
    q, m = lane // 128, lane % 128
    k = 9 * ((m // 16) % 2 - q % 2 + 1) + 3 * (m // 32) + q // 2
    wanted = (m < 96, iota((32, 768), 0))
    straight = one_hot(wanted[0] & (wanted[1] == k))[:27]
    flipped = one_hot(wanted[0] & (wanted[1] == 26 - k))[:27]
    r, c = iota((256, 768), 0), iota((256, 768), 1)
    to_in, to_out = r % 16 == c % 16, r // 16 == c % 16
    r, c = iota((16, 256), 0), iota((16, 256), 1)
    by_out, by_in = one_hot(c // 16 == r), one_hot(c % 16 == r)
    loads[3].wait()
    loads[4].wait()
    for n, (w, pick, mask, rows) in enumerate(
        (
            (w1, straight, to_in, by_out),
            (w2, flipped, to_out, by_in),
            (w1, flipped, to_out, by_in),
        )
    ):
        wide = jnp.where(mask, mm(w[...], pick), 0.0).astype(BF)
        strips = mm(rows, wide)
        for cc in range(3):
            for xo in range(2):
                first = 128 * (2 * cc + xo)
                strip = strips[:, first : first + 128]
                strip = jnp.concatenate([strip, jnp.zeros_like(strip)], 1)
                for yo in range(4):
                    moved = strip if yo == 0 else pltpu.roll(strip, 32 * yo, 1)
                    first = 32 * yo + 16 * xo
                    bands[n, cc, first : first + 16, :] = moved.astype(BF)

    inp3[...] = jnp.zeros_like(inp3)
    loads[5].wait()
    for a in range(3):
        inp3[64 * (2 - a) : 64 * (2 - a) + 1024, 128 * a : 128 * a + 128] = cin[...]
    vmat[0] = jnp.zeros((64, 1152), BF)
    vmat[17] = jnp.zeros((64, 1152), BF)
    qf[...] = jnp.zeros_like(qf)

    def valid(cond, value):
        return jnp.where(cond, value, jnp.zeros_like(value))

    for copy in halo:
        copy.wait()

    def turned(after, before):
        return jnp.concatenate([after, before], 0).astype(F32).T.astype(BF)

    def fill(dst, get_y, get_d, get_z):
        r, c = iota((32, 256), 0), iota((32, 256), 1)

        def place(row, ok):
            after = (r == row) & (c == 127) & side[1] & ok
            return one_hot(after | ((r == 16 + row) & (c == 128) & side[0] & ok))

        for s in (1, 0):
            ok = up[0] if s == 1 else up[1]
            mid = valid(ok, get_y(s))
            corner = turned(get_d(s, 0), get_d(s, 1))
            corner = corner[96:128] if s == 1 else corner[0:32]
            out = mm(mid, shifts[...]) + mm(corner, place(15 if s == 1 else 0, ok))
            rows, lanes = (slice(0, 32), slice(0, 128)) if s == 1 else (slice(1056, 1088), slice(128, 256))
            dst[0, rows, lanes] = mid
            dst[2, rows, lanes] = out[:, :128].astype(BF)
            dst[1, rows, lanes] = out[:, 128:].astype(BF)
        edge = turned(get_z(0), get_z(1))
        for h in range(2):
            lanes = slice(128 * h, 128 * h + 128)
            for j in range(8):
                rows = slice(32 + 128 * j, 160 + 128 * j)
                out = mm(dst[0, rows, lanes], shifts[...]) + mm(edge, place(8 * h + j, True))
                dst[2, rows, lanes] = out[:, :128].astype(BF)
                dst[1, rows, lanes] = out[:, 128:].astype(BF)
        for v in range(3):
            dst[v, 0:32, 128:256] = dst[v, 1024:1056, 0:128]
            dst[v, 1056:1088, 0:128] = dst[v, 32:64, 128:256]

    for n, dst in enumerate((xin, xcot)):
        rows, tile = slice(32 * n, 32 * n + 32), slice(16 * n, 16 * n + 16)
        fill(
            dst,
            lambda s, rows=rows: yrecv[s, rows, :],
            lambda s, t, tile=tile: drecv[s, t, tile, :],
            lambda t, tile=tile: zrecv[t, tile, :],
        )

    version = (1, 0, 2)

    def conv(n, src, g):
        rows = pl.ds(pl.multiple_of(g * 128, 128), 192)
        out = None
        for cc in range(3):
            term = mm(bands[n, cc, :, 0:192], src[version[cc], rows, :])
            out = term if out is None else out + term
        return out

    def forward(g, carry):
        pre = conv(0, xin, g)
        dact = conv(1, xcot, g)
        square = pre * pre
        t = jnp.tanh(C0 * pre * (1.0 + C1 * square))
        half = 0.5 + 0.5 * t
        slope = half + 0.5 * pre * (1.0 - t * t) * (C0 * (1.0 + (3.0 * C1) * square))
        act[pl.ds(pl.multiple_of(g * 128, 128), 128), :] = (pre * half).astype(BF)
        xdp[0, pl.ds(pl.multiple_of(g * 128 + 32, 32), 128), :] = (dact * slope).astype(BF)
        return carry

    lax.fori_loop(0, 8, forward, 0)

    columns = extract(xdp)
    zsend2[0] = columns[0:16]
    zsend2[1] = columns[16:32]
    ysend2[0] = xdp[0, 32:64, 0:128]
    ysend2[1] = xdp[0, 1024:1056, 128:256]
    halo2 = []
    for s in range(2):
        halo2.append(remote(ysend2.at[s], yrecv2.at[s], gs.at[s], gr.at[s], at(step[s], 0)))
        halo2.append(remote(zsend2.at[s], zrecv2.at[s], gs.at[2 + s], gr.at[2 + s], at(0, step[s])))
        for t in range(2):
            q = 4 + 2 * s + t
            dev = at(step[s], step[t])
            halo2.append(remote(zsend2.at[t], drecv2.at[s, t], gs.at[q], gr.at[q], dev))
    for copy in halo2:
        copy.start()

    for copy in halo_c:
        copy.wait()
    for x in range(16):
        rows = slice(8 * (x // 2 * 2), 16 + 8 * (x // 2 * 2))
        half = slice(8 * (x % 2), 8 * (x % 2) + 8)
        cflat[80 * x : 80 * x + 8, :] = valid(up[0], ycr[1, rows, :].astype(F32)[half])
        cflat[80 * x + 72 : 80 * x + 80, :] = valid(up[1], ycr[0, rows, :].astype(F32)[half])
    cplus[...] = pltpu.roll(cflat[...], 1279, 0)
    cminus[...] = pltpu.roll(cflat[...], 1, 0)
    for y in range(10):
        for ref, z, t, ok in ((cplus, 7, 0, side[1]), (cminus, 0, 1, side[0])):
            if y == 0:
                part, ok = dcr[1, t], ok & up[0]
            elif y == 9:
                part, ok = dcr[0, t], ok & up[1]
            else:
                part = zcr[t, 16 * (y - 1) : 16 * y, :]
            ref[pl.ds(8 * y + z, 16, stride=80), :] = valid(ok, part.astype(F32))

    def spread(x, carry):
        for b in range(3):
            for cc, ref in enumerate((cplus, cflat, cminus)):
                rows = ref[pl.ds(pl.multiple_of(x * 80 + 8 * (2 - b), 8), 64), :]
                q = 3 * b + cc
                vmat[x + 1, :, 128 * q : 128 * q + 128] = rows.astype(BF)
        return carry

    lax.fori_loop(0, 16, spread, 0)

    wide_o, nx = 128 // nty, nty // 2
    core, xme = lax.rem(ty, 2), lax.div(ty, 2)
    other = (dp, ty + 1 - 2 * core, tz)
    hop0 = []
    for b in range(3):
        left = vmat[:, :, 384 * b : 384 * b + 384].reshape(1152, 384)
        g = mm(left, inp3[...], TN)
        for a in range(3):
            for cc in range(3):
                part = g[128 * cc : 128 * cc + 128, 128 * a : 128 * a + 128]
                rsend[9 * b + 3 * a + cc] = part.astype(BF).reshape(nx, 2, wide_o, 128)
        src = rsend.at[pl.ds(9 * b, 9), :, 1 - core]
        hop0.append(remote(src, rpair.at[pl.ds(9 * b, 9)], ps.at[b], pr.at[b], other))
        hop0[b].start()

    acc1[...] = jnp.zeros_like(acc1)
    acc2[...] = jnp.zeros_like(acc2)

    def gram(g, carry):
        rows = pl.ds(pl.multiple_of(g * 128, 128), 192)
        own = xdp[0, pl.ds(pl.multiple_of(g * 128 + 32, 32), 128), :]
        a_own = act[pl.ds(pl.multiple_of(g * 128, 128), 128), :]
        for cc in range(3):
            acc1[cc, :, 0:192] += mm(own, xin[version[cc], rows, :], NT)
            acc2[cc] += mm(xcot[version[cc], rows, :], a_own, NT)
        return carry

    lax.fori_loop(0, 8, gram, 0)
    for cc in range(3):
        total = None
        for yo in range(4):
            part = acc1[cc, 32 * yo : 32 * yo + 32, :]
            part = part if yo == 0 else pltpu.roll(part, 256 - 32 * yo, 1)
            total = part if total is None else total + part
        fpart[32 * cc : 32 * cc + 32, :] = total[:, 0:128]
    total = jnp.zeros((96, 128), F32)
    lane = iota((96, 128), 1)
    for cc in range(3):
        band = None
        for yo in range(4):
            part = acc2[cc, 32 * yo : 32 * yo + 96, :]
            turn = (32 * cc - 32 * yo) % 128
            part = part if turn == 0 else pltpu.roll(part, turn, 1)
            band = part if band is None else band + part
        total = jnp.where(lane // 32 == cc, band, total)
    fpart[96:192, :] = total

    slab = 192 // nty
    hop_a = []
    for j in range(1, nty):
        t, dev = ty_peer(j)
        src = fpart.at[pl.ds(pl.multiple_of(t * slab, 8), slab), :]
        hop_a.append(remote(src, ar1.at[ty], a1s.at[j], a1r.at[nty - j], dev))
    for copy in hop_a:
        copy.start()
    ar1[ty] = fpart[pl.ds(pl.multiple_of(ty * slab, 8), slab), :]

    hop1 = []
    for b in range(3):
        hop0[b].wait()
        for q in range(9 * b, 9 * b + 9):
            psum[q] = (rsend[q, :, core].astype(F32) + rpair[q].astype(F32)).astype(BF)
        for j in range(1, nx):
            x = lax.rem(xme + j, nx)
            src, dst = psum.at[pl.ds(9 * b, 9), x], rs1.at[xme, pl.ds(9 * b, 9)]
            dev = (dp, 2 * x + core, tz)
            hop1.append(remote(src, dst, r1s.at[b, j], r1r.at[b, nx - j], dev))
            hop1[-1].start()

    loads[6].wait()

    def coarse(q, carry):
        out = None
        for a in range(3):
            left = vmat[pl.ds(q * 4 + 2 - a, 4)].reshape(256, 1152)
            term = mm(left, wc[1152 * a : 1152 * a + 1152, :])
            out = term if out is None else out + term
        g_gci[pl.ds(pl.multiple_of(q * 256, 256), 256), :] = out.astype(BF)
        return carry

    lax.fori_loop(0, 4, coarse, 0)
    stores = [pltpu.make_async_copy(g_gci, o_gci, ws.at[0])]
    stores[0].start()

    for copy in hop_a:
        copy.wait()
    total = ar1[0]
    for t in range(1, nty):
        total = total + ar1[t]
    fsum1[...] = total
    hop_b = []
    for j in range(1, zgroup):
        g, z, dev = z_peer(j)
        hop_b.append(remote(fsum1, ar2.at[me], a2s.at[j], a2r.at[zgroup - j], dev))
    for copy in hop_b:
        copy.start()
    ar2[me] = fsum1[...]

    for copy in halo2:
        copy.wait()
    fill(
        xdp,
        lambda s: yrecv2[s],
        lambda s, t: drecv2[s, t],
        lambda t: zrecv2[t],
    )

    def last(j, carry):
        parts = [conv(2, xdp, 4 * j + q).astype(BF) for q in range(4)]
        out = mm(perm[...], jnp.concatenate(parts, 0)).astype(BF)
        first = pl.multiple_of(16 * j, 16)
        g_gfi[:, pl.ds(first, 16), :] = out[:, :128].reshape(32, 16, 128)
        g_gfi[:, pl.ds(first + 32, 16), :] = out[:, 128:].reshape(32, 16, 128)
        return carry

    lax.fori_loop(0, 2, last, 0)
    stores.append(pltpu.make_async_copy(g_gfi, o_gfi, ws.at[1]))
    stores[1].start()

    for copy in hop_b:
        copy.wait()
    total = ar2[0]
    for t in range(1, zgroup):
        total = total + ar2[t]
    fsum2[...] = total
    hop_c = []
    for j in range(1, nty):
        t, dev = ty_peer(j)
        hop_c.append(remote(fsum2, gath.at[ty], a3s.at[j], a3r.at[nty - j], dev))
    for copy in hop_c:
        copy.start()
    gath[ty] = fsum2[...]

    rs1[xme] = psum[:, xme]
    for copy in hop1:
        copy.wait()

    def sum1(q, carry):
        total = rs1[0, q].astype(F32)
        for t in range(1, nx):
            total = total + rs1[t, q].astype(F32)
        k = 9 * (lax.div(q, 3) % 3) + 3 * lax.div(q, 9) + q % 3
        qf[pl.ds(k, wide_o, stride=32), :] = total
        return carry

    lax.fori_loop(0, 27, sum1, 0)
    qb[...] = qf[...].astype(BF)
    deep = 32 * wide_o // ntz

    hop2 = []
    for j in range(1, zgroup):
        g, z, dev = z_peer(j)
        src = qb.at[pl.ds(pl.multiple_of(z * deep, 16), deep), :]
        hop2.append(remote(src, rs2.at[me], r2s.at[j], r2r.at[zgroup - j], dev))
    for copy in hop2:
        copy.start()
    rs2[me] = qb[pl.ds(pl.multiple_of(tz * deep, 16), deep), :]

    for copy in hop_c:
        copy.wait()
    fpart[...] = gath[...].reshape(192, 128)
    for a in range(3):
        planes = [(xo, xo + a - 1) for xo in range(2) if 0 <= xo + a - 1 < 2]
        for b in range(3):
            for cc in range(3):
                k = 9 * a + 3 * b + cc
                one, two = None, None
                for xo, xi in planes:
                    first = 32 * cc + 16 * xo
                    lanes = slice(32 * b + 16 * xi, 32 * b + 16 * xi + 16)
                    part = fpart[first : first + 16, lanes]
                    one = part if one is None else one + part
                    first = 96 + 32 * b + 16 * xi
                    lanes = slice(32 * cc + 16 * xo, 32 * cc + 16 * xo + 16)
                    part = fpart[first : first + 16, lanes]
                    two = part if two is None else two + part
                g_gf[k] = one
                g_gs[26 - k] = two
    for n, (src, mid, dst) in enumerate(((g_gf, t_gf, o_gf), (g_gs, t_gs, o_gs))):
        for o in range(16):
            mid[o] = src[:, o, :].T
        stores.append(pltpu.make_async_copy(mid, dst, ws.at[2 + n]))
        stores[2 + n].start()

    for copy in hop2:
        copy.wait()
    total = rs2[0].astype(F32)
    for t in range(1, zgroup):
        total = total + rs2[t].astype(F32)
    for o in range(wide_o // ntz):
        g_gc[:, o, :] = total[32 * o : 32 * o + 27, :]
    stores.append(pltpu.make_async_copy(g_gc, o_gc, ws.at[4]))
    stores[4].start()
    for copy in stores:
        copy.wait()


def finish(*refs):
    srcs, dsts, mids, sems = refs[:5], refs[5:10], refs[10:15], refs[15]
    into = [pltpu.make_async_copy(srcs[n], mids[n], sems.at[n]) for n in range(5)]
    out = [pltpu.make_async_copy(mids[n], dsts[n], sems.at[5 + n]) for n in range(5)]
    for copy in into:
        copy.start()
    for n in range(5):
        into[n].wait()
        out[n].start()
    for copy in out:
        copy.wait()


def solution(mesh):
    sizes = tuple(mesh.shape[a] for a in ("dp", "ty", "tz"))
    ndp, nty, ntz = sizes
    zgroup = ndp * ntz
    wide_o, nx = 128 // nty, nty // 2
    slab = 192 // nty

    def per_device(fine_input, fine_cotangent, first_weight, second_weight, coarse_input, coarse_cotangent, coarse_weight):
        def by_offset(w):
            return w.transpose(1, 2, 0).reshape(256, 27)

        dma = pltpu.SemaphoreType.DMA
        scratch = [
            pltpu.VMEM((32, 64, 128), BF),
            pltpu.VMEM((32, 64, 128), BF),
            pltpu.VMEM((256, 27), BF),
            pltpu.VMEM((256, 27), BF),
            pltpu.VMEM((1024, 128), BF),
            pltpu.VMEM((1024, 128), BF),
            pltpu.VMEM((3456, 128), BF),
            pltpu.VMEM((512, 512), BF),
            pltpu.VMEM((128, 256), BF),
            pltpu.VMEM((3, ROWS, 256), BF),
            pltpu.VMEM((3, ROWS, 256), BF),
            pltpu.VMEM((3, ROWS, 256), BF),
            pltpu.VMEM((1024, 256), BF),
            pltpu.VMEM((3, 3, 128, 256), BF),
            pltpu.VMEM((2, 64, 128), BF),
            pltpu.VMEM((2, 64, 128), BF),
            pltpu.VMEM((2, 32, 128), BF),
            pltpu.VMEM((2, 32, 128), BF),
            pltpu.VMEM((2, 2, 32, 128), BF),
            pltpu.VMEM((2, 128, 128), BF),
            pltpu.VMEM((2, 128, 128), BF),
            pltpu.VMEM((2, 128, 128), BF),
            pltpu.VMEM((2, 128, 128), BF),
            pltpu.VMEM((2, 2, 16, 128), BF),
            pltpu.VMEM((2, 2, 16, 128), BF),
            pltpu.VMEM((2, 32, 128), BF),
            pltpu.VMEM((2, 32, 128), BF),
            pltpu.VMEM((2, 16, 128), BF),
            pltpu.VMEM((2, 16, 128), BF),
            pltpu.VMEM((2, 2, 16, 128), BF),
            pltpu.VMEM((1280, 128), F32),
            pltpu.VMEM((1280, 128), F32),
            pltpu.VMEM((1280, 128), F32),
            pltpu.VMEM((18, 64, 1152), BF),
            pltpu.VMEM((1152, 384), BF),
            pltpu.VMEM((27, nx, 2, wide_o, 128), BF),
            pltpu.VMEM((27, nx, wide_o, 128), BF),
            pltpu.VMEM((27, nx, wide_o, 128), BF),
            pltpu.VMEM((nx, 27, wide_o, 128), BF),
            pltpu.VMEM((32 * wide_o, 128), F32),
            pltpu.VMEM((32 * wide_o, 128), BF),
            pltpu.VMEM((zgroup, 32 * wide_o // ntz, 128), BF),
            pltpu.VMEM((1024, 128), BF),
            pltpu.VMEM((32, 64, 128), BF),
            pltpu.VMEM((27, 16, 16), F32),
            pltpu.VMEM((27, 16, 16), F32),
            pltpu.VMEM((16, 16, 27), F32),
            pltpu.VMEM((16, 16, 27), F32),
            pltpu.VMEM((27, wide_o // ntz, 128), F32),
            pltpu.VMEM((3, 128, 256), F32),
            pltpu.VMEM((3, 192, 128), F32),
            pltpu.VMEM((192, 128), F32),
            pltpu.VMEM((nty, slab, 128), F32),
            pltpu.VMEM((slab, 128), F32),
            pltpu.VMEM((zgroup, slab, 128), F32),
            pltpu.VMEM((slab, 128), F32),
            pltpu.VMEM((nty, slab, 128), F32),
            dma((7,)),
            dma((8,)),
            dma((8,)),
            dma((8,)),
            dma((8,)),
            dma((3,)),
            dma((3,)),
            dma((8,)),
            dma((8,)),
            dma((3, nx)),
            dma((3, nx)),
            dma((zgroup,)),
            dma((zgroup,)),
            dma((nty,)),
            dma((nty,)),
            dma((zgroup,)),
            dma((zgroup,)),
            dma((nty,)),
            dma((nty,)),
            dma((5,)),
        ]
        outs = pl.pallas_call(
            functools.partial(kernel, sizes),
            out_shape=(
                jax.ShapeDtypeStruct((32, 64, 128), BF),
                jax.ShapeDtypeStruct((16, 16, 27), F32),
                jax.ShapeDtypeStruct((16, 16, 27), F32),
                jax.ShapeDtypeStruct((1024, 128), BF),
                jax.ShapeDtypeStruct((27, wide_o // ntz, 128), F32),
            ),
            in_specs=[pl.BlockSpec(memory_space=pl.ANY)] * 7,
            out_specs=(pl.BlockSpec(memory_space=pl.ANY),) * 5,
            scratch_shapes=scratch,
            compiler_params=pltpu.CompilerParams(
                collective_id=0, has_side_effects=True, vmem_limit_bytes=60 * 1024 * 1024
            ),
        )(
            fine_input.reshape(32, 64, 128),
            fine_cotangent.reshape(32, 64, 128),
            by_offset(first_weight),
            by_offset(second_weight),
            coarse_input.reshape(1024, 128),
            coarse_cotangent.reshape(1024, 128),
            coarse_weight.reshape(3456, 128),
        )
        far = pl.BlockSpec(memory_space=pl.ANY)
        outs = pl.pallas_call(
            finish,
            out_shape=(
                jax.ShapeDtypeStruct((32, 64, 128), BF),
                jax.ShapeDtypeStruct((16, 16, 27), F32),
                jax.ShapeDtypeStruct((16, 16, 27), F32),
                jax.ShapeDtypeStruct((1024, 128), BF),
                jax.ShapeDtypeStruct((27, wide_o // ntz, 128), F32),
            ),
            in_specs=[far] * 5,
            out_specs=(far,) * 5,
            scratch_shapes=[
                pltpu.VMEM((32, 64, 128), BF),
                pltpu.VMEM((16, 16, 27), F32),
                pltpu.VMEM((16, 16, 27), F32),
                pltpu.VMEM((1024, 128), BF),
                pltpu.VMEM((27, wide_o // ntz, 128), F32),
                dma((10,)),
            ],
            compiler_params=pltpu.CompilerParams(vmem_limit_bytes=60 * 1024 * 1024),
        )(*outs)
        return (
            outs[0].reshape(fine_input.shape),
            outs[1].transpose(2, 0, 1),
            outs[2].transpose(2, 0, 1),
            outs[3].reshape(coarse_input.shape),
            outs[4].transpose(1, 0, 2),
        )

    fine = P("dp", None, None, "ty", "tz")
    wide = P("dp", None, "ty", "tz", None)
    return jax.shard_map(
        per_device,
        mesh=mesh,
        in_specs=(fine, fine, P(), P(), wide, wide, P()),
        out_specs=(fine, P(), P(), wide, P(("ty", "tz"), None, None)),
        check_vma=False,
    )
```

```python
import functools

import jax
import jax.numpy as jnp
from jax import lax
from jax.experimental import pallas as pl
from jax.experimental.pallas import tpu as pltpu
from jax.sharding import PartitionSpec as P

MESH = pl.DeviceIdType.MESH
BF = jnp.bfloat16
F32 = jnp.float32
NN = (((1,), (0,)), ((), ()))
NT = (((1,), (1,)), ((), ()))
TN = (((0,), (0,)), ((), ()))
ROWS = 34 * 32
C0 = 0.7978845608028654
C1 = 0.044715


def mm(a, b, dims=NN):
    return lax.dot_general(a, b, dims, preferred_element_type=F32)


def iota(shape, dim):
    return lax.broadcasted_iota(jnp.int32, shape, dim)


def one_hot(cond):
    return jnp.where(cond, 1.0, 0.0).astype(BF)


def kernel(
    sizes,
    h_fin,
    h_fcot,
    h_w1,
    h_w2,
    h_cin,
    h_ccot,
    h_wc,
    o_gfi,
    o_gf,
    o_gs,
    o_gci,
    o_gc,
    fin,
    fcot,
    w1,
    w2,
    cin,
    ccot,
    wc,
    perm,
    shifts,
    xin,
    xcot,
    xdp,
    act,
    bands,
    ysend,
    yrecv,
    zsend,
    zrecv,
    drecv,
    ycs,
    ycr,
    zcs,
    zcr,
    dcs,
    dcr,
    ysend2,
    yrecv2,
    zsend2,
    zrecv2,
    drecv2,
    cflat,
    cplus,
    cminus,
    vmat,
    inp3,
    rsend,
    rpair,
    psum,
    rs1,
    qf,
    qb,
    rs2,
    g_gci,
    g_gfi,
    g_gf,
    g_gs,
    t_gf,
    t_gs,
    g_gc,
    acc1,
    acc2,
    fpart,
    ar1,
    fsum1,
    ar2,
    fsum2,
    gath,
    ls,
    hs,
    hr,
    cs,
    cr,
    ps,
    pr,
    gs,
    gr,
    r1s,
    r1r,
    r2s,
    r2r,
    a1s,
    a1r,
    a2s,
    a2r,
    a3s,
    a3r,
    ws,
):
    ndp, nty, ntz = sizes
    dp, ty, tz = lax.axis_index("dp"), lax.axis_index("ty"), lax.axis_index("tz")
    zgroup = ndp * ntz
    me = dp * ntz + tz

    def at(dy, dz):
        return (dp, lax.rem(ty + dy + nty, nty), lax.rem(tz + dz + ntz, ntz))

    def ty_peer(j):
        t = lax.rem(ty + j, nty)
        return t, (dp, t, tz)

    def z_peer(j):
        g = lax.rem(me + j, zgroup)
        z = lax.rem(g, ntz)
        return g, z, (lax.div(g, ntz), ty, z)

    def remote(src, dst, ssem, rsem, dev):
        return pltpu.make_async_remote_copy(
            src_ref=src,
            dst_ref=dst,
            send_sem=ssem,
            recv_sem=rsem,
            device_id=dev,
            device_id_type=MESH,
        )

    loads = []
    pairs = ((h_ccot, ccot), (h_fin, fin), (h_fcot, fcot), (h_w1, w1), (h_w2, w2), (h_cin, cin), (h_wc, wc))
    for n, (src, dst) in enumerate(pairs):
        loads.append(pltpu.make_async_copy(src, dst, ls.at[n]))
        loads[n].start()

    up = (ty > 0, ty < nty - 1)
    side = (tz > 0, tz < ntz - 1)

    barrier = pltpu.get_barrier_semaphore()
    partners = [at(dy, dz) for dy in (-1, 1) for dz in (-1, 1)]
    partners += [ty_peer(j)[1] for j in range(1, nty)]
    partners += [z_peer(j)[2] for j in range(1, zgroup)]
    for dev in partners:
        pl.semaphore_signal(barrier, inc=1, device_id=dev, device_id_type=MESH)

    r, c = iota((512, 512), 0), iota((512, 512), 1)
    perm[...] = one_hot(c == (r % 16) * 32 + ((r // 16) % 2) * 16 + r // 32)
    r, c = iota((128, 256), 0), iota((128, 256), 1)
    shifts[...] = one_hot(((r == c + 1) & (c < 127)) | ((r + 1 == c - 128) & (c > 128)))

    def relayout(src, dst):
        for j in range(2):
            left = src[:, 16 * j : 16 * j + 16, :].reshape(512, 128)
            right = src[:, 32 + 16 * j : 48 + 16 * j, :].reshape(512, 128)
            both = jnp.concatenate([left, right], 1)
            dst[0, 32 + 512 * j : 544 + 512 * j, :] = mm(perm[...], both).astype(BF)

    def extract(src):
        r, c = iota((32, 256), 0), iota((32, 256), 1)
        total = None
        for j in range(8):
            sel = one_hot((r % 16 == 8 * (c // 128) + j) & (c % 128 == 127 * (r // 16)))
            part = mm(sel, src[0, 32 + 128 * j : 160 + 128 * j, :], NT)
            total = part if total is None else total + part
        return total.astype(BF)

    loads[1].wait()
    relayout(fin, xin)
    loads[2].wait()
    relayout(fcot, xcot)
    for n, src in enumerate((xin, xcot)):
        columns = extract(src)
        for t in range(2):
            tile = columns[16 * t : 16 * t + 16, :]
            zsend[t, 16 * n : 16 * n + 16, :] = tile

    loads[0].wait()
    for x in range(16):
        cflat[80 * x + 8 : 80 * x + 72, :] = ccot[64 * x : 64 * x + 64, :].astype(F32)

    def column(y, z):
        return cflat[pl.ds(8 * y + z, 16, stride=80), :]

    for y in range(8):
        zcs[0, 16 * y : 16 * y + 16, :] = column(y + 1, 0).astype(BF)
        zcs[1, 16 * y : 16 * y + 16, :] = column(y + 1, 7).astype(BF)
    for s in range(2):
        own = (slice(32, 64), slice(0, 128)) if s == 0 else (slice(1024, 1056), slice(128, 256))
        ysend[s, 0:32, :] = xin[(0, *own)]
        ysend[s, 32:64, :] = xcot[(0, *own)]
        first = 8 if s == 0 else 64
        for x in range(0, 16, 2):
            pair = [cflat[80 * (x + q) + first : 80 * (x + q) + first + 8, :] for q in range(2)]
            ycs[s, 8 * x : 8 * x + 16, :] = jnp.concatenate(pair, 0).astype(BF)
        for t in range(2):
            dcs[s, t] = column(1 if s == 0 else 8, 0 if t == 0 else 7).astype(BF)

    pl.semaphore_wait(barrier, len(partners))

    step = (-1, 1)
    halo, halo_c = [], []
    for s in range(2):
        for t in range(2):
            q, dev = 4 + 2 * s + t, at(step[s], step[t])
            halo.append(remote(zsend.at[t], drecv.at[s, t], hs.at[q], hr.at[q], dev))
            halo_c.append(remote(dcs.at[s, t], dcr.at[s, t], cs.at[q], cr.at[q], dev))
        y, z, q = at(step[s], 0), at(0, step[s]), 2 + s
        halo.append(remote(zsend.at[s], zrecv.at[s], hs.at[q], hr.at[q], z))
        halo.append(remote(ysend.at[s], yrecv.at[s], hs.at[s], hr.at[s], y))
        halo_c.append(remote(zcs.at[s], zcr.at[s], cs.at[q], cr.at[q], z))
        halo_c.append(remote(ycs.at[s], ycr.at[s], cs.at[s], cr.at[s], y))
    for copy in halo + halo_c:
        copy.start()

    lane = iota((32, 768), 1)
    q, m = lane // 128, lane % 128
    k = 9 * ((m // 16) % 2 - q % 2 + 1) + 3 * (m // 32) + q // 2
    wanted = (m < 96, iota((32, 768), 0))
    straight = one_hot(wanted[0] & (wanted[1] == k))[:27]
    flipped = one_hot(wanted[0] & (wanted[1] == 26 - k))[:27]
    r, c = iota((256, 768), 0), iota((256, 768), 1)
    to_in, to_out = r % 16 == c % 16, r // 16 == c % 16
    r, c = iota((16, 256), 0), iota((16, 256), 1)
    by_out, by_in = one_hot(c // 16 == r), one_hot(c % 16 == r)
    loads[3].wait()
    loads[4].wait()
    for n, (w, pick, mask, rows) in enumerate(
        (
            (w1, straight, to_in, by_out),
            (w2, flipped, to_out, by_in),
            (w1, flipped, to_out, by_in),
        )
    ):
        wide = jnp.where(mask, mm(w[...], pick), 0.0).astype(BF)
        strips = mm(rows, wide)
        for cc in range(3):
            for xo in range(2):
                first = 128 * (2 * cc + xo)
                strip = strips[:, first : first + 128]
                strip = jnp.concatenate([strip, jnp.zeros_like(strip)], 1)
                for yo in range(4):
                    moved = strip if yo == 0 else pltpu.roll(strip, 32 * yo, 1)
                    first = 32 * yo + 16 * xo
                    bands[n, cc, first : first + 16, :] = moved.astype(BF)

    inp3[...] = jnp.zeros_like(inp3)
    loads[5].wait()
    for a in range(3):
        inp3[64 * (2 - a) : 64 * (2 - a) + 1024, 128 * a : 128 * a + 128] = cin[...]
    vmat[0] = jnp.zeros((64, 1152), BF)
    vmat[17] = jnp.zeros((64, 1152), BF)
    qf[...] = jnp.zeros_like(qf)

    def valid(cond, value):
        return jnp.where(cond, value, jnp.zeros_like(value))

    for copy in halo:
        copy.wait()

    def turned(after, before):
        return jnp.concatenate([after, before], 0).astype(F32).T.astype(BF)

    def fill(dst, get_y, get_d, get_z):
        r, c = iota((32, 256), 0), iota((32, 256), 1)

        def place(row, ok):
            after = (r == row) & (c == 127) & side[1] & ok
            return one_hot(after | ((r == 16 + row) & (c == 128) & side[0] & ok))

        for s in (1, 0):
            ok = up[0] if s == 1 else up[1]
            mid = valid(ok, get_y(s))
            corner = turned(get_d(s, 0), get_d(s, 1))
            corner = corner[96:128] if s == 1 else corner[0:32]
            out = mm(mid, shifts[...]) + mm(corner, place(15 if s == 1 else 0, ok))
            rows, lanes = (slice(0, 32), slice(0, 128)) if s == 1 else (slice(1056, 1088), slice(128, 256))
            dst[0, rows, lanes] = mid
            dst[2, rows, lanes] = out[:, :128].astype(BF)
            dst[1, rows, lanes] = out[:, 128:].astype(BF)
        edge = turned(get_z(0), get_z(1))
        for h in range(2):
            lanes = slice(128 * h, 128 * h + 128)
            for j in range(8):
                rows = slice(32 + 128 * j, 160 + 128 * j)
                out = mm(dst[0, rows, lanes], shifts[...]) + mm(edge, place(8 * h + j, True))
                dst[2, rows, lanes] = out[:, :128].astype(BF)
                dst[1, rows, lanes] = out[:, 128:].astype(BF)
        for v in range(3):
            dst[v, 0:32, 128:256] = dst[v, 1024:1056, 0:128]
            dst[v, 1056:1088, 0:128] = dst[v, 32:64, 128:256]

    for n, dst in enumerate((xin, xcot)):
        rows, tile = slice(32 * n, 32 * n + 32), slice(16 * n, 16 * n + 16)
        fill(
            dst,
            lambda s, rows=rows: yrecv[s, rows, :],
            lambda s, t, tile=tile: drecv[s, t, tile, :],
            lambda t, tile=tile: zrecv[t, tile, :],
        )

    for copy in halo_c:
        copy.wait()
    for x in range(16):
        rows = slice(8 * (x // 2 * 2), 16 + 8 * (x // 2 * 2))
        half = slice(8 * (x % 2), 8 * (x % 2) + 8)
        cflat[80 * x : 80 * x + 8, :] = valid(up[0], ycr[1, rows, :].astype(F32)[half])
        cflat[80 * x + 72 : 80 * x + 80, :] = valid(up[1], ycr[0, rows, :].astype(F32)[half])
    cplus[...] = pltpu.roll(cflat[...], 1279, 0)
    cminus[...] = pltpu.roll(cflat[...], 1, 0)
    for y in range(10):
        for ref, z, t, ok in ((cplus, 7, 0, side[1]), (cminus, 0, 1, side[0])):
            if y == 0:
                part, ok = dcr[1, t], ok & up[0]
            elif y == 9:
                part, ok = dcr[0, t], ok & up[1]
            else:
                part = zcr[t, 16 * (y - 1) : 16 * y, :]
            ref[pl.ds(8 * y + z, 16, stride=80), :] = valid(ok, part.astype(F32))

    def spread(x, carry):
        for b in range(3):
            for cc, ref in enumerate((cplus, cflat, cminus)):
                rows = ref[pl.ds(pl.multiple_of(x * 80 + 8 * (2 - b), 8), 64), :]
                q = 3 * b + cc
                vmat[x + 1, :, 128 * q : 128 * q + 128] = rows.astype(BF)
        return carry

    lax.fori_loop(0, 16, spread, 0)

    wide_o, nx = 128 // nty, nty // 2
    core, xme = lax.rem(ty, 2), lax.div(ty, 2)
    other = (dp, ty + 1 - 2 * core, tz)
    hop0 = []
    for b in range(3):
        left = vmat[:, :, 384 * b : 384 * b + 384].reshape(1152, 384)
        g = mm(left, inp3[...], TN)
        for a in range(3):
            for cc in range(3):
                part = g[128 * cc : 128 * cc + 128, 128 * a : 128 * a + 128]
                rsend[9 * b + 3 * a + cc] = part.astype(BF).reshape(nx, 2, wide_o, 128)
        src = rsend.at[pl.ds(9 * b, 9), :, 1 - core]
        hop0.append(remote(src, rpair.at[pl.ds(9 * b, 9)], ps.at[b], pr.at[b], other))
        hop0[b].start()

    hop1 = []
    for b in range(3):
        hop0[b].wait()
        for q in range(9 * b, 9 * b + 9):
            psum[q] = (rsend[q, :, core].astype(F32) + rpair[q].astype(F32)).astype(BF)
        for j in range(1, nx):
            x = lax.rem(xme + j, nx)
            src, dst = psum.at[pl.ds(9 * b, 9), x], rs1.at[xme, pl.ds(9 * b, 9)]
            dev = (dp, 2 * x + core, tz)
            hop1.append(remote(src, dst, r1s.at[b, j], r1r.at[b, nx - j], dev))
            hop1[-1].start()

    version = (1, 0, 2)

    def conv(n, src, g):
        rows = pl.ds(pl.multiple_of(g * 128, 128), 192)
        out = None
        for cc in range(3):
            term = mm(bands[n, cc, :, 0:192], src[version[cc], rows, :])
            out = term if out is None else out + term
        return out

    def forward(g, carry):
        pre = conv(0, xin, g)
        dact = conv(1, xcot, g)
        square = pre * pre
        t = jnp.tanh(C0 * pre * (1.0 + C1 * square))
        half = 0.5 + 0.5 * t
        slope = half + 0.5 * pre * (1.0 - t * t) * (C0 * (1.0 + (3.0 * C1) * square))
        act[pl.ds(pl.multiple_of(g * 128, 128), 128), :] = (pre * half).astype(BF)
        xdp[0, pl.ds(pl.multiple_of(g * 128 + 32, 32), 128), :] = (dact * slope).astype(BF)
        return carry

    lax.fori_loop(0, 8, forward, 0)

    acc1[...] = jnp.zeros_like(acc1)
    acc2[...] = jnp.zeros_like(acc2)

    def gram(g, carry):
        rows = pl.ds(pl.multiple_of(g * 128, 128), 192)
        own = xdp[0, pl.ds(pl.multiple_of(g * 128 + 32, 32), 128), :]
        a_own = act[pl.ds(pl.multiple_of(g * 128, 128), 128), :]
        for cc in range(3):
            acc1[cc, :, 0:192] += mm(own, xin[version[cc], rows, :], NT)
            acc2[cc] += mm(xcot[version[cc], rows, :], a_own, NT)
        return carry

    lax.fori_loop(0, 8, gram, 0)
    for cc in range(3):
        total = None
        for yo in range(4):
            part = acc1[cc, 32 * yo : 32 * yo + 32, :]
            part = part if yo == 0 else pltpu.roll(part, 256 - 32 * yo, 1)
            total = part if total is None else total + part
        fpart[32 * cc : 32 * cc + 32, :] = total[:, 0:128]
    total = jnp.zeros((96, 128), F32)
    lane = iota((96, 128), 1)
    for cc in range(3):
        band = None
        for yo in range(4):
            part = acc2[cc, 32 * yo : 32 * yo + 96, :]
            turn = (32 * cc - 32 * yo) % 128
            part = part if turn == 0 else pltpu.roll(part, turn, 1)
            band = part if band is None else band + part
        total = jnp.where(lane // 32 == cc, band, total)
    fpart[96:192, :] = total

    slab = 192 // nty
    hop_a = []
    for j in range(1, nty):
        t, dev = ty_peer(j)
        src = fpart.at[pl.ds(pl.multiple_of(t * slab, 8), slab), :]
        hop_a.append(remote(src, ar1.at[ty], a1s.at[j], a1r.at[nty - j], dev))
    for copy in hop_a:
        copy.start()
    ar1[ty] = fpart[pl.ds(pl.multiple_of(ty * slab, 8), slab), :]

    columns = extract(xdp)
    zsend2[0] = columns[0:16]
    zsend2[1] = columns[16:32]
    ysend2[0] = xdp[0, 32:64, 0:128]
    ysend2[1] = xdp[0, 1024:1056, 128:256]
    halo2 = []
    for s in range(2):
        halo2.append(remote(ysend2.at[s], yrecv2.at[s], gs.at[s], gr.at[s], at(step[s], 0)))
        halo2.append(remote(zsend2.at[s], zrecv2.at[s], gs.at[2 + s], gr.at[2 + s], at(0, step[s])))
        for t in range(2):
            q = 4 + 2 * s + t
            dev = at(step[s], step[t])
            halo2.append(remote(zsend2.at[t], drecv2.at[s, t], gs.at[q], gr.at[q], dev))
    for copy in halo2:
        copy.start()

    loads[6].wait()

    def coarse(q, carry):
        out = None
        for a in range(3):
            left = vmat[pl.ds(q * 4 + 2 - a, 4)].reshape(256, 1152)
            term = mm(left, wc[1152 * a : 1152 * a + 1152, :])
            out = term if out is None else out + term
        g_gci[pl.ds(pl.multiple_of(q * 256, 256), 256), :] = out.astype(BF)
        return carry

    lax.fori_loop(0, 4, coarse, 0)
    stores = [pltpu.make_async_copy(g_gci, o_gci, ws.at[0])]
    stores[0].start()

    for copy in hop_a:
        copy.wait()
    total = ar1[0]
    for t in range(1, nty):
        total = total + ar1[t]
    fsum1[...] = total
    hop_b = []
    for j in range(1, zgroup):
        g, z, dev = z_peer(j)
        hop_b.append(remote(fsum1, ar2.at[me], a2s.at[j], a2r.at[zgroup - j], dev))
    for copy in hop_b:
        copy.start()
    ar2[me] = fsum1[...]

    rs1[xme] = psum[:, xme]
    for copy in hop1:
        copy.wait()

    def sum1(q, carry):
        total = rs1[0, q].astype(F32)
        for t in range(1, nx):
            total = total + rs1[t, q].astype(F32)
        k = 9 * (lax.div(q, 3) % 3) + 3 * lax.div(q, 9) + q % 3
        qf[pl.ds(k, wide_o, stride=32), :] = total
        return carry

    lax.fori_loop(0, 27, sum1, 0)
    qb[...] = qf[...].astype(BF)
    deep = 32 * wide_o // ntz

    hop2 = []
    for j in range(1, zgroup):
        g, z, dev = z_peer(j)
        src = qb.at[pl.ds(pl.multiple_of(z * deep, 16), deep), :]
        hop2.append(remote(src, rs2.at[me], r2s.at[j], r2r.at[zgroup - j], dev))
    for copy in hop2:
        copy.start()
    rs2[me] = qb[pl.ds(pl.multiple_of(tz * deep, 16), deep), :]

    for copy in halo2:
        copy.wait()
    fill(
        xdp,
        lambda s: yrecv2[s],
        lambda s, t: drecv2[s, t],
        lambda t: zrecv2[t],
    )

    def last(j, carry):
        parts = [conv(2, xdp, 4 * j + q).astype(BF) for q in range(4)]
        out = mm(perm[...], jnp.concatenate(parts, 0)).astype(BF)
        first = pl.multiple_of(16 * j, 16)
        g_gfi[:, pl.ds(first, 16), :] = out[:, :128].reshape(32, 16, 128)
        g_gfi[:, pl.ds(first + 32, 16), :] = out[:, 128:].reshape(32, 16, 128)
        return carry

    lax.fori_loop(0, 2, last, 0)
    stores.append(pltpu.make_async_copy(g_gfi, o_gfi, ws.at[1]))
    stores[1].start()

    for copy in hop_b:
        copy.wait()
    total = ar2[0]
    for t in range(1, zgroup):
        total = total + ar2[t]
    fsum2[...] = total
    hop_c = []
    for j in range(1, nty):
        t, dev = ty_peer(j)
        hop_c.append(remote(fsum2, gath.at[ty], a3s.at[j], a3r.at[nty - j], dev))
    for copy in hop_c:
        copy.start()
    gath[ty] = fsum2[...]

    for copy in hop2:
        copy.wait()
    total = rs2[0].astype(F32)
    for t in range(1, zgroup):
        total = total + rs2[t].astype(F32)
    for o in range(wide_o // ntz):
        g_gc[:, o, :] = total[32 * o : 32 * o + 27, :]
    stores.append(pltpu.make_async_copy(g_gc, o_gc, ws.at[2]))
    stores[2].start()

    for copy in hop_c:
        copy.wait()
    fpart[...] = gath[...].reshape(192, 128)
    for a in range(3):
        planes = [(xo, xo + a - 1) for xo in range(2) if 0 <= xo + a - 1 < 2]
        for b in range(3):
            for cc in range(3):
                k = 9 * a + 3 * b + cc
                one, two = None, None
                for xo, xi in planes:
                    first = 32 * cc + 16 * xo
                    lanes = slice(32 * b + 16 * xi, 32 * b + 16 * xi + 16)
                    part = fpart[first : first + 16, lanes]
                    one = part if one is None else one + part
                    first = 96 + 32 * b + 16 * xi
                    lanes = slice(32 * cc + 16 * xo, 32 * cc + 16 * xo + 16)
                    part = fpart[first : first + 16, lanes]
                    two = part if two is None else two + part
                g_gf[k] = one
                g_gs[26 - k] = two
    for n, (src, mid, dst) in enumerate(((g_gf, t_gf, o_gf), (g_gs, t_gs, o_gs))):
        for o in range(16):
            mid[o] = src[:, o, :].T
        stores.append(pltpu.make_async_copy(mid, dst, ws.at[3 + n]))
        stores[3 + n].start()
    for copy in stores:
        copy.wait()


def finish(*refs):
    srcs, dsts, mids, sems = refs[:5], refs[5:10], refs[10:15], refs[15]
    into = [pltpu.make_async_copy(srcs[n], mids[n], sems.at[n]) for n in range(5)]
    out = [pltpu.make_async_copy(mids[n], dsts[n], sems.at[5 + n]) for n in range(5)]
    for copy in into:
        copy.start()
    for n in range(5):
        into[n].wait()
        out[n].start()
    for copy in out:
        copy.wait()


def solution(mesh):
    sizes = tuple(mesh.shape[a] for a in ("dp", "ty", "tz"))
    ndp, nty, ntz = sizes
    zgroup = ndp * ntz
    wide_o, nx = 128 // nty, nty // 2
    slab = 192 // nty

    def per_device(fine_input, fine_cotangent, first_weight, second_weight, coarse_input, coarse_cotangent, coarse_weight):
        def by_offset(w):
            return w.transpose(1, 2, 0).reshape(256, 27)

        dma = pltpu.SemaphoreType.DMA
        scratch = [
            pltpu.VMEM((32, 64, 128), BF),
            pltpu.VMEM((32, 64, 128), BF),
            pltpu.VMEM((256, 27), BF),
            pltpu.VMEM((256, 27), BF),
            pltpu.VMEM((1024, 128), BF),
            pltpu.VMEM((1024, 128), BF),
            pltpu.VMEM((3456, 128), BF),
            pltpu.VMEM((512, 512), BF),
            pltpu.VMEM((128, 256), BF),
            pltpu.VMEM((3, ROWS, 256), BF),
            pltpu.VMEM((3, ROWS, 256), BF),
            pltpu.VMEM((3, ROWS, 256), BF),
            pltpu.VMEM((1024, 256), BF),
            pltpu.VMEM((3, 3, 128, 256), BF),
            pltpu.VMEM((2, 64, 128), BF),
            pltpu.VMEM((2, 64, 128), BF),
            pltpu.VMEM((2, 32, 128), BF),
            pltpu.VMEM((2, 32, 128), BF),
            pltpu.VMEM((2, 2, 32, 128), BF),
            pltpu.VMEM((2, 128, 128), BF),
            pltpu.VMEM((2, 128, 128), BF),
            pltpu.VMEM((2, 128, 128), BF),
            pltpu.VMEM((2, 128, 128), BF),
            pltpu.VMEM((2, 2, 16, 128), BF),
            pltpu.VMEM((2, 2, 16, 128), BF),
            pltpu.VMEM((2, 32, 128), BF),
            pltpu.VMEM((2, 32, 128), BF),
            pltpu.VMEM((2, 16, 128), BF),
            pltpu.VMEM((2, 16, 128), BF),
            pltpu.VMEM((2, 2, 16, 128), BF),
            pltpu.VMEM((1280, 128), F32),
            pltpu.VMEM((1280, 128), F32),
            pltpu.VMEM((1280, 128), F32),
            pltpu.VMEM((18, 64, 1152), BF),
            pltpu.VMEM((1152, 384), BF),
            pltpu.VMEM((27, nx, 2, wide_o, 128), BF),
            pltpu.VMEM((27, nx, wide_o, 128), BF),
            pltpu.VMEM((27, nx, wide_o, 128), BF),
            pltpu.VMEM((nx, 27, wide_o, 128), BF),
            pltpu.VMEM((32 * wide_o, 128), F32),
            pltpu.VMEM((32 * wide_o, 128), BF),
            pltpu.VMEM((zgroup, 32 * wide_o // ntz, 128), BF),
            pltpu.VMEM((1024, 128), BF),
            pltpu.VMEM((32, 64, 128), BF),
            pltpu.VMEM((27, 16, 16), F32),
            pltpu.VMEM((27, 16, 16), F32),
            pltpu.VMEM((16, 16, 27), F32),
            pltpu.VMEM((16, 16, 27), F32),
            pltpu.VMEM((27, wide_o // ntz, 128), F32),
            pltpu.VMEM((3, 128, 256), F32),
            pltpu.VMEM((3, 192, 128), F32),
            pltpu.VMEM((192, 128), F32),
            pltpu.VMEM((nty, slab, 128), F32),
            pltpu.VMEM((slab, 128), F32),
            pltpu.VMEM((zgroup, slab, 128), F32),
            pltpu.VMEM((slab, 128), F32),
            pltpu.VMEM((nty, slab, 128), F32),
            dma((7,)),
            dma((8,)),
            dma((8,)),
            dma((8,)),
            dma((8,)),
            dma((3,)),
            dma((3,)),
            dma((8,)),
            dma((8,)),
            dma((3, nx)),
            dma((3, nx)),
            dma((zgroup,)),
            dma((zgroup,)),
            dma((nty,)),
            dma((nty,)),
            dma((zgroup,)),
            dma((zgroup,)),
            dma((nty,)),
            dma((nty,)),
            dma((5,)),
        ]
        outs = pl.pallas_call(
            functools.partial(kernel, sizes),
            out_shape=(
                jax.ShapeDtypeStruct((32, 64, 128), BF),
                jax.ShapeDtypeStruct((16, 16, 27), F32),
                jax.ShapeDtypeStruct((16, 16, 27), F32),
                jax.ShapeDtypeStruct((1024, 128), BF),
                jax.ShapeDtypeStruct((27, wide_o // ntz, 128), F32),
            ),
            in_specs=[pl.BlockSpec(memory_space=pl.ANY)] * 7,
            out_specs=(pl.BlockSpec(memory_space=pl.ANY),) * 5,
            scratch_shapes=scratch,
            compiler_params=pltpu.CompilerParams(
                collective_id=0, has_side_effects=True, vmem_limit_bytes=60 * 1024 * 1024
            ),
        )(
            fine_input.reshape(32, 64, 128),
            fine_cotangent.reshape(32, 64, 128),
            by_offset(first_weight),
            by_offset(second_weight),
            coarse_input.reshape(1024, 128),
            coarse_cotangent.reshape(1024, 128),
            coarse_weight.reshape(3456, 128),
        )
        far = pl.BlockSpec(memory_space=pl.ANY)
        outs = pl.pallas_call(
            finish,
            out_shape=(
                jax.ShapeDtypeStruct((32, 64, 128), BF),
                jax.ShapeDtypeStruct((16, 16, 27), F32),
                jax.ShapeDtypeStruct((16, 16, 27), F32),
                jax.ShapeDtypeStruct((1024, 128), BF),
                jax.ShapeDtypeStruct((27, wide_o // ntz, 128), F32),
            ),
            in_specs=[far] * 5,
            out_specs=(far,) * 5,
            scratch_shapes=[
                pltpu.VMEM((32, 64, 128), BF),
                pltpu.VMEM((16, 16, 27), F32),
                pltpu.VMEM((16, 16, 27), F32),
                pltpu.VMEM((1024, 128), BF),
                pltpu.VMEM((27, wide_o // ntz, 128), F32),
                dma((10,)),
            ],
            compiler_params=pltpu.CompilerParams(vmem_limit_bytes=60 * 1024 * 1024),
        )(*outs)
        return (
            outs[0].reshape(fine_input.shape),
            outs[1].transpose(2, 0, 1),
            outs[2].transpose(2, 0, 1),
            outs[3].reshape(coarse_input.shape),
            outs[4].transpose(1, 0, 2),
        )

    fine = P("dp", None, None, "ty", "tz")
    wide = P("dp", None, "ty", "tz", None)
    return jax.shard_map(
        per_device,
        mesh=mesh,
        in_specs=(fine, fine, P(), P(), wide, wide, P()),
        out_specs=(fine, P(), P(), wide, P(("ty", "tz"), None, None)),
        check_vma=False,
    )
```

```python
import functools

import jax
import jax.numpy as jnp
from jax import lax
from jax.experimental import pallas as pl
from jax.experimental.pallas import tpu as pltpu
from jax.sharding import PartitionSpec as P

MESH = pl.DeviceIdType.MESH
BF = jnp.bfloat16
F32 = jnp.float32
NN = (((1,), (0,)), ((), ()))
NT = (((1,), (1,)), ((), ()))
TN = (((0,), (0,)), ((), ()))
ROWS = 34 * 32
C0 = 0.7978845608028654
C1 = 0.044715


def mm(a, b, dims=NN):
    return lax.dot_general(a, b, dims, preferred_element_type=F32)


def iota(shape, dim):
    return lax.broadcasted_iota(jnp.int32, shape, dim)


def one_hot(cond):
    return jnp.where(cond, 1.0, 0.0).astype(BF)


def kernel(
    sizes,
    h_fin,
    h_fcot,
    h_w1,
    h_w2,
    h_cin,
    h_ccot,
    h_wc,
    o_gfi,
    o_gf,
    o_gs,
    o_gci,
    o_gc,
    fin,
    fcot,
    w1,
    w2,
    cin,
    ccot,
    wc,
    perm,
    shifts,
    xin,
    xcot,
    xdp,
    act,
    bands,
    ysend,
    yrecv,
    zsend,
    zrecv,
    drecv,
    ycs,
    ycr,
    zcs,
    zcr,
    dcs,
    dcr,
    ysend2,
    yrecv2,
    zsend2,
    zrecv2,
    drecv2,
    cflat,
    cplus,
    cminus,
    vmat,
    inp3,
    rsend,
    rpair,
    psum,
    rs1,
    qf,
    qb,
    rs2,
    g_gci,
    g_gfi,
    g_gf,
    g_gs,
    t_gf,
    t_gs,
    g_gc,
    acc1,
    acc2,
    fpart,
    ar1,
    fsum1,
    ar2,
    fsum2,
    gath,
    ls,
    hs,
    hr,
    cs,
    cr,
    ps,
    pr,
    gs,
    gr,
    r1s,
    r1r,
    r2s,
    r2r,
    a1s,
    a1r,
    a2s,
    a2r,
    a3s,
    a3r,
    ws,
):
    ndp, nty, ntz = sizes
    dp, ty, tz = lax.axis_index("dp"), lax.axis_index("ty"), lax.axis_index("tz")
    zgroup = ndp * ntz
    me = dp * ntz + tz

    def at(dy, dz):
        return (dp, lax.rem(ty + dy + nty, nty), lax.rem(tz + dz + ntz, ntz))

    def ty_peer(j):
        t = lax.rem(ty + j, nty)
        return t, (dp, t, tz)

    def z_peer(j):
        g = lax.rem(me + j, zgroup)
        z = lax.rem(g, ntz)
        return g, z, (lax.div(g, ntz), ty, z)

    def remote(src, dst, ssem, rsem, dev):
        return pltpu.make_async_remote_copy(
            src_ref=src,
            dst_ref=dst,
            send_sem=ssem,
            recv_sem=rsem,
            device_id=dev,
            device_id_type=MESH,
        )

    loads = []
    pairs = ((h_ccot, ccot), (h_fin, fin), (h_fcot, fcot), (h_w1, w1), (h_w2, w2), (h_cin, cin), (h_wc, wc))
    for n, (src, dst) in enumerate(pairs):
        loads.append(pltpu.make_async_copy(src, dst, ls.at[n]))
        loads[n].start()

    def arrived(buf, count, ssem, rsem):
        part = buf.at[pl.ds(0, count)]
        for sem in (ssem, rsem):
            pltpu.make_async_copy(part, part, sem).wait()

    up = (ty > 0, ty < nty - 1)
    side = (tz > 0, tz < ntz - 1)

    barrier = pltpu.get_barrier_semaphore()
    partners = [at(dy, dz) for dy in (-1, 1) for dz in (-1, 1)]
    partners += [ty_peer(j)[1] for j in range(1, nty)]
    partners += [z_peer(j)[2] for j in range(1, zgroup)]
    for dev in partners:
        pl.semaphore_signal(barrier, inc=1, device_id=dev, device_id_type=MESH)

    r, c = iota((512, 512), 0), iota((512, 512), 1)
    perm[...] = one_hot(c == (r % 16) * 32 + ((r // 16) % 2) * 16 + r // 32)
    r, c = iota((128, 256), 0), iota((128, 256), 1)
    shifts[...] = one_hot(((r == c + 1) & (c < 127)) | ((r + 1 == c - 128) & (c > 128)))

    def relayout(src, dst):
        for j in range(2):
            left = src[:, 16 * j : 16 * j + 16, :].reshape(512, 128)
            right = src[:, 32 + 16 * j : 48 + 16 * j, :].reshape(512, 128)
            both = jnp.concatenate([left, right], 1)
            dst[0, 32 + 512 * j : 544 + 512 * j, :] = mm(perm[...], both).astype(BF)

    def extract(src):
        r, c = iota((32, 256), 0), iota((32, 256), 1)
        total = None
        for j in range(8):
            sel = one_hot((r % 16 == 8 * (c // 128) + j) & (c % 128 == 127 * (r // 16)))
            part = mm(sel, src[0, 32 + 128 * j : 160 + 128 * j, :], NT)
            total = part if total is None else total + part
        return total.astype(BF)

    loads[1].wait()
    relayout(fin, xin)
    loads[2].wait()
    relayout(fcot, xcot)
    for n, src in enumerate((xin, xcot)):
        columns = extract(src)
        for t in range(2):
            tile = columns[16 * t : 16 * t + 16, :]
            zsend[t, 16 * n : 16 * n + 16, :] = tile

    loads[0].wait()
    for x in range(16):
        cflat[80 * x + 8 : 80 * x + 72, :] = ccot[64 * x : 64 * x + 64, :].astype(F32)

    def column(y, z):
        return cflat[pl.ds(8 * y + z, 16, stride=80), :]

    for y in range(8):
        zcs[0, 16 * y : 16 * y + 16, :] = column(y + 1, 0).astype(BF)
        zcs[1, 16 * y : 16 * y + 16, :] = column(y + 1, 7).astype(BF)
    for s in range(2):
        own = (slice(32, 64), slice(0, 128)) if s == 0 else (slice(1024, 1056), slice(128, 256))
        ysend[s, 0:32, :] = xin[(0, *own)]
        ysend[s, 32:64, :] = xcot[(0, *own)]
        first = 8 if s == 0 else 64
        for x in range(0, 16, 2):
            pair = [cflat[80 * (x + q) + first : 80 * (x + q) + first + 8, :] for q in range(2)]
            ycs[s, 8 * x : 8 * x + 16, :] = jnp.concatenate(pair, 0).astype(BF)
        for t in range(2):
            dcs[s, t] = column(1 if s == 0 else 8, 0 if t == 0 else 7).astype(BF)

    pl.semaphore_wait(barrier, len(partners))

    step = (-1, 1)
    halo, halo_c = [], []
    for s in range(2):
        for t in range(2):
            q, dev = 4 + 2 * s + t, at(step[s], step[t])
            halo.append(remote(zsend.at[t], drecv.at[s, t], hs.at[q], hr.at[q], dev))
            halo_c.append(remote(dcs.at[s, t], dcr.at[s, t], cs.at[q], cr.at[q], dev))
        y, z, q = at(step[s], 0), at(0, step[s]), 2 + s
        halo.append(remote(zsend.at[s], zrecv.at[s], hs.at[q], hr.at[q], z))
        halo.append(remote(ysend.at[s], yrecv.at[s], hs.at[s], hr.at[s], y))
        halo_c.append(remote(zcs.at[s], zcr.at[s], cs.at[q], cr.at[q], z))
        halo_c.append(remote(ycs.at[s], ycr.at[s], cs.at[s], cr.at[s], y))
    for copy in halo + halo_c:
        copy.start()

    lane = iota((32, 768), 1)
    q, m = lane // 128, lane % 128
    k = 9 * ((m // 16) % 2 - q % 2 + 1) + 3 * (m // 32) + q // 2
    wanted = (m < 96, iota((32, 768), 0))
    straight = one_hot(wanted[0] & (wanted[1] == k))[:27]
    flipped = one_hot(wanted[0] & (wanted[1] == 26 - k))[:27]
    r, c = iota((256, 768), 0), iota((256, 768), 1)
    to_in, to_out = r % 16 == c % 16, r // 16 == c % 16
    r, c = iota((16, 256), 0), iota((16, 256), 1)
    by_out, by_in = one_hot(c // 16 == r), one_hot(c % 16 == r)
    loads[3].wait()
    loads[4].wait()
    for n, (w, pick, mask, rows) in enumerate(
        (
            (w1, straight, to_in, by_out),
            (w2, flipped, to_out, by_in),
            (w1, flipped, to_out, by_in),
        )
    ):
        wide = jnp.where(mask, mm(w[...], pick), 0.0).astype(BF)
        strips = mm(rows, wide)
        for cc in range(3):
            for xo in range(2):
                first = 128 * (2 * cc + xo)
                strip = strips[:, first : first + 128]
                strip = jnp.concatenate([strip, jnp.zeros_like(strip)], 1)
                for yo in range(4):
                    moved = strip if yo == 0 else pltpu.roll(strip, 32 * yo, 1)
                    first = 32 * yo + 16 * xo
                    bands[n, cc, first : first + 16, :] = moved.astype(BF)

    inp3[...] = jnp.zeros_like(inp3)
    loads[5].wait()
    for a in range(3):
        inp3[64 * (2 - a) : 64 * (2 - a) + 1024, 128 * a : 128 * a + 128] = cin[...]
    vmat[0] = jnp.zeros((64, 1152), BF)
    vmat[17] = jnp.zeros((64, 1152), BF)
    qf[...] = jnp.zeros_like(qf)

    def valid(cond, value):
        return jnp.where(cond, value, jnp.zeros_like(value))

    for copy in halo:
        copy.wait()

    def turned(after, before):
        return jnp.concatenate([after, before], 0).astype(F32).T.astype(BF)

    def fill(dst, get_y, get_d, get_z):
        r, c = iota((32, 256), 0), iota((32, 256), 1)

        def place(row, ok):
            after = (r == row) & (c == 127) & side[1] & ok
            return one_hot(after | ((r == 16 + row) & (c == 128) & side[0] & ok))

        for s in (1, 0):
            ok = up[0] if s == 1 else up[1]
            mid = valid(ok, get_y(s))
            corner = turned(get_d(s, 0), get_d(s, 1))
            corner = corner[96:128] if s == 1 else corner[0:32]
            out = mm(mid, shifts[...]) + mm(corner, place(15 if s == 1 else 0, ok))
            rows, lanes = (slice(0, 32), slice(0, 128)) if s == 1 else (slice(1056, 1088), slice(128, 256))
            dst[0, rows, lanes] = mid
            dst[2, rows, lanes] = out[:, :128].astype(BF)
            dst[1, rows, lanes] = out[:, 128:].astype(BF)
        edge = turned(get_z(0), get_z(1))
        for h in range(2):
            lanes = slice(128 * h, 128 * h + 128)
            for j in range(8):
                rows = slice(32 + 128 * j, 160 + 128 * j)
                out = mm(dst[0, rows, lanes], shifts[...]) + mm(edge, place(8 * h + j, True))
                dst[2, rows, lanes] = out[:, :128].astype(BF)
                dst[1, rows, lanes] = out[:, 128:].astype(BF)
        for v in range(3):
            dst[v, 0:32, 128:256] = dst[v, 1024:1056, 0:128]
            dst[v, 1056:1088, 0:128] = dst[v, 32:64, 128:256]

    for n, dst in enumerate((xin, xcot)):
        rows, tile = slice(32 * n, 32 * n + 32), slice(16 * n, 16 * n + 16)
        fill(
            dst,
            lambda s, rows=rows: yrecv[s, rows, :],
            lambda s, t, tile=tile: drecv[s, t, tile, :],
            lambda t, tile=tile: zrecv[t, tile, :],
        )

    for copy in halo_c:
        copy.wait()
    for x in range(16):
        rows = slice(8 * (x // 2 * 2), 16 + 8 * (x // 2 * 2))
        half = slice(8 * (x % 2), 8 * (x % 2) + 8)
        cflat[80 * x : 80 * x + 8, :] = valid(up[0], ycr[1, rows, :].astype(F32)[half])
        cflat[80 * x + 72 : 80 * x + 80, :] = valid(up[1], ycr[0, rows, :].astype(F32)[half])
    cplus[...] = pltpu.roll(cflat[...], 1279, 0)
    cminus[...] = pltpu.roll(cflat[...], 1, 0)
    for y in range(10):
        for ref, z, t, ok in ((cplus, 7, 0, side[1]), (cminus, 0, 1, side[0])):
            if y == 0:
                part, ok = dcr[1, t], ok & up[0]
            elif y == 9:
                part, ok = dcr[0, t], ok & up[1]
            else:
                part = zcr[t, 16 * (y - 1) : 16 * y, :]
            ref[pl.ds(8 * y + z, 16, stride=80), :] = valid(ok, part.astype(F32))

    def spread(x, carry):
        for b in range(3):
            for cc, ref in enumerate((cplus, cflat, cminus)):
                rows = ref[pl.ds(pl.multiple_of(x * 80 + 8 * (2 - b), 8), 64), :]
                q = 3 * b + cc
                vmat[x + 1, :, 128 * q : 128 * q + 128] = rows.astype(BF)
        return carry

    lax.fori_loop(0, 16, spread, 0)

    wide_o, nx = 128 // nty, nty // 2
    core, xme = lax.rem(ty, 2), lax.div(ty, 2)
    other = (dp, ty + 1 - 2 * core, tz)
    hop0 = []
    for b in range(3):
        left = vmat[:, :, 384 * b : 384 * b + 384].reshape(1152, 384)
        g = mm(left, inp3[...], TN)
        for a in range(3):
            for cc in range(3):
                part = g[128 * cc : 128 * cc + 128, 128 * a : 128 * a + 128]
                rsend[9 * b + 3 * a + cc] = part.astype(BF).reshape(nx, 2, wide_o, 128)
        src = rsend.at[pl.ds(9 * b, 9), :, 1 - core]
        hop0.append(remote(src, rpair.at[pl.ds(9 * b, 9)], ps.at[b], pr.at[b], other))
        hop0[b].start()

    hop1 = []
    for b in range(3):
        hop0[b].wait()
        for q in range(9 * b, 9 * b + 9):
            psum[q] = (rsend[q, :, core].astype(F32) + rpair[q].astype(F32)).astype(BF)
        for j in range(1, nx):
            x = lax.rem(xme + j, nx)
            src, dst = psum.at[pl.ds(9 * b, 9), x], rs1.at[xme, pl.ds(9 * b, 9)]
            dev = (dp, 2 * x + core, tz)
            hop1.append(remote(src, dst, r1s.at[0], r1r.at[0], dev))
            hop1[-1].start()

    version = (1, 0, 2)

    def conv(n, src, g):
        rows = pl.ds(pl.multiple_of(g * 128, 128), 192)
        out = None
        for cc in range(3):
            term = mm(bands[n, cc, :, 0:192], src[version[cc], rows, :])
            out = term if out is None else out + term
        return out

    def forward(g):
        pre = conv(0, xin, g)
        dact = conv(1, xcot, g)
        square = pre * pre
        t = jnp.tanh(C0 * pre * (1.0 + C1 * square))
        half = 0.5 + 0.5 * t
        slope = half + 0.5 * pre * (1.0 - t * t) * (C0 * (1.0 + (3.0 * C1) * square))
        act[pl.ds(pl.multiple_of(g * 128, 128), 128), :] = (pre * half).astype(BF)
        xdp[0, pl.ds(pl.multiple_of(g * 128 + 32, 32), 128), :] = (dact * slope).astype(BF)

    def four(i, carry):
        for q in range(4):
            forward(4 * i + q)
        return carry

    lax.fori_loop(0, 2, four, 0)

    def groups(ref, lead, first, count):
        return jnp.concatenate(
            [ref[(*lead, slice(128 * g + first, 128 * g + first + count))] for g in range(8)], 1
        )

    own, a_own = groups(xdp, (0,), 32, 128), groups(act, (), 0, 128)
    for cc in range(3):
        acc1[cc, :, 0:192] = mm(own, groups(xin, (version[cc],), 0, 192), NT)
        acc1[cc, :, 192:256] = jnp.zeros((128, 64), F32)
        acc2[cc] = mm(groups(xcot, (version[cc],), 0, 192), a_own, NT)
    for cc in range(3):
        total = None
        for yo in range(4):
            part = acc1[cc, 32 * yo : 32 * yo + 32, :]
            part = part if yo == 0 else pltpu.roll(part, 256 - 32 * yo, 1)
            total = part if total is None else total + part
        fpart[32 * cc : 32 * cc + 32, :] = total[:, 0:128]
    total = jnp.zeros((96, 128), F32)
    lane = iota((96, 128), 1)
    for cc in range(3):
        band = None
        for yo in range(4):
            part = acc2[cc, 32 * yo : 32 * yo + 96, :]
            turn = (32 * cc - 32 * yo) % 128
            part = part if turn == 0 else pltpu.roll(part, turn, 1)
            band = part if band is None else band + part
        total = jnp.where(lane // 32 == cc, band, total)
    fpart[96:192, :] = total

    slab = 192 // nty
    hop_a = []
    for j in range(1, nty):
        t, dev = ty_peer(j)
        src = fpart.at[pl.ds(pl.multiple_of(t * slab, 8), slab), :]
        hop_a.append(remote(src, ar1.at[ty], a1s.at[0], a1r.at[0], dev))
    for copy in hop_a:
        copy.start()
    ar1[ty] = fpart[pl.ds(pl.multiple_of(ty * slab, 8), slab), :]

    columns = extract(xdp)
    zsend2[0] = columns[0:16]
    zsend2[1] = columns[16:32]
    ysend2[0] = xdp[0, 32:64, 0:128]
    ysend2[1] = xdp[0, 1024:1056, 128:256]
    halo2 = []
    for s in range(2):
        halo2.append(remote(ysend2.at[s], yrecv2.at[s], gs.at[s], gr.at[s], at(step[s], 0)))
        halo2.append(remote(zsend2.at[s], zrecv2.at[s], gs.at[2 + s], gr.at[2 + s], at(0, step[s])))
        for t in range(2):
            q = 4 + 2 * s + t
            dev = at(step[s], step[t])
            halo2.append(remote(zsend2.at[t], drecv2.at[s, t], gs.at[q], gr.at[q], dev))
    for copy in halo2:
        copy.start()

    loads[6].wait()

    out = None
    for a in range(3):
        left = vmat[2 - a : 18 - a].reshape(1024, 1152)
        term = mm(left, wc[1152 * a : 1152 * a + 1152, :])
        out = term if out is None else out + term
    g_gci[...] = out.astype(BF)
    stores = [pltpu.make_async_copy(g_gci, o_gci, ws.at[0])]
    stores[0].start()

    arrived(ar1, nty - 1, a1s.at[0], a1r.at[0])
    total = ar1[0]
    for t in range(1, nty):
        total = total + ar1[t]
    fsum1[...] = total
    hop_b = []
    for j in range(1, zgroup):
        g, z, dev = z_peer(j)
        hop_b.append(remote(fsum1, ar2.at[me], a2s.at[0], a2r.at[0], dev))
    for copy in hop_b:
        copy.start()
    ar2[me] = fsum1[...]

    rs1[xme] = psum[:, xme]
    arrived(rs1, nx - 1, r1s.at[0], r1r.at[0])

    def sum1(q, carry):
        total = rs1[0, q].astype(F32)
        for t in range(1, nx):
            total = total + rs1[t, q].astype(F32)
        k = 9 * (lax.div(q, 3) % 3) + 3 * lax.div(q, 9) + q % 3
        qf[pl.ds(k, wide_o, stride=32), :] = total
        return carry

    lax.fori_loop(0, 27, sum1, 0)
    qb[...] = qf[...].astype(BF)
    deep = 32 * wide_o // ntz

    hop2 = []
    for j in range(1, zgroup):
        g, z, dev = z_peer(j)
        src = qb.at[pl.ds(pl.multiple_of(z * deep, 16), deep), :]
        hop2.append(remote(src, rs2.at[me], r2s.at[0], r2r.at[0], dev))
    for copy in hop2:
        copy.start()
    rs2[me] = qb[pl.ds(pl.multiple_of(tz * deep, 16), deep), :]

    for copy in halo2:
        copy.wait()
    fill(
        xdp,
        lambda s: yrecv2[s],
        lambda s, t: drecv2[s, t],
        lambda t: zrecv2[t],
    )

    def last(j, carry):
        parts = [conv(2, xdp, 4 * j + q).astype(BF) for q in range(4)]
        out = mm(perm[...], jnp.concatenate(parts, 0)).astype(BF)
        first = pl.multiple_of(16 * j, 16)
        g_gfi[:, pl.ds(first, 16), :] = out[:, :128].reshape(32, 16, 128)
        g_gfi[:, pl.ds(first + 32, 16), :] = out[:, 128:].reshape(32, 16, 128)
        return carry

    lax.fori_loop(0, 2, last, 0)
    stores.append(pltpu.make_async_copy(g_gfi, o_gfi, ws.at[1]))
    stores[1].start()

    arrived(ar2, zgroup - 1, a2s.at[0], a2r.at[0])
    total = ar2[0]
    for t in range(1, zgroup):
        total = total + ar2[t]
    fsum2[...] = total
    hop_c = []
    for j in range(1, nty):
        t, dev = ty_peer(j)
        hop_c.append(remote(fsum2, gath.at[ty], a3s.at[0], a3r.at[0], dev))
    for copy in hop_c:
        copy.start()
    gath[ty] = fsum2[...]

    arrived(rs2, zgroup - 1, r2s.at[0], r2r.at[0])
    total = rs2[0].astype(F32)
    for t in range(1, zgroup):
        total = total + rs2[t].astype(F32)
    for o in range(wide_o // ntz):
        g_gc[:, o, :] = total[32 * o : 32 * o + 27, :]
    stores.append(pltpu.make_async_copy(g_gc, o_gc, ws.at[2]))
    stores[2].start()

    arrived(gath, nty - 1, a3s.at[0], a3r.at[0])
    fpart[...] = gath[...].reshape(192, 128)
    for a in range(3):
        planes = [(xo, xo + a - 1) for xo in range(2) if 0 <= xo + a - 1 < 2]
        for b in range(3):
            for cc in range(3):
                k = 9 * a + 3 * b + cc
                one, two = None, None
                for xo, xi in planes:
                    first = 32 * cc + 16 * xo
                    lanes = slice(32 * b + 16 * xi, 32 * b + 16 * xi + 16)
                    part = fpart[first : first + 16, lanes]
                    one = part if one is None else one + part
                    first = 96 + 32 * b + 16 * xi
                    lanes = slice(32 * cc + 16 * xo, 32 * cc + 16 * xo + 16)
                    part = fpart[first : first + 16, lanes]
                    two = part if two is None else two + part
                g_gf[k] = one
                g_gs[26 - k] = two
    for n, (src, mid, dst) in enumerate(((g_gf, t_gf, o_gf), (g_gs, t_gs, o_gs))):
        for o in range(16):
            mid[o] = src[:, o, :].T
        stores.append(pltpu.make_async_copy(mid, dst, ws.at[3 + n]))
        stores[3 + n].start()
    for copy in stores:
        copy.wait()


def finish(*refs):
    srcs, dsts, mids, sems = refs[:5], refs[5:10], refs[10:15], refs[15]
    into = [pltpu.make_async_copy(srcs[n], mids[n], sems.at[n]) for n in range(5)]
    out = [pltpu.make_async_copy(mids[n], dsts[n], sems.at[5 + n]) for n in range(5)]
    for copy in into:
        copy.start()
    for n in range(5):
        into[n].wait()
        out[n].start()
    for copy in out:
        copy.wait()


def solution(mesh):
    sizes = tuple(mesh.shape[a] for a in ("dp", "ty", "tz"))
    ndp, nty, ntz = sizes
    zgroup = ndp * ntz
    wide_o, nx = 128 // nty, nty // 2
    slab = 192 // nty

    def per_device(fine_input, fine_cotangent, first_weight, second_weight, coarse_input, coarse_cotangent, coarse_weight):
        def by_offset(w):
            return w.transpose(1, 2, 0).reshape(256, 27)

        dma = pltpu.SemaphoreType.DMA
        scratch = [
            pltpu.VMEM((32, 64, 128), BF),
            pltpu.VMEM((32, 64, 128), BF),
            pltpu.VMEM((256, 27), BF),
            pltpu.VMEM((256, 27), BF),
            pltpu.VMEM((1024, 128), BF),
            pltpu.VMEM((1024, 128), BF),
            pltpu.VMEM((3456, 128), BF),
            pltpu.VMEM((512, 512), BF),
            pltpu.VMEM((128, 256), BF),
            pltpu.VMEM((3, ROWS, 256), BF),
            pltpu.VMEM((3, ROWS, 256), BF),
            pltpu.VMEM((3, ROWS, 256), BF),
            pltpu.VMEM((1024, 256), BF),
            pltpu.VMEM((3, 3, 128, 256), BF),
            pltpu.VMEM((2, 64, 128), BF),
            pltpu.VMEM((2, 64, 128), BF),
            pltpu.VMEM((2, 32, 128), BF),
            pltpu.VMEM((2, 32, 128), BF),
            pltpu.VMEM((2, 2, 32, 128), BF),
            pltpu.VMEM((2, 128, 128), BF),
            pltpu.VMEM((2, 128, 128), BF),
            pltpu.VMEM((2, 128, 128), BF),
            pltpu.VMEM((2, 128, 128), BF),
            pltpu.VMEM((2, 2, 16, 128), BF),
            pltpu.VMEM((2, 2, 16, 128), BF),
            pltpu.VMEM((2, 32, 128), BF),
            pltpu.VMEM((2, 32, 128), BF),
            pltpu.VMEM((2, 16, 128), BF),
            pltpu.VMEM((2, 16, 128), BF),
            pltpu.VMEM((2, 2, 16, 128), BF),
            pltpu.VMEM((1280, 128), F32),
            pltpu.VMEM((1280, 128), F32),
            pltpu.VMEM((1280, 128), F32),
            pltpu.VMEM((18, 64, 1152), BF),
            pltpu.VMEM((1152, 384), BF),
            pltpu.VMEM((27, nx, 2, wide_o, 128), BF),
            pltpu.VMEM((27, nx, wide_o, 128), BF),
            pltpu.VMEM((27, nx, wide_o, 128), BF),
            pltpu.VMEM((nx, 27, wide_o, 128), BF),
            pltpu.VMEM((32 * wide_o, 128), F32),
            pltpu.VMEM((32 * wide_o, 128), BF),
            pltpu.VMEM((zgroup, 32 * wide_o // ntz, 128), BF),
            pltpu.VMEM((1024, 128), BF),
            pltpu.VMEM((32, 64, 128), BF),
            pltpu.VMEM((27, 16, 16), F32),
            pltpu.VMEM((27, 16, 16), F32),
            pltpu.VMEM((16, 16, 27), F32),
            pltpu.VMEM((16, 16, 27), F32),
            pltpu.VMEM((27, wide_o // ntz, 128), F32),
            pltpu.VMEM((3, 128, 256), F32),
            pltpu.VMEM((3, 192, 128), F32),
            pltpu.VMEM((192, 128), F32),
            pltpu.VMEM((nty, slab, 128), F32),
            pltpu.VMEM((slab, 128), F32),
            pltpu.VMEM((zgroup, slab, 128), F32),
            pltpu.VMEM((slab, 128), F32),
            pltpu.VMEM((nty, slab, 128), F32),
            dma((7,)),
            dma((8,)),
            dma((8,)),
            dma((8,)),
            dma((8,)),
            dma((3,)),
            dma((3,)),
            dma((8,)),
            dma((8,)),
            dma((1,)),
            dma((1,)),
            dma((1,)),
            dma((1,)),
            dma((1,)),
            dma((1,)),
            dma((1,)),
            dma((1,)),
            dma((1,)),
            dma((1,)),
            dma((5,)),
        ]
        outs = pl.pallas_call(
            functools.partial(kernel, sizes),
            out_shape=(
                jax.ShapeDtypeStruct((32, 64, 128), BF),
                jax.ShapeDtypeStruct((16, 16, 27), F32),
                jax.ShapeDtypeStruct((16, 16, 27), F32),
                jax.ShapeDtypeStruct((1024, 128), BF),
                jax.ShapeDtypeStruct((27, wide_o // ntz, 128), F32),
            ),
            in_specs=[pl.BlockSpec(memory_space=pl.ANY)] * 7,
            out_specs=(pl.BlockSpec(memory_space=pl.ANY),) * 5,
            scratch_shapes=scratch,
            compiler_params=pltpu.CompilerParams(
                collective_id=0, has_side_effects=True, vmem_limit_bytes=60 * 1024 * 1024
            ),
        )(
            fine_input.reshape(32, 64, 128),
            fine_cotangent.reshape(32, 64, 128),
            by_offset(first_weight),
            by_offset(second_weight),
            coarse_input.reshape(1024, 128),
            coarse_cotangent.reshape(1024, 128),
            coarse_weight.reshape(3456, 128),
        )
        far = pl.BlockSpec(memory_space=pl.ANY)
        outs = pl.pallas_call(
            finish,
            out_shape=(
                jax.ShapeDtypeStruct((32, 64, 128), BF),
                jax.ShapeDtypeStruct((16, 16, 27), F32),
                jax.ShapeDtypeStruct((16, 16, 27), F32),
                jax.ShapeDtypeStruct((1024, 128), BF),
                jax.ShapeDtypeStruct((27, wide_o // ntz, 128), F32),
            ),
            in_specs=[far] * 5,
            out_specs=(far,) * 5,
            scratch_shapes=[
                pltpu.VMEM((32, 64, 128), BF),
                pltpu.VMEM((16, 16, 27), F32),
                pltpu.VMEM((16, 16, 27), F32),
                pltpu.VMEM((1024, 128), BF),
                pltpu.VMEM((27, wide_o // ntz, 128), F32),
                dma((10,)),
            ],
            compiler_params=pltpu.CompilerParams(vmem_limit_bytes=60 * 1024 * 1024),
        )(*outs)
        return (
            outs[0].reshape(fine_input.shape),
            outs[1].transpose(2, 0, 1),
            outs[2].transpose(2, 0, 1),
            outs[3].reshape(coarse_input.shape),
            outs[4].transpose(1, 0, 2),
        )

    fine = P("dp", None, None, "ty", "tz")
    wide = P("dp", None, "ty", "tz", None)
    return jax.shard_map(
        per_device,
        mesh=mesh,
        in_specs=(fine, fine, P(), P(), wide, wide, P()),
        out_specs=(fine, P(), P(), wide, P(("ty", "tz"), None, None)),
        check_vma=False,
    )
```

```python
import functools

import jax
import jax.numpy as jnp
from jax import lax
from jax.experimental import pallas as pl
from jax.experimental.pallas import tpu as pltpu
from jax.sharding import PartitionSpec as P

MESH = pl.DeviceIdType.MESH
BF = jnp.bfloat16
F32 = jnp.float32
NN = (((1,), (0,)), ((), ()))
NT = (((1,), (1,)), ((), ()))
TN = (((0,), (0,)), ((), ()))
ROWS = 34 * 32
C0 = 0.7978845608028654
C1 = 0.044715


def mm(a, b, dims=NN):
    return lax.dot_general(a, b, dims, preferred_element_type=F32)


def iota(shape, dim):
    return lax.broadcasted_iota(jnp.int32, shape, dim)


def one_hot(cond):
    return jnp.where(cond, 1.0, 0.0).astype(BF)


def kernel(
    sizes,
    h_fin,
    h_fcot,
    h_w1,
    h_w2,
    h_cin,
    h_ccot,
    h_wc,
    o_gfi,
    o_gf,
    o_gs,
    o_gci,
    o_gc,
    fin,
    fcot,
    w1,
    w2,
    cin,
    ccot,
    wc,
    perm,
    shifts,
    xin,
    xcot,
    xdp,
    act,
    bands,
    ysend,
    yrecv,
    zsend,
    zrecv,
    drecv,
    ycs,
    ycr,
    zcs,
    zcr,
    dcs,
    dcr,
    ysend2,
    yrecv2,
    zsend2,
    zrecv2,
    drecv2,
    cflat,
    cplus,
    cminus,
    vmat,
    inp3,
    rsend,
    rpair,
    psum,
    rs1,
    qf,
    qb,
    rs2,
    g_gci,
    g_gfi,
    g_gf,
    g_gs,
    t_gf,
    t_gs,
    g_gc,
    acc1,
    acc2,
    fpart,
    ar1,
    fsum1,
    ar2,
    fsum2,
    gath,
    ls,
    hs,
    hr,
    cs,
    cr,
    ps,
    pr,
    gs,
    gr,
    r1s,
    r1r,
    r2s,
    r2r,
    a1s,
    a1r,
    a2s,
    a2r,
    a3s,
    a3r,
    ws,
):
    ndp, nty, ntz = sizes
    dp, ty, tz = lax.axis_index("dp"), lax.axis_index("ty"), lax.axis_index("tz")
    zgroup = ndp * ntz
    me = dp * ntz + tz

    def at(dy, dz):
        return (dp, lax.rem(ty + dy + nty, nty), lax.rem(tz + dz + ntz, ntz))

    def ty_peer(j):
        t = lax.rem(ty + j, nty)
        return t, (dp, t, tz)

    def z_peer(j):
        g = lax.rem(me + j, zgroup)
        z = lax.rem(g, ntz)
        return g, z, (lax.div(g, ntz), ty, z)

    def remote(src, dst, ssem, rsem, dev):
        return pltpu.make_async_remote_copy(
            src_ref=src,
            dst_ref=dst,
            send_sem=ssem,
            recv_sem=rsem,
            device_id=dev,
            device_id_type=MESH,
        )

    def arrived(buf, count, ssem, rsem):
        part = buf.at[pl.ds(0, count)]
        for sem in (ssem, rsem):
            pltpu.make_async_copy(part, part, sem).wait()

    up = (ty > 0, ty < nty - 1)
    side = (tz > 0, tz < ntz - 1)

    barrier = pltpu.get_barrier_semaphore()
    partners = [at(dy, dz) for dy in (-1, 1) for dz in (-1, 1)]
    partners += [ty_peer(j)[1] for j in range(1, nty)]
    partners += [z_peer(j)[2] for j in range(1, zgroup)]
    for dev in partners:
        pl.semaphore_signal(barrier, inc=1, device_id=dev, device_id_type=MESH)

    loads = []
    pairs = ((h_ccot, ccot), (h_fin, fin), (h_fcot, fcot), (h_w1, w1), (h_w2, w2), (h_cin, cin), (h_wc, wc))
    for n, (src, dst) in enumerate(pairs):
        loads.append(pltpu.make_async_copy(src, dst, ls.at[n]))
        loads[n].start()

    r, c = iota((512, 512), 0), iota((512, 512), 1)
    perm[...] = one_hot(c == (r % 16) * 32 + ((r // 16) % 2) * 16 + r // 32)
    r, c = iota((128, 256), 0), iota((128, 256), 1)
    shifts[...] = one_hot(((r == c + 1) & (c < 127)) | ((r + 1 == c - 128) & (c > 128)))

    def relayout(src, dst):
        for j in range(2):
            left = src[:, 16 * j : 16 * j + 16, :].reshape(512, 128)
            right = src[:, 32 + 16 * j : 48 + 16 * j, :].reshape(512, 128)
            both = jnp.concatenate([left, right], 1)
            dst[0, 32 + 512 * j : 544 + 512 * j, :] = mm(perm[...], both).astype(BF)

    def extract(src):
        r, c = iota((32, 256), 0), iota((32, 256), 1)
        total = None
        for j in range(8):
            sel = one_hot((r % 16 == 8 * (c // 128) + j) & (c % 128 == 127 * (r // 16)))
            part = mm(sel, src[0, 32 + 128 * j : 160 + 128 * j, :], NT)
            total = part if total is None else total + part
        return total.astype(BF)

    loads[1].wait()
    relayout(fin, xin)
    loads[2].wait()
    relayout(fcot, xcot)
    for n, src in enumerate((xin, xcot)):
        columns = extract(src)
        for t in range(2):
            tile = columns[16 * t : 16 * t + 16, :]
            zsend[t, 16 * n : 16 * n + 16, :] = tile

    loads[0].wait()
    for x in range(16):
        cflat[80 * x + 8 : 80 * x + 72, :] = ccot[64 * x : 64 * x + 64, :].astype(F32)

    def column(y, z):
        return cflat[pl.ds(8 * y + z, 16, stride=80), :]

    for y in range(8):
        zcs[0, 16 * y : 16 * y + 16, :] = column(y + 1, 0).astype(BF)
        zcs[1, 16 * y : 16 * y + 16, :] = column(y + 1, 7).astype(BF)
    for s in range(2):
        own = (slice(32, 64), slice(0, 128)) if s == 0 else (slice(1024, 1056), slice(128, 256))
        ysend[s, 0:32, :] = xin[(0, *own)]
        ysend[s, 32:64, :] = xcot[(0, *own)]
        first = 8 if s == 0 else 64
        for x in range(0, 16, 2):
            pair = [cflat[80 * (x + q) + first : 80 * (x + q) + first + 8, :] for q in range(2)]
            ycs[s, 8 * x : 8 * x + 16, :] = jnp.concatenate(pair, 0).astype(BF)
        for t in range(2):
            dcs[s, t] = column(1 if s == 0 else 8, 0 if t == 0 else 7).astype(BF)

    pl.semaphore_wait(barrier, len(partners))

    step = (-1, 1)
    halo, halo_c = [], []
    for s in range(2):
        for t in range(2):
            q, dev = 4 + 2 * s + t, at(step[s], step[t])
            halo.append(remote(zsend.at[t], drecv.at[s, t], hs.at[q], hr.at[q], dev))
            halo_c.append(remote(dcs.at[s, t], dcr.at[s, t], cs.at[q], cr.at[q], dev))
        y, z, q = at(step[s], 0), at(0, step[s]), 2 + s
        halo.append(remote(zsend.at[s], zrecv.at[s], hs.at[q], hr.at[q], z))
        halo.append(remote(ysend.at[s], yrecv.at[s], hs.at[s], hr.at[s], y))
        halo_c.append(remote(zcs.at[s], zcr.at[s], cs.at[q], cr.at[q], z))
        halo_c.append(remote(ycs.at[s], ycr.at[s], cs.at[s], cr.at[s], y))
    for copy in halo + halo_c:
        copy.start()

    lane = iota((32, 768), 1)
    q, m = lane // 128, lane % 128
    k = 9 * ((m // 16) % 2 - q % 2 + 1) + 3 * (m // 32) + q // 2
    wanted = (m < 96, iota((32, 768), 0))
    straight = one_hot(wanted[0] & (wanted[1] == k))[:27]
    flipped = one_hot(wanted[0] & (wanted[1] == 26 - k))[:27]
    r, c = iota((256, 768), 0), iota((256, 768), 1)
    to_in, to_out = r % 16 == c % 16, r // 16 == c % 16
    r, c = iota((16, 256), 0), iota((16, 256), 1)
    by_out, by_in = one_hot(c // 16 == r), one_hot(c % 16 == r)
    loads[3].wait()
    loads[4].wait()
    for n, (w, pick, mask, rows) in enumerate(
        (
            (w1, straight, to_in, by_out),
            (w2, flipped, to_out, by_in),
            (w1, flipped, to_out, by_in),
        )
    ):
        wide = jnp.where(mask, mm(w[...], pick), 0.0).astype(BF)
        strips = mm(rows, wide)
        for cc in range(3):
            for xo in range(2):
                first = 128 * (2 * cc + xo)
                strip = strips[:, first : first + 128]
                strip = jnp.concatenate([strip, jnp.zeros_like(strip)], 1)
                for yo in range(4):
                    moved = strip if yo == 0 else pltpu.roll(strip, 32 * yo, 1)
                    first = 32 * yo + 16 * xo
                    bands[n, cc, first : first + 16, :] = moved.astype(BF)

    inp3[...] = jnp.zeros_like(inp3)
    loads[5].wait()
    for a in range(3):
        inp3[64 * (2 - a) : 64 * (2 - a) + 1024, 128 * a : 128 * a + 128] = cin[...]
    vmat[0] = jnp.zeros((64, 1152), BF)
    vmat[17] = jnp.zeros((64, 1152), BF)
    qf[...] = jnp.zeros_like(qf)

    def valid(cond, value):
        return jnp.where(cond, value, jnp.zeros_like(value))

    for copy in halo:
        copy.wait()

    def turned(after, before):
        return jnp.concatenate([after, before], 0).astype(F32).T.astype(BF)

    def fill(dst, get_y, get_d, get_z):
        r, c = iota((32, 256), 0), iota((32, 256), 1)

        def place(row, ok):
            after = (r == row) & (c == 127) & side[1] & ok
            return one_hot(after | ((r == 16 + row) & (c == 128) & side[0] & ok))

        for s in (1, 0):
            ok = up[0] if s == 1 else up[1]
            mid = valid(ok, get_y(s))
            corner = turned(get_d(s, 0), get_d(s, 1))
            corner = corner[96:128] if s == 1 else corner[0:32]
            out = mm(mid, shifts[...]) + mm(corner, place(15 if s == 1 else 0, ok))
            rows, lanes = (slice(0, 32), slice(0, 128)) if s == 1 else (slice(1056, 1088), slice(128, 256))
            dst[0, rows, lanes] = mid
            dst[2, rows, lanes] = out[:, :128].astype(BF)
            dst[1, rows, lanes] = out[:, 128:].astype(BF)
        edge = turned(get_z(0), get_z(1))
        for h in range(2):
            lanes = slice(128 * h, 128 * h + 128)
            for j in range(8):
                rows = slice(32 + 128 * j, 160 + 128 * j)
                out = mm(dst[0, rows, lanes], shifts[...]) + mm(edge, place(8 * h + j, True))
                dst[2, rows, lanes] = out[:, :128].astype(BF)
                dst[1, rows, lanes] = out[:, 128:].astype(BF)
        for v in range(3):
            dst[v, 0:32, 128:256] = dst[v, 1024:1056, 0:128]
            dst[v, 1056:1088, 0:128] = dst[v, 32:64, 128:256]

    def fill_first(n, dst):
        rows, tile = slice(32 * n, 32 * n + 32), slice(16 * n, 16 * n + 16)
        fill(
            dst,
            lambda s: yrecv[s, rows, :],
            lambda s, t: drecv[s, t, tile, :],
            lambda t: zrecv[t, tile, :],
        )

    fill_first(0, xin)

    for copy in halo_c:
        copy.wait()
    for x in range(16):
        rows = slice(8 * (x // 2 * 2), 16 + 8 * (x // 2 * 2))
        half = slice(8 * (x % 2), 8 * (x % 2) + 8)
        cflat[80 * x : 80 * x + 8, :] = valid(up[0], ycr[1, rows, :].astype(F32)[half])
        cflat[80 * x + 72 : 80 * x + 80, :] = valid(up[1], ycr[0, rows, :].astype(F32)[half])
    cplus[...] = pltpu.roll(cflat[...], 1279, 0)
    cminus[...] = pltpu.roll(cflat[...], 1, 0)
    for y in range(10):
        for ref, z, t, ok in ((cplus, 7, 0, side[1]), (cminus, 0, 1, side[0])):
            if y == 0:
                part, ok = dcr[1, t], ok & up[0]
            elif y == 9:
                part, ok = dcr[0, t], ok & up[1]
            else:
                part = zcr[t, 16 * (y - 1) : 16 * y, :]
            ref[pl.ds(8 * y + z, 16, stride=80), :] = valid(ok, part.astype(F32))

    def spread(x, carry):
        for b in range(3):
            for cc, ref in enumerate((cplus, cflat, cminus)):
                rows = ref[pl.ds(pl.multiple_of(x * 80 + 8 * (2 - b), 8), 64), :]
                q = 3 * b + cc
                vmat[x + 1, :, 128 * q : 128 * q + 128] = rows.astype(BF)
        return carry

    lax.fori_loop(0, 16, spread, 0)

    wide_o, nx = 128 // nty, nty // 2
    core, xme = lax.rem(ty, 2), lax.div(ty, 2)
    other = (dp, ty + 1 - 2 * core, tz)
    hop0 = []
    g = mm(vmat[...].reshape(1152, 1152), inp3[...], TN)
    for b in range(3):
        for a in range(3):
            for cc in range(3):
                first = 384 * b + 128 * cc
                part = g[first : first + 128, 128 * a : 128 * a + 128]
                rsend[9 * b + 3 * a + cc] = part.astype(BF).reshape(nx, 2, wide_o, 128)
        src = rsend.at[pl.ds(9 * b, 9), :, 1 - core]
        hop0.append(remote(src, rpair.at[pl.ds(9 * b, 9)], ps.at[b], pr.at[b], other))
        hop0[b].start()

    fill_first(1, xcot)

    hop1 = []
    for b in range(3):
        hop0[b].wait()
        for q in range(9 * b, 9 * b + 9):
            psum[q] = (rsend[q, :, core].astype(F32) + rpair[q].astype(F32)).astype(BF)
        for j in range(1, nx):
            x = lax.rem(xme + j, nx)
            src, dst = psum.at[pl.ds(9 * b, 9), x], rs1.at[xme, pl.ds(9 * b, 9)]
            dev = (dp, 2 * x + core, tz)
            hop1.append(remote(src, dst, r1s.at[0], r1r.at[0], dev))
            hop1[-1].start()

    version = (1, 0, 2)

    def conv(n, src, g):
        rows = pl.ds(pl.multiple_of(g * 128, 128), 192)
        out = None
        for cc in range(3):
            term = mm(bands[n, cc, :, 0:192], src[version[cc], rows, :])
            out = term if out is None else out + term
        return out

    def forward(g):
        pre = conv(0, xin, g)
        dact = conv(1, xcot, g)
        square = pre * pre
        t = jnp.tanh(C0 * pre * (1.0 + C1 * square))
        half = 0.5 + 0.5 * t
        slope = half + 0.5 * pre * (1.0 - t * t) * (C0 * (1.0 + (3.0 * C1) * square))
        act[pl.ds(pl.multiple_of(g * 128, 128), 128), :] = (pre * half).astype(BF)
        xdp[0, pl.ds(pl.multiple_of(g * 128 + 32, 32), 128), :] = (dact * slope).astype(BF)

    def four(i, carry):
        for q in range(4):
            forward(4 * i + q)
        return carry

    lax.fori_loop(0, 2, four, 0)

    def groups(ref, lead, first, count):
        return jnp.concatenate(
            [ref[(*lead, slice(128 * g + first, 128 * g + first + count))] for g in range(8)], 1
        )

    own, a_own = groups(xdp, (0,), 32, 128), groups(act, (), 0, 128)
    for cc in range(3):
        acc1[cc, :, 0:192] = mm(own, groups(xin, (version[cc],), 0, 192), NT)
        acc1[cc, :, 192:256] = jnp.zeros((128, 64), F32)
        acc2[cc] = mm(groups(xcot, (version[cc],), 0, 192), a_own, NT)
    for cc in range(3):
        total = None
        for yo in range(4):
            part = acc1[cc, 32 * yo : 32 * yo + 32, :]
            part = part if yo == 0 else pltpu.roll(part, 256 - 32 * yo, 1)
            total = part if total is None else total + part
        fpart[32 * cc : 32 * cc + 32, :] = total[:, 0:128]
    total = jnp.zeros((96, 128), F32)
    lane = iota((96, 128), 1)
    for cc in range(3):
        band = None
        for yo in range(4):
            part = acc2[cc, 32 * yo : 32 * yo + 96, :]
            turn = (32 * cc - 32 * yo) % 128
            part = part if turn == 0 else pltpu.roll(part, turn, 1)
            band = part if band is None else band + part
        total = jnp.where(lane // 32 == cc, band, total)
    fpart[96:192, :] = total

    slab = 192 // nty
    hop_a = []
    for j in range(1, nty):
        t, dev = ty_peer(j)
        src = fpart.at[pl.ds(pl.multiple_of(t * slab, 8), slab), :]
        hop_a.append(remote(src, ar1.at[ty], a1s.at[0], a1r.at[0], dev))
    for copy in hop_a:
        copy.start()
    ar1[ty] = fpart[pl.ds(pl.multiple_of(ty * slab, 8), slab), :]

    columns = extract(xdp)
    zsend2[0] = columns[0:16]
    zsend2[1] = columns[16:32]
    ysend2[0] = xdp[0, 32:64, 0:128]
    ysend2[1] = xdp[0, 1024:1056, 128:256]
    halo2 = []
    for s in range(2):
        halo2.append(remote(ysend2.at[s], yrecv2.at[s], gs.at[s], gr.at[s], at(step[s], 0)))
        halo2.append(remote(zsend2.at[s], zrecv2.at[s], gs.at[2 + s], gr.at[2 + s], at(0, step[s])))
        for t in range(2):
            q = 4 + 2 * s + t
            dev = at(step[s], step[t])
            halo2.append(remote(zsend2.at[t], drecv2.at[s, t], gs.at[q], gr.at[q], dev))
    for copy in halo2:
        copy.start()

    loads[6].wait()

    out = None
    for a in range(3):
        left = vmat[2 - a : 18 - a].reshape(1024, 1152)
        term = mm(left, wc[1152 * a : 1152 * a + 1152, :])
        out = term if out is None else out + term
    g_gci[...] = out.astype(BF)
    stores = [pltpu.make_async_copy(g_gci, o_gci, ws.at[0])]
    stores[0].start()

    arrived(ar1, nty - 1, a1s.at[0], a1r.at[0])
    total = ar1[0]
    for t in range(1, nty):
        total = total + ar1[t]
    fsum1[...] = total
    hop_b = []
    for j in range(1, zgroup):
        g, z, dev = z_peer(j)
        hop_b.append(remote(fsum1, ar2.at[me], a2s.at[0], a2r.at[0], dev))
    for copy in hop_b:
        copy.start()
    ar2[me] = fsum1[...]

    rs1[xme] = psum[:, xme]
    arrived(rs1, nx - 1, r1s.at[0], r1r.at[0])

    def sum1(q, carry):
        total = rs1[0, q].astype(F32)
        for t in range(1, nx):
            total = total + rs1[t, q].astype(F32)
        k = 9 * (lax.div(q, 3) % 3) + 3 * lax.div(q, 9) + q % 3
        qf[pl.ds(k, wide_o, stride=32), :] = total
        return carry

    lax.fori_loop(0, 27, sum1, 0)
    qb[...] = qf[...].astype(BF)
    deep = 32 * wide_o // ntz

    hop2 = []
    for j in range(1, zgroup):
        g, z, dev = z_peer(j)
        src = qb.at[pl.ds(pl.multiple_of(z * deep, 16), deep), :]
        hop2.append(remote(src, rs2.at[me], r2s.at[0], r2r.at[0], dev))
    for copy in hop2:
        copy.start()
    rs2[me] = qb[pl.ds(pl.multiple_of(tz * deep, 16), deep), :]

    for copy in halo2:
        copy.wait()
    fill(
        xdp,
        lambda s: yrecv2[s],
        lambda s, t: drecv2[s, t],
        lambda t: zrecv2[t],
    )

    def last(j, carry):
        parts = [conv(2, xdp, 4 * j + q).astype(BF) for q in range(4)]
        out = mm(perm[...], jnp.concatenate(parts, 0)).astype(BF)
        first = pl.multiple_of(16 * j, 16)
        g_gfi[:, pl.ds(first, 16), :] = out[:, :128].reshape(32, 16, 128)
        g_gfi[:, pl.ds(first + 32, 16), :] = out[:, 128:].reshape(32, 16, 128)
        return carry

    lax.fori_loop(0, 2, last, 0)
    stores.append(pltpu.make_async_copy(g_gfi, o_gfi, ws.at[1]))
    stores[1].start()

    arrived(ar2, zgroup - 1, a2s.at[0], a2r.at[0])
    total = ar2[0]
    for t in range(1, zgroup):
        total = total + ar2[t]
    fsum2[...] = total
    hop_c = []
    for j in range(1, nty):
        t, dev = ty_peer(j)
        hop_c.append(remote(fsum2, gath.at[ty], a3s.at[0], a3r.at[0], dev))
    for copy in hop_c:
        copy.start()
    gath[ty] = fsum2[...]

    arrived(rs2, zgroup - 1, r2s.at[0], r2r.at[0])
    total = rs2[0].astype(F32)
    for t in range(1, zgroup):
        total = total + rs2[t].astype(F32)
    for o in range(wide_o // ntz):
        g_gc[:, o, :] = total[32 * o : 32 * o + 27, :]
    stores.append(pltpu.make_async_copy(g_gc, o_gc, ws.at[2]))
    stores[2].start()

    arrived(gath, nty - 1, a3s.at[0], a3r.at[0])
    fpart[...] = gath[...].reshape(192, 128)
    for a in range(3):
        planes = [(xo, xo + a - 1) for xo in range(2) if 0 <= xo + a - 1 < 2]
        for b in range(3):
            for cc in range(3):
                k = 9 * a + 3 * b + cc
                one, two = None, None
                for xo, xi in planes:
                    first = 32 * cc + 16 * xo
                    lanes = slice(32 * b + 16 * xi, 32 * b + 16 * xi + 16)
                    part = fpart[first : first + 16, lanes]
                    one = part if one is None else one + part
                    first = 96 + 32 * b + 16 * xi
                    lanes = slice(32 * cc + 16 * xo, 32 * cc + 16 * xo + 16)
                    part = fpart[first : first + 16, lanes]
                    two = part if two is None else two + part
                g_gf[k] = one
                g_gs[26 - k] = two
    for n, (src, mid, dst) in enumerate(((g_gf, t_gf, o_gf), (g_gs, t_gs, o_gs))):
        for o in range(16):
            mid[o] = src[:, o, :].T
        stores.append(pltpu.make_async_copy(mid, dst, ws.at[3 + n]))
        stores[3 + n].start()
    for copy in stores:
        copy.wait()


def finish(*refs):
    srcs, dsts, mids, sems = refs[:5], refs[5:10], refs[10:15], refs[15]
    pieces = [(0, pl.ds(8 * q, 8)) for q in range(4)] + [(3, pl.ds(512 * q, 512)) for q in range(2)]
    pieces += [(n, pl.ds(0, srcs[n].shape[0])) for n in (1, 2, 4)]
    into, out = [], []
    for q, (n, rows) in enumerate(pieces):
        into.append(pltpu.make_async_copy(srcs[n].at[rows], mids[n].at[rows], sems.at[0, q]))
        out.append(pltpu.make_async_copy(mids[n].at[rows], dsts[n].at[rows], sems.at[1, q]))
        into[q].start()
    for q in range(len(pieces)):
        into[q].wait()
        out[q].start()
    for copy in out:
        copy.wait()


def solution(mesh):
    sizes = tuple(mesh.shape[a] for a in ("dp", "ty", "tz"))
    ndp, nty, ntz = sizes
    zgroup = ndp * ntz
    wide_o, nx = 128 // nty, nty // 2
    slab = 192 // nty

    def per_device(fine_input, fine_cotangent, first_weight, second_weight, coarse_input, coarse_cotangent, coarse_weight):
        def by_offset(w):
            return w.transpose(1, 2, 0).reshape(256, 27)

        dma = pltpu.SemaphoreType.DMA
        scratch = [
            pltpu.VMEM((32, 64, 128), BF),
            pltpu.VMEM((32, 64, 128), BF),
            pltpu.VMEM((256, 27), BF),
            pltpu.VMEM((256, 27), BF),
            pltpu.VMEM((1024, 128), BF),
            pltpu.VMEM((1024, 128), BF),
            pltpu.VMEM((3456, 128), BF),
            pltpu.VMEM((512, 512), BF),
            pltpu.VMEM((128, 256), BF),
            pltpu.VMEM((3, ROWS, 256), BF),
            pltpu.VMEM((3, ROWS, 256), BF),
            pltpu.VMEM((3, ROWS, 256), BF),
            pltpu.VMEM((1024, 256), BF),
            pltpu.VMEM((3, 3, 128, 256), BF),
            pltpu.VMEM((2, 64, 128), BF),
            pltpu.VMEM((2, 64, 128), BF),
            pltpu.VMEM((2, 32, 128), BF),
            pltpu.VMEM((2, 32, 128), BF),
            pltpu.VMEM((2, 2, 32, 128), BF),
            pltpu.VMEM((2, 128, 128), BF),
            pltpu.VMEM((2, 128, 128), BF),
            pltpu.VMEM((2, 128, 128), BF),
            pltpu.VMEM((2, 128, 128), BF),
            pltpu.VMEM((2, 2, 16, 128), BF),
            pltpu.VMEM((2, 2, 16, 128), BF),
            pltpu.VMEM((2, 32, 128), BF),
            pltpu.VMEM((2, 32, 128), BF),
            pltpu.VMEM((2, 16, 128), BF),
            pltpu.VMEM((2, 16, 128), BF),
            pltpu.VMEM((2, 2, 16, 128), BF),
            pltpu.VMEM((1280, 128), F32),
            pltpu.VMEM((1280, 128), F32),
            pltpu.VMEM((1280, 128), F32),
            pltpu.VMEM((18, 64, 1152), BF),
            pltpu.VMEM((1152, 384), BF),
            pltpu.VMEM((27, nx, 2, wide_o, 128), BF),
            pltpu.VMEM((27, nx, wide_o, 128), BF),
            pltpu.VMEM((27, nx, wide_o, 128), BF),
            pltpu.VMEM((nx, 27, wide_o, 128), BF),
            pltpu.VMEM((32 * wide_o, 128), F32),
            pltpu.VMEM((32 * wide_o, 128), BF),
            pltpu.VMEM((zgroup, 32 * wide_o // ntz, 128), BF),
            pltpu.VMEM((1024, 128), BF),
            pltpu.VMEM((32, 64, 128), BF),
            pltpu.VMEM((27, 16, 16), F32),
            pltpu.VMEM((27, 16, 16), F32),
            pltpu.VMEM((16, 16, 27), F32),
            pltpu.VMEM((16, 16, 27), F32),
            pltpu.VMEM((27, wide_o // ntz, 128), F32),
            pltpu.VMEM((3, 128, 256), F32),
            pltpu.VMEM((3, 192, 128), F32),
            pltpu.VMEM((192, 128), F32),
            pltpu.VMEM((nty, slab, 128), F32),
            pltpu.VMEM((slab, 128), F32),
            pltpu.VMEM((zgroup, slab, 128), F32),
            pltpu.VMEM((slab, 128), F32),
            pltpu.VMEM((nty, slab, 128), F32),
            dma((7,)),
            dma((8,)),
            dma((8,)),
            dma((8,)),
            dma((8,)),
            dma((3,)),
            dma((3,)),
            dma((8,)),
            dma((8,)),
            dma((1,)),
            dma((1,)),
            dma((1,)),
            dma((1,)),
            dma((1,)),
            dma((1,)),
            dma((1,)),
            dma((1,)),
            dma((1,)),
            dma((1,)),
            dma((5,)),
        ]
        outs = pl.pallas_call(
            functools.partial(kernel, sizes),
            out_shape=(
                jax.ShapeDtypeStruct((32, 64, 128), BF),
                jax.ShapeDtypeStruct((16, 16, 27), F32),
                jax.ShapeDtypeStruct((16, 16, 27), F32),
                jax.ShapeDtypeStruct((1024, 128), BF),
                jax.ShapeDtypeStruct((27, wide_o // ntz, 128), F32),
            ),
            in_specs=[pl.BlockSpec(memory_space=pl.ANY)] * 7,
            out_specs=(pl.BlockSpec(memory_space=pl.ANY),) * 5,
            scratch_shapes=scratch,
            compiler_params=pltpu.CompilerParams(
                collective_id=0, has_side_effects=True, vmem_limit_bytes=60 * 1024 * 1024
            ),
        )(
            fine_input.reshape(32, 64, 128),
            fine_cotangent.reshape(32, 64, 128),
            by_offset(first_weight),
            by_offset(second_weight),
            coarse_input.reshape(1024, 128),
            coarse_cotangent.reshape(1024, 128),
            coarse_weight.reshape(3456, 128),
        )
        far = pl.BlockSpec(memory_space=pl.ANY)
        outs = pl.pallas_call(
            finish,
            out_shape=(
                jax.ShapeDtypeStruct((32, 64, 128), BF),
                jax.ShapeDtypeStruct((16, 16, 27), F32),
                jax.ShapeDtypeStruct((16, 16, 27), F32),
                jax.ShapeDtypeStruct((1024, 128), BF),
                jax.ShapeDtypeStruct((27, wide_o // ntz, 128), F32),
            ),
            in_specs=[far] * 5,
            out_specs=(far,) * 5,
            scratch_shapes=[
                pltpu.VMEM((32, 64, 128), BF),
                pltpu.VMEM((16, 16, 27), F32),
                pltpu.VMEM((16, 16, 27), F32),
                pltpu.VMEM((1024, 128), BF),
                pltpu.VMEM((27, wide_o // ntz, 128), F32),
                dma((2, 9)),
            ],
            compiler_params=pltpu.CompilerParams(vmem_limit_bytes=60 * 1024 * 1024),
        )(*outs)
        return (
            outs[0].reshape(fine_input.shape),
            outs[1].transpose(2, 0, 1),
            outs[2].transpose(2, 0, 1),
            outs[3].reshape(coarse_input.shape),
            outs[4].transpose(1, 0, 2),
        )

    fine = P("dp", None, None, "ty", "tz")
    wide = P("dp", None, "ty", "tz", None)
    return jax.shard_map(
        per_device,
        mesh=mesh,
        in_specs=(fine, fine, P(), P(), wide, wide, P()),
        out_specs=(fine, P(), P(), wide, P(("ty", "tz"), None, None)),
        check_vma=False,
    )
```

```python
import functools

import jax
import jax.numpy as jnp
from jax import lax
from jax.experimental import pallas as pl
from jax.experimental.pallas import tpu as pltpu
from jax.sharding import PartitionSpec as P

MESH = pl.DeviceIdType.MESH
BF = jnp.bfloat16
F32 = jnp.float32
NN = (((1,), (0,)), ((), ()))
NT = (((1,), (1,)), ((), ()))
TN = (((0,), (0,)), ((), ()))
ROWS = 34 * 32
C0 = 0.7978845608028654
C1 = 0.044715


def mm(a, b, dims=NN):
    return lax.dot_general(a, b, dims, preferred_element_type=F32)


def iota(shape, dim):
    return lax.broadcasted_iota(jnp.int32, shape, dim)


def one_hot(cond):
    return jnp.where(cond, 1.0, 0.0).astype(BF)


def kernel(
    sizes,
    h_fin,
    h_fcot,
    h_w1,
    h_w2,
    h_cin,
    h_ccot,
    h_wc,
    o_gfi,
    o_gf,
    o_gs,
    o_gci,
    o_gc,
    fin,
    fcot,
    w1,
    w2,
    cin,
    ccot,
    wc,
    perm,
    shifts,
    xin,
    xcot,
    xdp,
    act,
    bands,
    ysend,
    yrecv,
    zsend,
    zrecv,
    drecv,
    ycs,
    ycr,
    zcs,
    zcr,
    dcs,
    dcr,
    ysend2,
    yrecv2,
    zsend2,
    zrecv2,
    drecv2,
    cflat,
    cplus,
    cminus,
    vmat,
    inp3,
    rsend,
    rpair,
    psum,
    rs1,
    qf,
    qb,
    rs2,
    g_gci,
    g_gfi,
    g_gf,
    g_gs,
    t_gf,
    t_gs,
    g_gc,
    acc1,
    acc2,
    fpart,
    ar1,
    fsum1,
    ar2,
    fsum2,
    gath,
    ls,
    hs,
    hr,
    cs,
    cr,
    ps,
    pr,
    gs,
    gr,
    r1s,
    r1r,
    r2s,
    r2r,
    a1s,
    a1r,
    a2s,
    a2r,
    a3s,
    a3r,
    ws,
):
    ndp, nty, ntz = sizes
    dp, ty, tz = lax.axis_index("dp"), lax.axis_index("ty"), lax.axis_index("tz")
    zgroup = ndp * ntz
    me = dp * ntz + tz

    def at(dy, dz):
        return (dp, lax.rem(ty + dy + nty, nty), lax.rem(tz + dz + ntz, ntz))

    def ty_peer(j):
        t = lax.rem(ty + j, nty)
        return t, (dp, t, tz)

    def z_peer(j):
        g = lax.rem(me + j, zgroup)
        z = lax.rem(g, ntz)
        return g, z, (lax.div(g, ntz), ty, z)

    def remote(src, dst, ssem, rsem, dev):
        return pltpu.make_async_remote_copy(
            src_ref=src,
            dst_ref=dst,
            send_sem=ssem,
            recv_sem=rsem,
            device_id=dev,
            device_id_type=MESH,
        )

    def arrived(buf, count, ssem, rsem):
        part = buf.at[pl.ds(0, count)]
        for sem in (ssem, rsem):
            pltpu.make_async_copy(part, part, sem).wait()

    up = (ty > 0, ty < nty - 1)
    side = (tz > 0, tz < ntz - 1)

    barrier = pltpu.get_barrier_semaphore()
    partners = [at(dy, dz) for dy in (-1, 1) for dz in (-1, 1)]
    partners += [ty_peer(j)[1] for j in range(1, nty)]
    partners += [z_peer(j)[2] for j in range(1, zgroup)]
    for dev in partners:
        pl.semaphore_signal(barrier, inc=1, device_id=dev, device_id_type=MESH)

    loads = []
    pairs = ((h_ccot, ccot), (h_fin, fin), (h_fcot, fcot), (h_w1, w1), (h_w2, w2), (h_cin, cin), (h_wc, wc))
    for n, (src, dst) in enumerate(pairs):
        loads.append(pltpu.make_async_copy(src, dst, ls.at[n]))
        loads[n].start()

    r, c = iota((512, 512), 0), iota((512, 512), 1)
    perm[...] = one_hot(c == (r % 16) * 32 + ((r // 16) % 2) * 16 + r // 32)
    r, c = iota((128, 256), 0), iota((128, 256), 1)
    shifts[...] = one_hot(((r == c + 1) & (c < 127)) | ((r + 1 == c - 128) & (c > 128)))

    def relayout(src, dst):
        for j in range(2):
            left = src[:, 16 * j : 16 * j + 16, :].reshape(512, 128)
            right = src[:, 32 + 16 * j : 48 + 16 * j, :].reshape(512, 128)
            both = jnp.concatenate([left, right], 1)
            dst[0, 32 + 512 * j : 544 + 512 * j, :] = mm(perm[...], both).astype(BF)

    def extract(src):
        r, c = iota((32, 256), 0), iota((32, 256), 1)
        total = None
        for j in range(8):
            sel = one_hot((r % 16 == 8 * (c // 128) + j) & (c % 128 == 127 * (r // 16)))
            part = mm(sel, src[0, 32 + 128 * j : 160 + 128 * j, :], NT)
            total = part if total is None else total + part
        return total.astype(BF)

    loads[1].wait()
    relayout(fin, xin)
    loads[2].wait()
    relayout(fcot, xcot)
    for n, src in enumerate((xin, xcot)):
        columns = extract(src)
        for t in range(2):
            tile = columns[16 * t : 16 * t + 16, :]
            zsend[t, 16 * n : 16 * n + 16, :] = tile

    loads[0].wait()
    for x in range(16):
        cflat[80 * x + 8 : 80 * x + 72, :] = ccot[64 * x : 64 * x + 64, :].astype(F32)

    def column(y, z):
        return cflat[pl.ds(8 * y + z, 16, stride=80), :]

    for y in range(8):
        zcs[0, 16 * y : 16 * y + 16, :] = column(y + 1, 0).astype(BF)
        zcs[1, 16 * y : 16 * y + 16, :] = column(y + 1, 7).astype(BF)
    for s in range(2):
        own = (slice(32, 64), slice(0, 128)) if s == 0 else (slice(1024, 1056), slice(128, 256))
        ysend[s, 0:32, :] = xin[(0, *own)]
        ysend[s, 32:64, :] = xcot[(0, *own)]
        first = 8 if s == 0 else 64
        for x in range(0, 16, 2):
            pair = [cflat[80 * (x + q) + first : 80 * (x + q) + first + 8, :] for q in range(2)]
            ycs[s, 8 * x : 8 * x + 16, :] = jnp.concatenate(pair, 0).astype(BF)
        for t in range(2):
            dcs[s, t] = column(1 if s == 0 else 8, 0 if t == 0 else 7).astype(BF)

    pl.semaphore_wait(barrier, len(partners))

    step = (-1, 1)
    halo, halo_c = [], []
    for s in range(2):
        for t in range(2):
            q, dev = 4 + 2 * s + t, at(step[s], step[t])
            halo.append(remote(zsend.at[t], drecv.at[s, t], hs.at[q], hr.at[q], dev))
            halo_c.append(remote(dcs.at[s, t], dcr.at[s, t], cs.at[q], cr.at[q], dev))
        y, z, q = at(step[s], 0), at(0, step[s]), 2 + s
        halo.append(remote(zsend.at[s], zrecv.at[s], hs.at[q], hr.at[q], z))
        halo.append(remote(ysend.at[s], yrecv.at[s], hs.at[s], hr.at[s], y))
        halo_c.append(remote(zcs.at[s], zcr.at[s], cs.at[q], cr.at[q], z))
        halo_c.append(remote(ycs.at[s], ycr.at[s], cs.at[s], cr.at[s], y))
    for copy in halo + halo_c:
        copy.start()

    lane = iota((32, 768), 1)
    q, m = lane // 128, lane % 128
    k = 9 * ((m // 16) % 2 - q % 2 + 1) + 3 * (m // 32) + q // 2
    wanted = (m < 96, iota((32, 768), 0))
    straight = one_hot(wanted[0] & (wanted[1] == k))[:27]
    flipped = one_hot(wanted[0] & (wanted[1] == 26 - k))[:27]
    r, c = iota((256, 768), 0), iota((256, 768), 1)
    to_in, to_out = r % 16 == c % 16, r // 16 == c % 16
    r, c = iota((16, 256), 0), iota((16, 256), 1)
    by_out, by_in = one_hot(c // 16 == r), one_hot(c % 16 == r)
    loads[3].wait()
    loads[4].wait()
    for n, (w, pick, mask, rows) in enumerate(
        (
            (w1, straight, to_in, by_out),
            (w2, flipped, to_out, by_in),
            (w1, flipped, to_out, by_in),
        )
    ):
        wide = jnp.where(mask, mm(w[...], pick), 0.0).astype(BF)
        strips = mm(rows, wide)
        for cc in range(3):
            for xo in range(2):
                first = 128 * (2 * cc + xo)
                strip = strips[:, first : first + 128]
                strip = jnp.concatenate([strip, jnp.zeros_like(strip)], 1)
                for yo in range(4):
                    moved = strip if yo == 0 else pltpu.roll(strip, 32 * yo, 1)
                    first = 32 * yo + 16 * xo
                    bands[n, cc, first : first + 16, :] = moved.astype(BF)

    inp3[...] = jnp.zeros_like(inp3)
    loads[5].wait()
    for a in range(3):
        inp3[64 * (2 - a) : 64 * (2 - a) + 1024, 128 * a : 128 * a + 128] = cin[...]
    vmat[0] = jnp.zeros((64, 1152), BF)
    vmat[17] = jnp.zeros((64, 1152), BF)
    qf[...] = jnp.zeros_like(qf)

    def valid(cond, value):
        return jnp.where(cond, value, jnp.zeros_like(value))

    for copy in halo:
        copy.wait()

    def turned(after, before):
        return jnp.concatenate([after, before], 0).astype(F32).T.astype(BF)

    def fill(dst, get_y, get_d, get_z):
        r, c = iota((32, 256), 0), iota((32, 256), 1)

        def place(row, ok):
            after = (r == row) & (c == 127) & side[1] & ok
            return one_hot(after | ((r == 16 + row) & (c == 128) & side[0] & ok))

        for s in (1, 0):
            ok = up[0] if s == 1 else up[1]
            mid = valid(ok, get_y(s))
            corner = turned(get_d(s, 0), get_d(s, 1))
            corner = corner[96:128] if s == 1 else corner[0:32]
            out = mm(mid, shifts[...]) + mm(corner, place(15 if s == 1 else 0, ok))
            rows, lanes = (slice(0, 32), slice(0, 128)) if s == 1 else (slice(1056, 1088), slice(128, 256))
            dst[0, rows, lanes] = mid
            dst[2, rows, lanes] = out[:, :128].astype(BF)
            dst[1, rows, lanes] = out[:, 128:].astype(BF)
        edge = turned(get_z(0), get_z(1))
        for h in range(2):
            lanes = slice(128 * h, 128 * h + 128)
            for j in range(8):
                rows = slice(32 + 128 * j, 160 + 128 * j)
                out = mm(dst[0, rows, lanes], shifts[...]) + mm(edge, place(8 * h + j, True))
                dst[2, rows, lanes] = out[:, :128].astype(BF)
                dst[1, rows, lanes] = out[:, 128:].astype(BF)
        for v in range(3):
            dst[v, 0:32, 128:256] = dst[v, 1024:1056, 0:128]
            dst[v, 1056:1088, 0:128] = dst[v, 32:64, 128:256]

    def fill_first(n, dst):
        rows, tile = slice(32 * n, 32 * n + 32), slice(16 * n, 16 * n + 16)
        fill(
            dst,
            lambda s: yrecv[s, rows, :],
            lambda s, t: drecv[s, t, tile, :],
            lambda t: zrecv[t, tile, :],
        )

    fill_first(0, xin)

    for copy in halo_c:
        copy.wait()
    for x in range(16):
        rows = slice(8 * (x // 2 * 2), 16 + 8 * (x // 2 * 2))
        half = slice(8 * (x % 2), 8 * (x % 2) + 8)
        cflat[80 * x : 80 * x + 8, :] = valid(up[0], ycr[1, rows, :].astype(F32)[half])
        cflat[80 * x + 72 : 80 * x + 80, :] = valid(up[1], ycr[0, rows, :].astype(F32)[half])
    cplus[...] = pltpu.roll(cflat[...], 1279, 0)
    cminus[...] = pltpu.roll(cflat[...], 1, 0)
    for y in range(10):
        for ref, z, t, ok in ((cplus, 7, 0, side[1]), (cminus, 0, 1, side[0])):
            if y == 0:
                part, ok = dcr[1, t], ok & up[0]
            elif y == 9:
                part, ok = dcr[0, t], ok & up[1]
            else:
                part = zcr[t, 16 * (y - 1) : 16 * y, :]
            ref[pl.ds(8 * y + z, 16, stride=80), :] = valid(ok, part.astype(F32))

    def spread(x, carry):
        for b in range(3):
            for cc, ref in enumerate((cplus, cflat, cminus)):
                rows = ref[pl.ds(pl.multiple_of(x * 80 + 8 * (2 - b), 8), 64), :]
                q = 3 * b + cc
                vmat[x + 1, :, 128 * q : 128 * q + 128] = rows.astype(BF)
        return carry

    lax.fori_loop(0, 16, spread, 0)

    wide_o, nx = 128 // nty, nty // 2
    core, xme = lax.rem(ty, 2), lax.div(ty, 2)
    other = (dp, ty + 1 - 2 * core, tz)
    hop0 = []
    g = mm(vmat[...].reshape(1152, 1152), inp3[...], TN)
    for b in range(3):
        for a in range(3):
            for cc in range(3):
                first = 384 * b + 128 * cc
                part = g[first : first + 128, 128 * a : 128 * a + 128]
                rsend[9 * b + 3 * a + cc] = part.astype(BF).reshape(nx, 2, wide_o, 128)
        src = rsend.at[pl.ds(9 * b, 9), :, 1 - core]
        hop0.append(remote(src, rpair.at[pl.ds(9 * b, 9)], ps.at[b], pr.at[b], other))
        hop0[b].start()

    fill_first(1, xcot)

    version = (1, 0, 2)

    def conv(n, src, g):
        rows = pl.ds(pl.multiple_of(g * 128, 128), 192)
        out = None
        for cc in range(3):
            term = mm(bands[n, cc, :, 0:192], src[version[cc], rows, :])
            out = term if out is None else out + term
        return out

    def forward(g):
        pre = conv(0, xin, g)
        dact = conv(1, xcot, g)
        square = pre * pre
        t = jnp.tanh(C0 * pre * (1.0 + C1 * square))
        half = 0.5 + 0.5 * t
        slope = half + 0.5 * pre * (1.0 - t * t) * (C0 * (1.0 + (3.0 * C1) * square))
        act[pl.ds(pl.multiple_of(g * 128, 128), 128), :] = (pre * half).astype(BF)
        xdp[0, pl.ds(pl.multiple_of(g * 128 + 32, 32), 128), :] = (dact * slope).astype(BF)

    hop1 = []

    def send_sum(b):
        hop0[b].wait()
        for q in range(9 * b, 9 * b + 9):
            psum[q] = (rsend[q, :, core].astype(F32) + rpair[q].astype(F32)).astype(BF)
        for j in range(1, nx):
            x = lax.rem(xme + j, nx)
            src, dst = psum.at[pl.ds(9 * b, 9), x], rs1.at[xme, pl.ds(9 * b, 9)]
            dev = (dp, 2 * x + core, tz)
            hop1.append(remote(src, dst, r1s.at[0], r1r.at[0], dev))
            hop1[-1].start()

    send_sum(0)
    for g in range(8):
        forward(g)
        if g == 3:
            send_sum(1)
    send_sum(2)

    def groups(ref, lead, first, count):
        return jnp.concatenate(
            [ref[(*lead, slice(128 * g + first, 128 * g + first + count))] for g in range(8)], 1
        )

    own, a_own = groups(xdp, (0,), 32, 128), groups(act, (), 0, 128)
    for cc in range(3):
        acc1[cc, :, 0:192] = mm(own, groups(xin, (version[cc],), 0, 192), NT)
        acc1[cc, :, 192:256] = jnp.zeros((128, 64), F32)
        acc2[cc] = mm(groups(xcot, (version[cc],), 0, 192), a_own, NT)
    for cc in range(3):
        total = None
        for yo in range(4):
            part = acc1[cc, 32 * yo : 32 * yo + 32, :]
            part = part if yo == 0 else pltpu.roll(part, 256 - 32 * yo, 1)
            total = part if total is None else total + part
        fpart[32 * cc : 32 * cc + 32, :] = total[:, 0:128]
    total = jnp.zeros((96, 128), F32)
    lane = iota((96, 128), 1)
    for cc in range(3):
        band = None
        for yo in range(4):
            part = acc2[cc, 32 * yo : 32 * yo + 96, :]
            turn = (32 * cc - 32 * yo) % 128
            part = part if turn == 0 else pltpu.roll(part, turn, 1)
            band = part if band is None else band + part
        total = jnp.where(lane // 32 == cc, band, total)
    fpart[96:192, :] = total

    slab = 192 // nty
    hop_a = []
    for j in range(1, nty):
        t, dev = ty_peer(j)
        src = fpart.at[pl.ds(pl.multiple_of(t * slab, 8), slab), :]
        hop_a.append(remote(src, ar1.at[ty], a1s.at[0], a1r.at[0], dev))
    for copy in hop_a:
        copy.start()
    ar1[ty] = fpart[pl.ds(pl.multiple_of(ty * slab, 8), slab), :]

    columns = extract(xdp)
    zsend2[0] = columns[0:16]
    zsend2[1] = columns[16:32]
    ysend2[0] = xdp[0, 32:64, 0:128]
    ysend2[1] = xdp[0, 1024:1056, 128:256]
    halo2 = []
    for s in range(2):
        halo2.append(remote(ysend2.at[s], yrecv2.at[s], gs.at[s], gr.at[s], at(step[s], 0)))
        halo2.append(remote(zsend2.at[s], zrecv2.at[s], gs.at[2 + s], gr.at[2 + s], at(0, step[s])))
        for t in range(2):
            q = 4 + 2 * s + t
            dev = at(step[s], step[t])
            halo2.append(remote(zsend2.at[t], drecv2.at[s, t], gs.at[q], gr.at[q], dev))
    for copy in halo2:
        copy.start()

    loads[6].wait()

    out = None
    for a in range(3):
        left = vmat[2 - a : 18 - a].reshape(1024, 1152)
        term = mm(left, wc[1152 * a : 1152 * a + 1152, :])
        out = term if out is None else out + term
    g_gci[...] = out.astype(BF)
    stores = [pltpu.make_async_copy(g_gci, o_gci, ws.at[0])]
    stores[0].start()

    arrived(ar1, nty - 1, a1s.at[0], a1r.at[0])
    total = ar1[0]
    for t in range(1, nty):
        total = total + ar1[t]
    fsum1[...] = total
    hop_b = []
    for j in range(1, zgroup):
        g, z, dev = z_peer(j)
        hop_b.append(remote(fsum1, ar2.at[me], a2s.at[0], a2r.at[0], dev))
    for copy in hop_b:
        copy.start()
    ar2[me] = fsum1[...]

    for copy in halo2:
        copy.wait()
    fill(
        xdp,
        lambda s: yrecv2[s],
        lambda s, t: drecv2[s, t],
        lambda t: zrecv2[t],
    )

    rs1[xme] = psum[:, xme]
    arrived(rs1, nx - 1, r1s.at[0], r1r.at[0])

    def sum1(q, carry):
        total = rs1[0, q].astype(F32)
        for t in range(1, nx):
            total = total + rs1[t, q].astype(F32)
        k = 9 * (lax.div(q, 3) % 3) + 3 * lax.div(q, 9) + q % 3
        qf[pl.ds(k, wide_o, stride=32), :] = total
        return carry

    lax.fori_loop(0, 27, sum1, 0)
    qb[...] = qf[...].astype(BF)
    deep = 32 * wide_o // ntz

    hop2 = []
    for j in range(1, zgroup):
        g, z, dev = z_peer(j)
        src = qb.at[pl.ds(pl.multiple_of(z * deep, 16), deep), :]
        hop2.append(remote(src, rs2.at[me], r2s.at[0], r2r.at[0], dev))
    for copy in hop2:
        copy.start()
    rs2[me] = qb[pl.ds(pl.multiple_of(tz * deep, 16), deep), :]

    def last(j, carry):
        parts = [conv(2, xdp, 4 * j + q).astype(BF) for q in range(4)]
        out = mm(perm[...], jnp.concatenate(parts, 0)).astype(BF)
        first = pl.multiple_of(16 * j, 16)
        g_gfi[:, pl.ds(first, 16), :] = out[:, :128].reshape(32, 16, 128)
        g_gfi[:, pl.ds(first + 32, 16), :] = out[:, 128:].reshape(32, 16, 128)
        return carry

    lax.fori_loop(0, 2, last, 0)
    stores.append(pltpu.make_async_copy(g_gfi, o_gfi, ws.at[1]))
    stores[1].start()

    arrived(ar2, zgroup - 1, a2s.at[0], a2r.at[0])
    total = ar2[0]
    for t in range(1, zgroup):
        total = total + ar2[t]
    fsum2[...] = total
    hop_c = []
    for j in range(1, nty):
        t, dev = ty_peer(j)
        hop_c.append(remote(fsum2, gath.at[ty], a3s.at[0], a3r.at[0], dev))
    for copy in hop_c:
        copy.start()
    gath[ty] = fsum2[...]

    arrived(rs2, zgroup - 1, r2s.at[0], r2r.at[0])
    total = rs2[0].astype(F32)
    for t in range(1, zgroup):
        total = total + rs2[t].astype(F32)
    for o in range(wide_o // ntz):
        g_gc[:, o, :] = total[32 * o : 32 * o + 27, :]
    stores.append(pltpu.make_async_copy(g_gc, o_gc, ws.at[2]))
    stores[2].start()

    arrived(gath, nty - 1, a3s.at[0], a3r.at[0])
    fpart[...] = gath[...].reshape(192, 128)
    for a in range(3):
        planes = [(xo, xo + a - 1) for xo in range(2) if 0 <= xo + a - 1 < 2]
        for b in range(3):
            for cc in range(3):
                k = 9 * a + 3 * b + cc
                one, two = None, None
                for xo, xi in planes:
                    first = 32 * cc + 16 * xo
                    lanes = slice(32 * b + 16 * xi, 32 * b + 16 * xi + 16)
                    part = fpart[first : first + 16, lanes]
                    one = part if one is None else one + part
                    first = 96 + 32 * b + 16 * xi
                    lanes = slice(32 * cc + 16 * xo, 32 * cc + 16 * xo + 16)
                    part = fpart[first : first + 16, lanes]
                    two = part if two is None else two + part
                g_gf[k] = one
                g_gs[26 - k] = two
    for n, (src, mid, dst) in enumerate(((g_gf, t_gf, o_gf), (g_gs, t_gs, o_gs))):
        for o in range(16):
            mid[o] = src[:, o, :].T
        stores.append(pltpu.make_async_copy(mid, dst, ws.at[3 + n]))
        stores[3 + n].start()
    for copy in stores:
        copy.wait()


def finish(*refs):
    srcs, dsts, mids, sems = refs[:5], refs[5:10], refs[10:15], refs[15]
    pieces = [(0, pl.ds(8 * q, 8)) for q in range(4)] + [(3, pl.ds(512 * q, 512)) for q in range(2)]
    pieces += [(n, pl.ds(0, srcs[n].shape[0])) for n in (1, 2, 4)]
    into, out = [], []
    for q, (n, rows) in enumerate(pieces):
        into.append(pltpu.make_async_copy(srcs[n].at[rows], mids[n].at[rows], sems.at[0, q]))
        out.append(pltpu.make_async_copy(mids[n].at[rows], dsts[n].at[rows], sems.at[1, q]))
        into[q].start()
    for q in range(len(pieces)):
        into[q].wait()
        out[q].start()
    for copy in out:
        copy.wait()


def solution(mesh):
    sizes = tuple(mesh.shape[a] for a in ("dp", "ty", "tz"))
    ndp, nty, ntz = sizes
    zgroup = ndp * ntz
    wide_o, nx = 128 // nty, nty // 2
    slab = 192 // nty

    def per_device(fine_input, fine_cotangent, first_weight, second_weight, coarse_input, coarse_cotangent, coarse_weight):
        def by_offset(w):
            return w.transpose(1, 2, 0).reshape(256, 27)

        dma = pltpu.SemaphoreType.DMA
        scratch = [
            pltpu.VMEM((32, 64, 128), BF),
            pltpu.VMEM((32, 64, 128), BF),
            pltpu.VMEM((256, 27), BF),
            pltpu.VMEM((256, 27), BF),
            pltpu.VMEM((1024, 128), BF),
            pltpu.VMEM((1024, 128), BF),
            pltpu.VMEM((3456, 128), BF),
            pltpu.VMEM((512, 512), BF),
            pltpu.VMEM((128, 256), BF),
            pltpu.VMEM((3, ROWS, 256), BF),
            pltpu.VMEM((3, ROWS, 256), BF),
            pltpu.VMEM((3, ROWS, 256), BF),
            pltpu.VMEM((1024, 256), BF),
            pltpu.VMEM((3, 3, 128, 256), BF),
            pltpu.VMEM((2, 64, 128), BF),
            pltpu.VMEM((2, 64, 128), BF),
            pltpu.VMEM((2, 32, 128), BF),
            pltpu.VMEM((2, 32, 128), BF),
            pltpu.VMEM((2, 2, 32, 128), BF),
            pltpu.VMEM((2, 128, 128), BF),
            pltpu.VMEM((2, 128, 128), BF),
            pltpu.VMEM((2, 128, 128), BF),
            pltpu.VMEM((2, 128, 128), BF),
            pltpu.VMEM((2, 2, 16, 128), BF),
            pltpu.VMEM((2, 2, 16, 128), BF),
            pltpu.VMEM((2, 32, 128), BF),
            pltpu.VMEM((2, 32, 128), BF),
            pltpu.VMEM((2, 16, 128), BF),
            pltpu.VMEM((2, 16, 128), BF),
            pltpu.VMEM((2, 2, 16, 128), BF),
            pltpu.VMEM((1280, 128), F32),
            pltpu.VMEM((1280, 128), F32),
            pltpu.VMEM((1280, 128), F32),
            pltpu.VMEM((18, 64, 1152), BF),
            pltpu.VMEM((1152, 384), BF),
            pltpu.VMEM((27, nx, 2, wide_o, 128), BF),
            pltpu.VMEM((27, nx, wide_o, 128), BF),
            pltpu.VMEM((27, nx, wide_o, 128), BF),
            pltpu.VMEM((nx, 27, wide_o, 128), BF),
            pltpu.VMEM((32 * wide_o, 128), F32),
            pltpu.VMEM((32 * wide_o, 128), BF),
            pltpu.VMEM((zgroup, 32 * wide_o // ntz, 128), BF),
            pltpu.VMEM((1024, 128), BF),
            pltpu.VMEM((32, 64, 128), BF),
            pltpu.VMEM((27, 16, 16), F32),
            pltpu.VMEM((27, 16, 16), F32),
            pltpu.VMEM((16, 16, 27), F32),
            pltpu.VMEM((16, 16, 27), F32),
            pltpu.VMEM((27, wide_o // ntz, 128), F32),
            pltpu.VMEM((3, 128, 256), F32),
            pltpu.VMEM((3, 192, 128), F32),
            pltpu.VMEM((192, 128), F32),
            pltpu.VMEM((nty, slab, 128), F32),
            pltpu.VMEM((slab, 128), F32),
            pltpu.VMEM((zgroup, slab, 128), F32),
            pltpu.VMEM((slab, 128), F32),
            pltpu.VMEM((nty, slab, 128), F32),
            dma((7,)),
            dma((8,)),
            dma((8,)),
            dma((8,)),
            dma((8,)),
            dma((3,)),
            dma((3,)),
            dma((8,)),
            dma((8,)),
            dma((1,)),
            dma((1,)),
            dma((1,)),
            dma((1,)),
            dma((1,)),
            dma((1,)),
            dma((1,)),
            dma((1,)),
            dma((1,)),
            dma((1,)),
            dma((5,)),
        ]
        outs = pl.pallas_call(
            functools.partial(kernel, sizes),
            out_shape=(
                jax.ShapeDtypeStruct((32, 64, 128), BF),
                jax.ShapeDtypeStruct((16, 16, 27), F32),
                jax.ShapeDtypeStruct((16, 16, 27), F32),
                jax.ShapeDtypeStruct((1024, 128), BF),
                jax.ShapeDtypeStruct((27, wide_o // ntz, 128), F32),
            ),
            in_specs=[pl.BlockSpec(memory_space=pl.ANY)] * 7,
            out_specs=(pl.BlockSpec(memory_space=pl.ANY),) * 5,
            scratch_shapes=scratch,
            compiler_params=pltpu.CompilerParams(
                collective_id=0, has_side_effects=True, vmem_limit_bytes=60 * 1024 * 1024
            ),
        )(
            fine_input.reshape(32, 64, 128),
            fine_cotangent.reshape(32, 64, 128),
            by_offset(first_weight),
            by_offset(second_weight),
            coarse_input.reshape(1024, 128),
            coarse_cotangent.reshape(1024, 128),
            coarse_weight.reshape(3456, 128),
        )
        far = pl.BlockSpec(memory_space=pl.ANY)
        outs = pl.pallas_call(
            finish,
            out_shape=(
                jax.ShapeDtypeStruct((32, 64, 128), BF),
                jax.ShapeDtypeStruct((16, 16, 27), F32),
                jax.ShapeDtypeStruct((16, 16, 27), F32),
                jax.ShapeDtypeStruct((1024, 128), BF),
                jax.ShapeDtypeStruct((27, wide_o // ntz, 128), F32),
            ),
            in_specs=[far] * 5,
            out_specs=(far,) * 5,
            scratch_shapes=[
                pltpu.VMEM((32, 64, 128), BF),
                pltpu.VMEM((16, 16, 27), F32),
                pltpu.VMEM((16, 16, 27), F32),
                pltpu.VMEM((1024, 128), BF),
                pltpu.VMEM((27, wide_o // ntz, 128), F32),
                dma((2, 9)),
            ],
            compiler_params=pltpu.CompilerParams(vmem_limit_bytes=60 * 1024 * 1024),
        )(*outs)
        return (
            outs[0].reshape(fine_input.shape),
            outs[1].transpose(2, 0, 1),
            outs[2].transpose(2, 0, 1),
            outs[3].reshape(coarse_input.shape),
            outs[4].transpose(1, 0, 2),
        )

    fine = P("dp", None, None, "ty", "tz")
    wide = P("dp", None, "ty", "tz", None)
    return jax.shard_map(
        per_device,
        mesh=mesh,
        in_specs=(fine, fine, P(), P(), wide, wide, P()),
        out_specs=(fine, P(), P(), wide, P(("ty", "tz"), None, None)),
        check_vma=False,
    )
```

```python
import functools

import jax
import jax.numpy as jnp
from jax import lax
from jax.experimental import pallas as pl
from jax.experimental.pallas import tpu as pltpu
from jax.sharding import PartitionSpec as P

MESH = pl.DeviceIdType.MESH
BF = jnp.bfloat16
F32 = jnp.float32
NN = (((1,), (0,)), ((), ()))
NT = (((1,), (1,)), ((), ()))
TN = (((0,), (0,)), ((), ()))
ROWS = 34 * 32
C0 = 0.7978845608028654
C1 = 0.044715


def mm(a, b, dims=NN):
    return lax.dot_general(a, b, dims, preferred_element_type=F32)


def iota(shape, dim):
    return lax.broadcasted_iota(jnp.int32, shape, dim)


def one_hot(cond):
    return jnp.where(cond, 1.0, 0.0).astype(BF)


def kernel(
    sizes,
    h_fin,
    h_fcot,
    h_w1,
    h_w2,
    h_cin,
    h_ccot,
    h_wc,
    o_gfi,
    o_gf,
    o_gs,
    o_gci,
    o_gc,
    fin,
    fcot,
    w1,
    w2,
    cin,
    ccot,
    wc,
    perm,
    shifts,
    xin,
    xcot,
    xdp,
    act,
    bands,
    ysend,
    yrecv,
    zsend,
    zrecv,
    drecv,
    ycs,
    ycr,
    zcs,
    zcr,
    dcs,
    dcr,
    ysend2,
    yrecv2,
    zsend2,
    zrecv2,
    drecv2,
    cflat,
    cplus,
    cminus,
    vmat,
    inp3,
    rsend,
    rpair,
    psum,
    rs1,
    qf,
    qb,
    rs2,
    g_gci,
    g_gfi,
    g_gf,
    g_gs,
    t_gf,
    t_gs,
    g_gc,
    acc1,
    acc2,
    fpart,
    ar1,
    fsum1,
    ar2,
    fsum2,
    gath,
    ls,
    hs,
    hr,
    cs,
    cr,
    ps,
    pr,
    gs,
    gr,
    r1s,
    r1r,
    r2s,
    r2r,
    a1s,
    a1r,
    a2s,
    a2r,
    a3s,
    a3r,
    ws,
):
    ndp, nty, ntz = sizes
    dp, ty, tz = lax.axis_index("dp"), lax.axis_index("ty"), lax.axis_index("tz")
    zgroup = ndp * ntz
    me = dp * ntz + tz

    def at(dy, dz):
        return (dp, lax.rem(ty + dy + nty, nty), lax.rem(tz + dz + ntz, ntz))

    def ty_peer(j):
        t = lax.rem(ty + j, nty)
        return t, (dp, t, tz)

    def z_peer(j):
        g = lax.rem(me + j, zgroup)
        z = lax.rem(g, ntz)
        return g, z, (lax.div(g, ntz), ty, z)

    def remote(src, dst, ssem, rsem, dev):
        return pltpu.make_async_remote_copy(
            src_ref=src,
            dst_ref=dst,
            send_sem=ssem,
            recv_sem=rsem,
            device_id=dev,
            device_id_type=MESH,
        )

    def arrived(buf, count, ssem, rsem):
        part = buf.at[pl.ds(0, count)]
        for sem in (ssem, rsem):
            pltpu.make_async_copy(part, part, sem).wait()

    up = (ty > 0, ty < nty - 1)
    side = (tz > 0, tz < ntz - 1)

    barrier = pltpu.get_barrier_semaphore()
    partners = [at(dy, dz) for dy in (-1, 1) for dz in (-1, 1)]
    partners += [ty_peer(j)[1] for j in range(1, nty)]
    partners += [z_peer(j)[2] for j in range(1, zgroup)]
    for dev in partners:
        pl.semaphore_signal(barrier, inc=1, device_id=dev, device_id_type=MESH)

    loads = []
    pairs = ((h_ccot, ccot), (h_fin, fin), (h_fcot, fcot), (h_w1, w1), (h_w2, w2), (h_cin, cin), (h_wc, wc))
    for n, (src, dst) in enumerate(pairs):
        loads.append(pltpu.make_async_copy(src, dst, ls.at[n]))
        loads[n].start()

    r, c = iota((512, 512), 0), iota((512, 512), 1)
    perm[...] = one_hot(c == (r % 16) * 32 + ((r // 16) % 2) * 16 + r // 32)
    r, c = iota((128, 256), 0), iota((128, 256), 1)
    shifts[...] = one_hot(((r == c + 1) & (c < 127)) | ((r + 1 == c - 128) & (c > 128)))

    def relayout(src, dst):
        for j in range(2):
            left = src[:, 16 * j : 16 * j + 16, :].reshape(512, 128)
            right = src[:, 32 + 16 * j : 48 + 16 * j, :].reshape(512, 128)
            both = jnp.concatenate([left, right], 1)
            dst[0, 32 + 512 * j : 544 + 512 * j, :] = mm(perm[...], both).astype(BF)

    def extract(src):
        r, c = iota((32, 256), 0), iota((32, 256), 1)
        total = None
        for j in range(8):
            sel = one_hot((r % 16 == 8 * (c // 128) + j) & (c % 128 == 127 * (r // 16)))
            part = mm(sel, src[0, 32 + 128 * j : 160 + 128 * j, :], NT)
            total = part if total is None else total + part
        return total.astype(BF)

    loads[1].wait()
    relayout(fin, xin)
    loads[2].wait()
    relayout(fcot, xcot)
    for n, src in enumerate((xin, xcot)):
        columns = extract(src)
        for t in range(2):
            tile = columns[16 * t : 16 * t + 16, :]
            zsend[t, 16 * n : 16 * n + 16, :] = tile

    loads[0].wait()
    for x in range(16):
        cflat[80 * x + 8 : 80 * x + 72, :] = ccot[64 * x : 64 * x + 64, :].astype(F32)

    def column(y, z):
        return cflat[pl.ds(8 * y + z, 16, stride=80), :]

    for y in range(8):
        zcs[0, 16 * y : 16 * y + 16, :] = column(y + 1, 0).astype(BF)
        zcs[1, 16 * y : 16 * y + 16, :] = column(y + 1, 7).astype(BF)
    for s in range(2):
        own = (slice(32, 64), slice(0, 128)) if s == 0 else (slice(1024, 1056), slice(128, 256))
        ysend[s, 0:32, :] = xin[(0, *own)]
        ysend[s, 32:64, :] = xcot[(0, *own)]
        first = 8 if s == 0 else 64
        for x in range(0, 16, 2):
            pair = [cflat[80 * (x + q) + first : 80 * (x + q) + first + 8, :] for q in range(2)]
            ycs[s, 8 * x : 8 * x + 16, :] = jnp.concatenate(pair, 0).astype(BF)
        for t in range(2):
            dcs[s, t] = column(1 if s == 0 else 8, 0 if t == 0 else 7).astype(BF)

    pl.semaphore_wait(barrier, len(partners))

    step = (-1, 1)
    halo, halo_c = [], []
    for s in range(2):
        for t in range(2):
            q, dev = 4 + 2 * s + t, at(step[s], step[t])
            halo.append(remote(zsend.at[t], drecv.at[s, t], hs.at[q], hr.at[q], dev))
            halo_c.append(remote(dcs.at[s, t], dcr.at[s, t], cs.at[q], cr.at[q], dev))
        y, z, q = at(step[s], 0), at(0, step[s]), 2 + s
        halo.append(remote(zsend.at[s], zrecv.at[s], hs.at[q], hr.at[q], z))
        halo.append(remote(ysend.at[s], yrecv.at[s], hs.at[s], hr.at[s], y))
        halo_c.append(remote(zcs.at[s], zcr.at[s], cs.at[q], cr.at[q], z))
        halo_c.append(remote(ycs.at[s], ycr.at[s], cs.at[s], cr.at[s], y))
    for copy in halo + halo_c:
        copy.start()

    lane = iota((32, 768), 1)
    q, m = lane // 128, lane % 128
    k = 9 * ((m // 16) % 2 - q % 2 + 1) + 3 * (m // 32) + q // 2
    wanted = (m < 96, iota((32, 768), 0))
    straight = one_hot(wanted[0] & (wanted[1] == k))[:27]
    flipped = one_hot(wanted[0] & (wanted[1] == 26 - k))[:27]
    r, c = iota((256, 768), 0), iota((256, 768), 1)
    to_in, to_out = r % 16 == c % 16, r // 16 == c % 16
    r, c = iota((16, 256), 0), iota((16, 256), 1)
    by_out, by_in = one_hot(c // 16 == r), one_hot(c % 16 == r)
    loads[3].wait()
    loads[4].wait()
    for n, (w, pick, mask, rows) in enumerate(
        (
            (w1, straight, to_in, by_out),
            (w2, flipped, to_out, by_in),
            (w1, flipped, to_out, by_in),
        )
    ):
        wide = jnp.where(mask, mm(w[...], pick), 0.0).astype(BF)
        strips = mm(rows, wide)
        for cc in range(3):
            for xo in range(2):
                first = 128 * (2 * cc + xo)
                strip = strips[:, first : first + 128]
                strip = jnp.concatenate([strip, jnp.zeros_like(strip)], 1)
                for yo in range(4):
                    moved = strip if yo == 0 else pltpu.roll(strip, 32 * yo, 1)
                    first = 32 * yo + 16 * xo
                    bands[n, cc, first : first + 16, :] = moved.astype(BF)

    inp3[...] = jnp.zeros_like(inp3)
    loads[5].wait()
    for a in range(3):
        inp3[64 * (2 - a) : 64 * (2 - a) + 1024, 128 * a : 128 * a + 128] = cin[...]
    vmat[0] = jnp.zeros((64, 1152), BF)
    vmat[17] = jnp.zeros((64, 1152), BF)
    qf[...] = jnp.zeros_like(qf)

    def valid(cond, value):
        return jnp.where(cond, value, jnp.zeros_like(value))

    for copy in halo:
        copy.wait()

    def turned(after, before):
        return jnp.concatenate([after, before], 0).astype(F32).T.astype(BF)

    def fill(dst, get_y, get_d, get_z):
        r, c = iota((32, 256), 0), iota((32, 256), 1)

        def place(row, ok):
            after = (r == row) & (c == 127) & side[1] & ok
            return one_hot(after | ((r == 16 + row) & (c == 128) & side[0] & ok))

        for s in (1, 0):
            ok = up[0] if s == 1 else up[1]
            mid = valid(ok, get_y(s))
            corner = turned(get_d(s, 0), get_d(s, 1))
            corner = corner[96:128] if s == 1 else corner[0:32]
            out = mm(mid, shifts[...]) + mm(corner, place(15 if s == 1 else 0, ok))
            rows, lanes = (slice(0, 32), slice(0, 128)) if s == 1 else (slice(1056, 1088), slice(128, 256))
            dst[0, rows, lanes] = mid
            dst[2, rows, lanes] = out[:, :128].astype(BF)
            dst[1, rows, lanes] = out[:, 128:].astype(BF)
        edge = turned(get_z(0), get_z(1))
        for h in range(2):
            lanes = slice(128 * h, 128 * h + 128)
            for j in range(8):
                rows = slice(32 + 128 * j, 160 + 128 * j)
                out = mm(dst[0, rows, lanes], shifts[...]) + mm(edge, place(8 * h + j, True))
                dst[2, rows, lanes] = out[:, :128].astype(BF)
                dst[1, rows, lanes] = out[:, 128:].astype(BF)
        for v in range(3):
            dst[v, 0:32, 128:256] = dst[v, 1024:1056, 0:128]
            dst[v, 1056:1088, 0:128] = dst[v, 32:64, 128:256]

    def fill_first(n, dst):
        rows, tile = slice(32 * n, 32 * n + 32), slice(16 * n, 16 * n + 16)
        fill(
            dst,
            lambda s: yrecv[s, rows, :],
            lambda s, t: drecv[s, t, tile, :],
            lambda t: zrecv[t, tile, :],
        )

    fill_first(0, xin)
    fill_first(1, xcot)

    version = (1, 0, 2)

    def conv(n, src, g):
        rows = pl.ds(pl.multiple_of(g * 128, 128), 192)
        out = None
        for cc in range(3):
            term = mm(bands[n, cc, :, 0:192], src[version[cc], rows, :])
            out = term if out is None else out + term
        return out

    def forward(g):
        pre = conv(0, xin, g)
        dact = conv(1, xcot, g)
        square = pre * pre
        t = jnp.tanh(C0 * pre * (1.0 + C1 * square))
        half = 0.5 + 0.5 * t
        slope = half + 0.5 * pre * (1.0 - t * t) * (C0 * (1.0 + (3.0 * C1) * square))
        act[pl.ds(pl.multiple_of(g * 128, 128), 128), :] = (pre * half).astype(BF)
        xdp[0, pl.ds(pl.multiple_of(g * 128 + 32, 32), 128), :] = (dact * slope).astype(BF)

    for g in range(8):
        forward(g)

    def groups(ref, lead, first, count):
        return jnp.concatenate(
            [ref[(*lead, slice(128 * g + first, 128 * g + first + count))] for g in range(8)], 1
        )

    own, a_own = groups(xdp, (0,), 32, 128), groups(act, (), 0, 128)
    for cc in range(3):
        acc1[cc, :, 0:192] = mm(own, groups(xin, (version[cc],), 0, 192), NT)
        acc1[cc, :, 192:256] = jnp.zeros((128, 64), F32)
        acc2[cc] = mm(groups(xcot, (version[cc],), 0, 192), a_own, NT)
    for cc in range(3):
        total = None
        for yo in range(4):
            part = acc1[cc, 32 * yo : 32 * yo + 32, :]
            part = part if yo == 0 else pltpu.roll(part, 256 - 32 * yo, 1)
            total = part if total is None else total + part
        fpart[32 * cc : 32 * cc + 32, :] = total[:, 0:128]
    total = jnp.zeros((96, 128), F32)
    lane = iota((96, 128), 1)
    for cc in range(3):
        band = None
        for yo in range(4):
            part = acc2[cc, 32 * yo : 32 * yo + 96, :]
            turn = (32 * cc - 32 * yo) % 128
            part = part if turn == 0 else pltpu.roll(part, turn, 1)
            band = part if band is None else band + part
        total = jnp.where(lane // 32 == cc, band, total)
    fpart[96:192, :] = total

    slab = 192 // nty
    hop_a = []
    for j in range(1, nty):
        t, dev = ty_peer(j)
        src = fpart.at[pl.ds(pl.multiple_of(t * slab, 8), slab), :]
        hop_a.append(remote(src, ar1.at[ty], a1s.at[0], a1r.at[0], dev))
    for copy in hop_a:
        copy.start()
    ar1[ty] = fpart[pl.ds(pl.multiple_of(ty * slab, 8), slab), :]

    columns = extract(xdp)
    zsend2[0] = columns[0:16]
    zsend2[1] = columns[16:32]
    ysend2[0] = xdp[0, 32:64, 0:128]
    ysend2[1] = xdp[0, 1024:1056, 128:256]
    halo2 = []
    for s in range(2):
        halo2.append(remote(ysend2.at[s], yrecv2.at[s], gs.at[s], gr.at[s], at(step[s], 0)))
        halo2.append(remote(zsend2.at[s], zrecv2.at[s], gs.at[2 + s], gr.at[2 + s], at(0, step[s])))
        for t in range(2):
            q = 4 + 2 * s + t
            dev = at(step[s], step[t])
            halo2.append(remote(zsend2.at[t], drecv2.at[s, t], gs.at[q], gr.at[q], dev))
    for copy in halo2:
        copy.start()

    for copy in halo_c:
        copy.wait()
    for x in range(16):
        rows = slice(8 * (x // 2 * 2), 16 + 8 * (x // 2 * 2))
        half = slice(8 * (x % 2), 8 * (x % 2) + 8)
        cflat[80 * x : 80 * x + 8, :] = valid(up[0], ycr[1, rows, :].astype(F32)[half])
        cflat[80 * x + 72 : 80 * x + 80, :] = valid(up[1], ycr[0, rows, :].astype(F32)[half])
    cplus[...] = pltpu.roll(cflat[...], 1279, 0)
    cminus[...] = pltpu.roll(cflat[...], 1, 0)
    for y in range(10):
        for ref, z, t, ok in ((cplus, 7, 0, side[1]), (cminus, 0, 1, side[0])):
            if y == 0:
                part, ok = dcr[1, t], ok & up[0]
            elif y == 9:
                part, ok = dcr[0, t], ok & up[1]
            else:
                part = zcr[t, 16 * (y - 1) : 16 * y, :]
            ref[pl.ds(8 * y + z, 16, stride=80), :] = valid(ok, part.astype(F32))

    def spread(x, carry):
        for b in range(3):
            for cc, ref in enumerate((cplus, cflat, cminus)):
                rows = ref[pl.ds(pl.multiple_of(x * 80 + 8 * (2 - b), 8), 64), :]
                q = 3 * b + cc
                vmat[x + 1, :, 128 * q : 128 * q + 128] = rows.astype(BF)
        return carry

    lax.fori_loop(0, 16, spread, 0)

    wide_o, nx = 128 // nty, nty // 2
    core, xme = lax.rem(ty, 2), lax.div(ty, 2)
    other = (dp, ty + 1 - 2 * core, tz)
    hop0 = []
    g = mm(vmat[...].reshape(1152, 1152), inp3[...], TN)
    for b in range(3):
        for a in range(3):
            for cc in range(3):
                first = 384 * b + 128 * cc
                part = g[first : first + 128, 128 * a : 128 * a + 128]
                rsend[9 * b + 3 * a + cc] = part.astype(BF).reshape(nx, 2, wide_o, 128)
        src = rsend.at[pl.ds(9 * b, 9), :, 1 - core]
        hop0.append(remote(src, rpair.at[pl.ds(9 * b, 9)], ps.at[b], pr.at[b], other))
        hop0[b].start()

    arrived(ar1, nty - 1, a1s.at[0], a1r.at[0])
    total = ar1[0]
    for t in range(1, nty):
        total = total + ar1[t]
    fsum1[...] = total
    hop_b = []
    for j in range(1, zgroup):
        g, z, dev = z_peer(j)
        hop_b.append(remote(fsum1, ar2.at[me], a2s.at[0], a2r.at[0], dev))
    for copy in hop_b:
        copy.start()
    ar2[me] = fsum1[...]

    hop1 = []

    def send_sum(b):
        hop0[b].wait()
        for q in range(9 * b, 9 * b + 9):
            psum[q] = (rsend[q, :, core].astype(F32) + rpair[q].astype(F32)).astype(BF)
        for j in range(1, nx):
            x = lax.rem(xme + j, nx)
            src, dst = psum.at[pl.ds(9 * b, 9), x], rs1.at[xme, pl.ds(9 * b, 9)]
            dev = (dp, 2 * x + core, tz)
            hop1.append(remote(src, dst, r1s.at[0], r1r.at[0], dev))
            hop1[-1].start()

    for b in range(3):
        send_sum(b)

    loads[6].wait()

    out = None
    for a in range(3):
        left = vmat[2 - a : 18 - a].reshape(1024, 1152)
        term = mm(left, wc[1152 * a : 1152 * a + 1152, :])
        out = term if out is None else out + term
    g_gci[...] = out.astype(BF)
    stores = [pltpu.make_async_copy(g_gci, o_gci, ws.at[0])]
    stores[0].start()

    for copy in halo2:
        copy.wait()
    fill(
        xdp,
        lambda s: yrecv2[s],
        lambda s, t: drecv2[s, t],
        lambda t: zrecv2[t],
    )

    arrived(ar2, zgroup - 1, a2s.at[0], a2r.at[0])
    total = ar2[0]
    for t in range(1, zgroup):
        total = total + ar2[t]
    fsum2[...] = total
    hop_c = []
    for j in range(1, nty):
        t, dev = ty_peer(j)
        hop_c.append(remote(fsum2, gath.at[ty], a3s.at[0], a3r.at[0], dev))
    for copy in hop_c:
        copy.start()
    gath[ty] = fsum2[...]

    def last(j, carry):
        parts = [conv(2, xdp, 4 * j + q).astype(BF) for q in range(4)]
        out = mm(perm[...], jnp.concatenate(parts, 0)).astype(BF)
        first = pl.multiple_of(16 * j, 16)
        g_gfi[:, pl.ds(first, 16), :] = out[:, :128].reshape(32, 16, 128)
        g_gfi[:, pl.ds(first + 32, 16), :] = out[:, 128:].reshape(32, 16, 128)
        return carry

    lax.fori_loop(0, 2, last, 0)
    stores.append(pltpu.make_async_copy(g_gfi, o_gfi, ws.at[1]))
    stores[1].start()

    rs1[xme] = psum[:, xme]
    arrived(rs1, nx - 1, r1s.at[0], r1r.at[0])

    def sum1(q, carry):
        total = rs1[0, q].astype(F32)
        for t in range(1, nx):
            total = total + rs1[t, q].astype(F32)
        k = 9 * (lax.div(q, 3) % 3) + 3 * lax.div(q, 9) + q % 3
        qf[pl.ds(k, wide_o, stride=32), :] = total
        return carry

    lax.fori_loop(0, 27, sum1, 0)
    qb[...] = qf[...].astype(BF)
    deep = 32 * wide_o // ntz

    hop2 = []
    for j in range(1, zgroup):
        g, z, dev = z_peer(j)
        src = qb.at[pl.ds(pl.multiple_of(z * deep, 16), deep), :]
        hop2.append(remote(src, rs2.at[me], r2s.at[0], r2r.at[0], dev))
    for copy in hop2:
        copy.start()
    rs2[me] = qb[pl.ds(pl.multiple_of(tz * deep, 16), deep), :]

    arrived(gath, nty - 1, a3s.at[0], a3r.at[0])
    fpart[...] = gath[...].reshape(192, 128)
    for a in range(3):
        planes = [(xo, xo + a - 1) for xo in range(2) if 0 <= xo + a - 1 < 2]
        for b in range(3):
            for cc in range(3):
                k = 9 * a + 3 * b + cc
                one, two = None, None
                for xo, xi in planes:
                    first = 32 * cc + 16 * xo
                    lanes = slice(32 * b + 16 * xi, 32 * b + 16 * xi + 16)
                    part = fpart[first : first + 16, lanes]
                    one = part if one is None else one + part
                    first = 96 + 32 * b + 16 * xi
                    lanes = slice(32 * cc + 16 * xo, 32 * cc + 16 * xo + 16)
                    part = fpart[first : first + 16, lanes]
                    two = part if two is None else two + part
                g_gf[k] = one
                g_gs[26 - k] = two
    for n, (src, mid, dst) in enumerate(((g_gf, t_gf, o_gf), (g_gs, t_gs, o_gs))):
        for o in range(16):
            mid[o] = src[:, o, :].T
        stores.append(pltpu.make_async_copy(mid, dst, ws.at[2 + n]))
        stores[2 + n].start()

    arrived(rs2, zgroup - 1, r2s.at[0], r2r.at[0])
    total = rs2[0].astype(F32)
    for t in range(1, zgroup):
        total = total + rs2[t].astype(F32)
    for o in range(wide_o // ntz):
        g_gc[:, o, :] = total[32 * o : 32 * o + 27, :]
    stores.append(pltpu.make_async_copy(g_gc, o_gc, ws.at[4]))
    stores[4].start()
    for copy in stores:
        copy.wait()


def finish(*refs):
    srcs, dsts, mids, sems = refs[:5], refs[5:10], refs[10:15], refs[15]
    pieces = [(0, pl.ds(8 * q, 8)) for q in range(4)] + [(3, pl.ds(512 * q, 512)) for q in range(2)]
    pieces += [(n, pl.ds(0, srcs[n].shape[0])) for n in (1, 2, 4)]
    into, out = [], []
    for q, (n, rows) in enumerate(pieces):
        into.append(pltpu.make_async_copy(srcs[n].at[rows], mids[n].at[rows], sems.at[0, q]))
        out.append(pltpu.make_async_copy(mids[n].at[rows], dsts[n].at[rows], sems.at[1, q]))
        into[q].start()
    for q in range(len(pieces)):
        into[q].wait()
        out[q].start()
    for copy in out:
        copy.wait()


def solution(mesh):
    sizes = tuple(mesh.shape[a] for a in ("dp", "ty", "tz"))
    ndp, nty, ntz = sizes
    zgroup = ndp * ntz
    wide_o, nx = 128 // nty, nty // 2
    slab = 192 // nty

    def per_device(fine_input, fine_cotangent, first_weight, second_weight, coarse_input, coarse_cotangent, coarse_weight):
        def by_offset(w):
            return w.transpose(1, 2, 0).reshape(256, 27)

        dma = pltpu.SemaphoreType.DMA
        scratch = [
            pltpu.VMEM((32, 64, 128), BF),
            pltpu.VMEM((32, 64, 128), BF),
            pltpu.VMEM((256, 27), BF),
            pltpu.VMEM((256, 27), BF),
            pltpu.VMEM((1024, 128), BF),
            pltpu.VMEM((1024, 128), BF),
            pltpu.VMEM((3456, 128), BF),
            pltpu.VMEM((512, 512), BF),
            pltpu.VMEM((128, 256), BF),
            pltpu.VMEM((3, ROWS, 256), BF),
            pltpu.VMEM((3, ROWS, 256), BF),
            pltpu.VMEM((3, ROWS, 256), BF),
            pltpu.VMEM((1024, 256), BF),
            pltpu.VMEM((3, 3, 128, 256), BF),
            pltpu.VMEM((2, 64, 128), BF),
            pltpu.VMEM((2, 64, 128), BF),
            pltpu.VMEM((2, 32, 128), BF),
            pltpu.VMEM((2, 32, 128), BF),
            pltpu.VMEM((2, 2, 32, 128), BF),
            pltpu.VMEM((2, 128, 128), BF),
            pltpu.VMEM((2, 128, 128), BF),
            pltpu.VMEM((2, 128, 128), BF),
            pltpu.VMEM((2, 128, 128), BF),
            pltpu.VMEM((2, 2, 16, 128), BF),
            pltpu.VMEM((2, 2, 16, 128), BF),
            pltpu.VMEM((2, 32, 128), BF),
            pltpu.VMEM((2, 32, 128), BF),
            pltpu.VMEM((2, 16, 128), BF),
            pltpu.VMEM((2, 16, 128), BF),
            pltpu.VMEM((2, 2, 16, 128), BF),
            pltpu.VMEM((1280, 128), F32),
            pltpu.VMEM((1280, 128), F32),
            pltpu.VMEM((1280, 128), F32),
            pltpu.VMEM((18, 64, 1152), BF),
            pltpu.VMEM((1152, 384), BF),
            pltpu.VMEM((27, nx, 2, wide_o, 128), BF),
            pltpu.VMEM((27, nx, wide_o, 128), BF),
            pltpu.VMEM((27, nx, wide_o, 128), BF),
            pltpu.VMEM((nx, 27, wide_o, 128), BF),
            pltpu.VMEM((32 * wide_o, 128), F32),
            pltpu.VMEM((32 * wide_o, 128), BF),
            pltpu.VMEM((zgroup, 32 * wide_o // ntz, 128), BF),
            pltpu.VMEM((1024, 128), BF),
            pltpu.VMEM((32, 64, 128), BF),
            pltpu.VMEM((27, 16, 16), F32),
            pltpu.VMEM((27, 16, 16), F32),
            pltpu.VMEM((16, 16, 27), F32),
            pltpu.VMEM((16, 16, 27), F32),
            pltpu.VMEM((27, wide_o // ntz, 128), F32),
            pltpu.VMEM((3, 128, 256), F32),
            pltpu.VMEM((3, 192, 128), F32),
            pltpu.VMEM((192, 128), F32),
            pltpu.VMEM((nty, slab, 128), F32),
            pltpu.VMEM((slab, 128), F32),
            pltpu.VMEM((zgroup, slab, 128), F32),
            pltpu.VMEM((slab, 128), F32),
            pltpu.VMEM((nty, slab, 128), F32),
            dma((7,)),
            dma((8,)),
            dma((8,)),
            dma((8,)),
            dma((8,)),
            dma((3,)),
            dma((3,)),
            dma((8,)),
            dma((8,)),
            dma((1,)),
            dma((1,)),
            dma((1,)),
            dma((1,)),
            dma((1,)),
            dma((1,)),
            dma((1,)),
            dma((1,)),
            dma((1,)),
            dma((1,)),
            dma((5,)),
        ]
        outs = pl.pallas_call(
            functools.partial(kernel, sizes),
            out_shape=(
                jax.ShapeDtypeStruct((32, 64, 128), BF),
                jax.ShapeDtypeStruct((16, 16, 27), F32),
                jax.ShapeDtypeStruct((16, 16, 27), F32),
                jax.ShapeDtypeStruct((1024, 128), BF),
                jax.ShapeDtypeStruct((27, wide_o // ntz, 128), F32),
            ),
            in_specs=[pl.BlockSpec(memory_space=pl.ANY)] * 7,
            out_specs=(pl.BlockSpec(memory_space=pl.ANY),) * 5,
            scratch_shapes=scratch,
            compiler_params=pltpu.CompilerParams(
                collective_id=0, has_side_effects=True, vmem_limit_bytes=60 * 1024 * 1024
            ),
        )(
            fine_input.reshape(32, 64, 128),
            fine_cotangent.reshape(32, 64, 128),
            by_offset(first_weight),
            by_offset(second_weight),
            coarse_input.reshape(1024, 128),
            coarse_cotangent.reshape(1024, 128),
            coarse_weight.reshape(3456, 128),
        )
        far = pl.BlockSpec(memory_space=pl.ANY)
        outs = pl.pallas_call(
            finish,
            out_shape=(
                jax.ShapeDtypeStruct((32, 64, 128), BF),
                jax.ShapeDtypeStruct((16, 16, 27), F32),
                jax.ShapeDtypeStruct((16, 16, 27), F32),
                jax.ShapeDtypeStruct((1024, 128), BF),
                jax.ShapeDtypeStruct((27, wide_o // ntz, 128), F32),
            ),
            in_specs=[far] * 5,
            out_specs=(far,) * 5,
            scratch_shapes=[
                pltpu.VMEM((32, 64, 128), BF),
                pltpu.VMEM((16, 16, 27), F32),
                pltpu.VMEM((16, 16, 27), F32),
                pltpu.VMEM((1024, 128), BF),
                pltpu.VMEM((27, wide_o // ntz, 128), F32),
                dma((2, 9)),
            ],
            compiler_params=pltpu.CompilerParams(vmem_limit_bytes=60 * 1024 * 1024),
        )(*outs)
        return (
            outs[0].reshape(fine_input.shape),
            outs[1].transpose(2, 0, 1),
            outs[2].transpose(2, 0, 1),
            outs[3].reshape(coarse_input.shape),
            outs[4].transpose(1, 0, 2),
        )

    fine = P("dp", None, None, "ty", "tz")
    wide = P("dp", None, "ty", "tz", None)
    return jax.shard_map(
        per_device,
        mesh=mesh,
        in_specs=(fine, fine, P(), P(), wide, wide, P()),
        out_specs=(fine, P(), P(), wide, P(("ty", "tz"), None, None)),
        check_vma=False,
    )
```

```python
import functools

import jax
import jax.numpy as jnp
from jax import lax
from jax.experimental import pallas as pl
from jax.experimental.pallas import tpu as pltpu
from jax.sharding import PartitionSpec as P

MESH = pl.DeviceIdType.MESH
BF = jnp.bfloat16
F32 = jnp.float32
NN = (((1,), (0,)), ((), ()))
NT = (((1,), (1,)), ((), ()))
TN = (((0,), (0,)), ((), ()))
ROWS = 34 * 32
C0 = 0.7978845608028654
C1 = 0.044715


def mm(a, b, dims=NN):
    return lax.dot_general(a, b, dims, preferred_element_type=F32)


def iota(shape, dim):
    return lax.broadcasted_iota(jnp.int32, shape, dim)


def one_hot(cond):
    return jnp.where(cond, 1.0, 0.0).astype(BF)


def kernel(
    sizes,
    h_fin,
    h_fcot,
    h_w1,
    h_w2,
    h_cin,
    h_ccot,
    h_wc,
    o_gfi,
    o_gf,
    o_gs,
    o_gci,
    o_gc,
    fin,
    fcot,
    w1,
    w2,
    cin,
    ccot,
    wc,
    perm,
    shifts,
    xin,
    xcot,
    xdp,
    act,
    bands,
    ysend,
    yrecv,
    zsend,
    zrecv,
    drecv,
    ycs,
    ycr,
    zcs,
    zcr,
    dcs,
    dcr,
    ysend2,
    yrecv2,
    zsend2,
    zrecv2,
    drecv2,
    cflat,
    cplus,
    cminus,
    vmat,
    inp3,
    rsend,
    rpair,
    psum,
    rs1,
    qf,
    qb,
    rs2,
    g_gci,
    g_gfi,
    g_gf,
    g_gs,
    t_gf,
    t_gs,
    g_gc,
    acc1,
    acc2,
    fpart,
    ar1,
    fsum1,
    ar2,
    fsum2,
    gath,
    ls,
    hs,
    hr,
    cs,
    cr,
    ps,
    pr,
    gs,
    gr,
    r1s,
    r1r,
    r2s,
    r2r,
    a1s,
    a1r,
    a2s,
    a2r,
    a3s,
    a3r,
    ws,
):
    ndp, nty, ntz = sizes
    dp, ty, tz = lax.axis_index("dp"), lax.axis_index("ty"), lax.axis_index("tz")
    zgroup = ndp * ntz
    me = dp * ntz + tz

    def at(dy, dz):
        return (dp, lax.rem(ty + dy + nty, nty), lax.rem(tz + dz + ntz, ntz))

    def ty_peer(j):
        t = lax.rem(ty + j, nty)
        return t, (dp, t, tz)

    def z_peer(j):
        g = lax.rem(me + j, zgroup)
        z = lax.rem(g, ntz)
        return g, z, (lax.div(g, ntz), ty, z)

    def remote(src, dst, ssem, rsem, dev):
        return pltpu.make_async_remote_copy(
            src_ref=src,
            dst_ref=dst,
            send_sem=ssem,
            recv_sem=rsem,
            device_id=dev,
            device_id_type=MESH,
        )

    def arrived(buf, count, ssem, rsem):
        part = buf.at[pl.ds(0, count)]
        for sem in (ssem, rsem):
            pltpu.make_async_copy(part, part, sem).wait()

    up = (ty > 0, ty < nty - 1)
    side = (tz > 0, tz < ntz - 1)

    barrier = pltpu.get_barrier_semaphore()
    partners = [at(dy, dz) for dy in (-1, 1) for dz in (-1, 1)]
    partners += [ty_peer(j)[1] for j in range(1, nty)]
    partners += [z_peer(j)[2] for j in range(1, zgroup)]
    for dev in partners:
        pl.semaphore_signal(barrier, inc=1, device_id=dev, device_id_type=MESH)

    loads = []
    pairs = ((h_ccot, ccot), (h_fin, fin), (h_fcot, fcot), (h_w1, w1), (h_w2, w2), (h_cin, cin), (h_wc, wc))
    for n, (src, dst) in enumerate(pairs):
        loads.append(pltpu.make_async_copy(src, dst, ls.at[n]))
        loads[n].start()

    r, c = iota((512, 512), 0), iota((512, 512), 1)
    perm[...] = one_hot(c == (r % 16) * 32 + ((r // 16) % 2) * 16 + r // 32)
    r, c = iota((128, 256), 0), iota((128, 256), 1)
    shifts[...] = one_hot(((r == c + 1) & (c < 127)) | ((r + 1 == c - 128) & (c > 128)))

    def relayout(src, dst):
        for j in range(2):
            left = src[:, 16 * j : 16 * j + 16, :].reshape(512, 128)
            right = src[:, 32 + 16 * j : 48 + 16 * j, :].reshape(512, 128)
            both = jnp.concatenate([left, right], 1)
            dst[0, 32 + 512 * j : 544 + 512 * j, :] = mm(perm[...], both).astype(BF)

    def extract(src):
        r, c = iota((32, 256), 0), iota((32, 256), 1)
        total = None
        for j in range(8):
            sel = one_hot((r % 16 == 8 * (c // 128) + j) & (c % 128 == 127 * (r // 16)))
            part = mm(sel, src[0, 32 + 128 * j : 160 + 128 * j, :], NT)
            total = part if total is None else total + part
        return total.astype(BF)

    loads[1].wait()
    relayout(fin, xin)
    loads[2].wait()
    relayout(fcot, xcot)
    for n, src in enumerate((xin, xcot)):
        columns = extract(src)
        for t in range(2):
            tile = columns[16 * t : 16 * t + 16, :]
            zsend[t, 16 * n : 16 * n + 16, :] = tile

    loads[0].wait()
    for x in range(16):
        cflat[80 * x + 8 : 80 * x + 72, :] = ccot[64 * x : 64 * x + 64, :].astype(F32)

    def column(y, z):
        return cflat[pl.ds(8 * y + z, 16, stride=80), :]

    for y in range(8):
        zcs[0, 16 * y : 16 * y + 16, :] = column(y + 1, 0).astype(BF)
        zcs[1, 16 * y : 16 * y + 16, :] = column(y + 1, 7).astype(BF)
    for s in range(2):
        own = (slice(32, 64), slice(0, 128)) if s == 0 else (slice(1024, 1056), slice(128, 256))
        ysend[s, 0:32, :] = xin[(0, *own)]
        ysend[s, 32:64, :] = xcot[(0, *own)]
        first = 8 if s == 0 else 64
        for x in range(0, 16, 2):
            pair = [cflat[80 * (x + q) + first : 80 * (x + q) + first + 8, :] for q in range(2)]
            ycs[s, 8 * x : 8 * x + 16, :] = jnp.concatenate(pair, 0).astype(BF)
        for t in range(2):
            dcs[s, t] = column(1 if s == 0 else 8, 0 if t == 0 else 7).astype(BF)

    pl.semaphore_wait(barrier, len(partners))

    step = (-1, 1)
    halo, halo_c = [], []
    for s in range(2):
        for t in range(2):
            q, dev = 4 + 2 * s + t, at(step[s], step[t])
            halo.append(remote(zsend.at[t], drecv.at[s, t], hs.at[q], hr.at[q], dev))
            halo_c.append(remote(dcs.at[s, t], dcr.at[s, t], cs.at[q], cr.at[q], dev))
        y, z, q = at(step[s], 0), at(0, step[s]), 2 + s
        halo.append(remote(zsend.at[s], zrecv.at[s], hs.at[q], hr.at[q], z))
        halo.append(remote(ysend.at[s], yrecv.at[s], hs.at[s], hr.at[s], y))
        halo_c.append(remote(zcs.at[s], zcr.at[s], cs.at[q], cr.at[q], z))
        halo_c.append(remote(ycs.at[s], ycr.at[s], cs.at[s], cr.at[s], y))
    for copy in halo + halo_c:
        copy.start()

    lane = iota((32, 768), 1)
    q, m = lane // 128, lane % 128
    k = 9 * ((m // 16) % 2 - q % 2 + 1) + 3 * (m // 32) + q // 2
    wanted = (m < 96, iota((32, 768), 0))
    straight = one_hot(wanted[0] & (wanted[1] == k))[:27]
    flipped = one_hot(wanted[0] & (wanted[1] == 26 - k))[:27]
    r, c = iota((256, 768), 0), iota((256, 768), 1)
    to_in, to_out = r % 16 == c % 16, r // 16 == c % 16
    r, c = iota((16, 256), 0), iota((16, 256), 1)
    by_out, by_in = one_hot(c // 16 == r), one_hot(c % 16 == r)
    loads[3].wait()
    loads[4].wait()
    for n, (w, pick, mask, rows) in enumerate(
        (
            (w1, straight, to_in, by_out),
            (w2, flipped, to_out, by_in),
            (w1, flipped, to_out, by_in),
        )
    ):
        wide = jnp.where(mask, mm(w[...], pick), 0.0).astype(BF)
        strips = mm(rows, wide)
        for cc in range(3):
            for xo in range(2):
                first = 128 * (2 * cc + xo)
                strip = strips[:, first : first + 128]
                strip = jnp.concatenate([strip, jnp.zeros_like(strip)], 1)
                for yo in range(4):
                    moved = strip if yo == 0 else pltpu.roll(strip, 32 * yo, 1)
                    first = 32 * yo + 16 * xo
                    bands[n, cc, first : first + 16, :] = moved.astype(BF)

    inp3[...] = jnp.zeros_like(inp3)
    loads[5].wait()
    for a in range(3):
        inp3[64 * (2 - a) : 64 * (2 - a) + 1024, 128 * a : 128 * a + 128] = cin[...]
    vmat[0] = jnp.zeros((64, 1152), BF)
    vmat[17] = jnp.zeros((64, 1152), BF)
    qf[...] = jnp.zeros_like(qf)

    def valid(cond, value):
        return jnp.where(cond, value, jnp.zeros_like(value))

    for copy in halo:
        copy.wait()

    def turned(after, before):
        return jnp.concatenate([after, before], 0).astype(F32).T.astype(BF)

    def fill(dst, get_y, get_d, get_z):
        r, c = iota((32, 256), 0), iota((32, 256), 1)

        def place(row, ok):
            after = (r == row) & (c == 127) & side[1] & ok
            return one_hot(after | ((r == 16 + row) & (c == 128) & side[0] & ok))

        for s in (1, 0):
            ok = up[0] if s == 1 else up[1]
            mid = valid(ok, get_y(s))
            corner = turned(get_d(s, 0), get_d(s, 1))
            corner = corner[96:128] if s == 1 else corner[0:32]
            out = mm(mid, shifts[...]) + mm(corner, place(15 if s == 1 else 0, ok))
            rows, lanes = (slice(0, 32), slice(0, 128)) if s == 1 else (slice(1056, 1088), slice(128, 256))
            dst[0, rows, lanes] = mid
            dst[2, rows, lanes] = out[:, :128].astype(BF)
            dst[1, rows, lanes] = out[:, 128:].astype(BF)
        edge = turned(get_z(0), get_z(1))
        for h in range(2):
            lanes = slice(128 * h, 128 * h + 128)
            for j in range(8):
                rows = slice(32 + 128 * j, 160 + 128 * j)
                out = mm(dst[0, rows, lanes], shifts[...]) + mm(edge, place(8 * h + j, True))
                dst[2, rows, lanes] = out[:, :128].astype(BF)
                dst[1, rows, lanes] = out[:, 128:].astype(BF)
        for v in range(3):
            dst[v, 0:32, 128:256] = dst[v, 1024:1056, 0:128]
            dst[v, 1056:1088, 0:128] = dst[v, 32:64, 128:256]

    def fill_first(n, dst):
        rows, tile = slice(32 * n, 32 * n + 32), slice(16 * n, 16 * n + 16)
        fill(
            dst,
            lambda s: yrecv[s, rows, :],
            lambda s, t: drecv[s, t, tile, :],
            lambda t: zrecv[t, tile, :],
        )

    fill_first(0, xin)
    fill_first(1, xcot)

    version = (1, 0, 2)

    def conv(n, src, g):
        rows = pl.ds(pl.multiple_of(g * 128, 128), 192)
        out = None
        for cc in range(3):
            term = mm(bands[n, cc, :, 0:192], src[version[cc], rows, :])
            out = term if out is None else out + term
        return out

    def forward(g):
        pre = conv(0, xin, g)
        dact = conv(1, xcot, g)
        square = pre * pre
        t = jnp.tanh(C0 * pre * (1.0 + C1 * square))
        half = 0.5 + 0.5 * t
        slope = half + 0.5 * pre * (1.0 - t * t) * (C0 * (1.0 + (3.0 * C1) * square))
        act[pl.ds(pl.multiple_of(g * 128, 128), 128), :] = (pre * half).astype(BF)
        xdp[0, pl.ds(pl.multiple_of(g * 128 + 32, 32), 128), :] = (dact * slope).astype(BF)

    for g in range(8):
        forward(g)

    def groups(ref, lead, first, count):
        return jnp.concatenate(
            [ref[(*lead, slice(128 * g + first, 128 * g + first + count))] for g in range(8)], 1
        )

    own, a_own = groups(xdp, (0,), 32, 128), groups(act, (), 0, 128)
    for cc in range(3):
        acc1[cc, :, 0:192] = mm(own, groups(xin, (version[cc],), 0, 192), NT)
        acc1[cc, :, 192:256] = jnp.zeros((128, 64), F32)
        acc2[cc] = mm(groups(xcot, (version[cc],), 0, 192), a_own, NT)
    for cc in range(3):
        total = None
        for yo in range(4):
            part = acc1[cc, 32 * yo : 32 * yo + 32, :]
            part = part if yo == 0 else pltpu.roll(part, 256 - 32 * yo, 1)
            total = part if total is None else total + part
        fpart[32 * cc : 32 * cc + 32, :] = total[:, 0:128]
    total = jnp.zeros((96, 128), F32)
    lane = iota((96, 128), 1)
    for cc in range(3):
        band = None
        for yo in range(4):
            part = acc2[cc, 32 * yo : 32 * yo + 96, :]
            turn = (32 * cc - 32 * yo) % 128
            part = part if turn == 0 else pltpu.roll(part, turn, 1)
            band = part if band is None else band + part
        total = jnp.where(lane // 32 == cc, band, total)
    fpart[96:192, :] = total

    slab = 192 // nty
    hop_a = []
    for j in range(1, nty):
        t, dev = ty_peer(j)
        src = fpart.at[pl.ds(pl.multiple_of(t * slab, 8), slab), :]
        hop_a.append(remote(src, ar1.at[ty], a1s.at[0], a1r.at[0], dev))
    for copy in hop_a:
        copy.start()
    ar1[ty] = fpart[pl.ds(pl.multiple_of(ty * slab, 8), slab), :]

    columns = extract(xdp)
    zsend2[0] = columns[0:16]
    zsend2[1] = columns[16:32]
    ysend2[0] = xdp[0, 32:64, 0:128]
    ysend2[1] = xdp[0, 1024:1056, 128:256]
    halo2 = []
    for s in range(2):
        halo2.append(remote(ysend2.at[s], yrecv2.at[s], gs.at[s], gr.at[s], at(step[s], 0)))
        halo2.append(remote(zsend2.at[s], zrecv2.at[s], gs.at[2 + s], gr.at[2 + s], at(0, step[s])))
        for t in range(2):
            q = 4 + 2 * s + t
            dev = at(step[s], step[t])
            halo2.append(remote(zsend2.at[t], drecv2.at[s, t], gs.at[q], gr.at[q], dev))
    for copy in halo2:
        copy.start()

    for copy in halo_c:
        copy.wait()
    for x in range(16):
        rows = slice(8 * (x // 2 * 2), 16 + 8 * (x // 2 * 2))
        half = slice(8 * (x % 2), 8 * (x % 2) + 8)
        cflat[80 * x : 80 * x + 8, :] = valid(up[0], ycr[1, rows, :].astype(F32)[half])
        cflat[80 * x + 72 : 80 * x + 80, :] = valid(up[1], ycr[0, rows, :].astype(F32)[half])
    cplus[...] = pltpu.roll(cflat[...], 1279, 0)
    cminus[...] = pltpu.roll(cflat[...], 1, 0)
    for y in range(10):
        for ref, z, t, ok in ((cplus, 7, 0, side[1]), (cminus, 0, 1, side[0])):
            if y == 0:
                part, ok = dcr[1, t], ok & up[0]
            elif y == 9:
                part, ok = dcr[0, t], ok & up[1]
            else:
                part = zcr[t, 16 * (y - 1) : 16 * y, :]
            ref[pl.ds(8 * y + z, 16, stride=80), :] = valid(ok, part.astype(F32))

    def spread(x, carry):
        for b in range(3):
            for cc, ref in enumerate((cplus, cflat, cminus)):
                rows = ref[pl.ds(pl.multiple_of(x * 80 + 8 * (2 - b), 8), 64), :]
                q = 3 * b + cc
                vmat[x + 1, :, 128 * q : 128 * q + 128] = rows.astype(BF)
        return carry

    lax.fori_loop(0, 16, spread, 0)

    wide_o, nx = 128 // nty, nty // 2
    core, xme = lax.rem(ty, 2), lax.div(ty, 2)
    other = (dp, ty + 1 - 2 * core, tz)
    hop0 = []
    for b in range(3):
        left = vmat[:, :, 384 * b : 384 * b + 384].reshape(1152, 384)
        g = mm(left, inp3[...], TN)
        for a in range(3):
            for cc in range(3):
                first = 128 * cc
                part = g[first : first + 128, 128 * a : 128 * a + 128]
                rsend[9 * b + 3 * a + cc] = part.astype(BF).reshape(nx, 2, wide_o, 128)
        src = rsend.at[pl.ds(9 * b, 9), :, 1 - core]
        hop0.append(remote(src, rpair.at[pl.ds(9 * b, 9)], ps.at[b], pr.at[b], other))
        hop0[b].start()

    arrived(ar1, nty - 1, a1s.at[0], a1r.at[0])
    total = ar1[0]
    for t in range(1, nty):
        total = total + ar1[t]
    fsum1[...] = total
    hop_b = []
    for j in range(1, zgroup):
        g, z, dev = z_peer(j)
        hop_b.append(remote(fsum1, ar2.at[me], a2s.at[0], a2r.at[0], dev))
    for copy in hop_b:
        copy.start()
    ar2[me] = fsum1[...]

    hop1 = []

    def send_sum(b):
        hop0[b].wait()
        for q in range(9 * b, 9 * b + 9):
            psum[q] = (rsend[q, :, core].astype(F32) + rpair[q].astype(F32)).astype(BF)
        for j in range(1, nx):
            x = lax.rem(xme + j, nx)
            src, dst = psum.at[pl.ds(9 * b, 9), x], rs1.at[xme, pl.ds(9 * b, 9)]
            dev = (dp, 2 * x + core, tz)
            hop1.append(remote(src, dst, r1s.at[0], r1r.at[0], dev))
            hop1[-1].start()

    for b in range(3):
        send_sum(b)

    loads[6].wait()

    out = None
    for a in range(3):
        left = vmat[2 - a : 18 - a].reshape(1024, 1152)
        term = mm(left, wc[1152 * a : 1152 * a + 1152, :])
        out = term if out is None else out + term
    g_gci[...] = out.astype(BF)
    stores = [pltpu.make_async_copy(g_gci, o_gci, ws.at[0])]
    stores[0].start()

    for copy in halo2:
        copy.wait()
    fill(
        xdp,
        lambda s: yrecv2[s],
        lambda s, t: drecv2[s, t],
        lambda t: zrecv2[t],
    )

    arrived(ar2, zgroup - 1, a2s.at[0], a2r.at[0])
    total = ar2[0]
    for t in range(1, zgroup):
        total = total + ar2[t]
    fsum2[...] = total
    hop_c = []
    for j in range(1, nty):
        t, dev = ty_peer(j)
        hop_c.append(remote(fsum2, gath.at[ty], a3s.at[0], a3r.at[0], dev))
    for copy in hop_c:
        copy.start()
    gath[ty] = fsum2[...]

    def last(j, carry):
        parts = [conv(2, xdp, 4 * j + q).astype(BF) for q in range(4)]
        out = mm(perm[...], jnp.concatenate(parts, 0)).astype(BF)
        first = pl.multiple_of(16 * j, 16)
        g_gfi[:, pl.ds(first, 16), :] = out[:, :128].reshape(32, 16, 128)
        g_gfi[:, pl.ds(first + 32, 16), :] = out[:, 128:].reshape(32, 16, 128)
        return carry

    lax.fori_loop(0, 2, last, 0)
    stores.append(pltpu.make_async_copy(g_gfi, o_gfi, ws.at[1]))
    stores[1].start()

    rs1[xme] = psum[:, xme]
    arrived(rs1, nx - 1, r1s.at[0], r1r.at[0])

    def sum1(q, carry):
        total = rs1[0, q].astype(F32)
        for t in range(1, nx):
            total = total + rs1[t, q].astype(F32)
        k = 9 * (lax.div(q, 3) % 3) + 3 * lax.div(q, 9) + q % 3
        qf[pl.ds(k, wide_o, stride=32), :] = total
        return carry

    lax.fori_loop(0, 27, sum1, 0)
    qb[...] = qf[...].astype(BF)
    deep = 32 * wide_o // ntz

    hop2 = []
    for j in range(1, zgroup):
        g, z, dev = z_peer(j)
        src = qb.at[pl.ds(pl.multiple_of(z * deep, 16), deep), :]
        hop2.append(remote(src, rs2.at[me], r2s.at[0], r2r.at[0], dev))
    for copy in hop2:
        copy.start()
    rs2[me] = qb[pl.ds(pl.multiple_of(tz * deep, 16), deep), :]

    arrived(gath, nty - 1, a3s.at[0], a3r.at[0])
    fpart[...] = gath[...].reshape(192, 128)
    for a in range(3):
        planes = [(xo, xo + a - 1) for xo in range(2) if 0 <= xo + a - 1 < 2]
        for b in range(3):
            for cc in range(3):
                k = 9 * a + 3 * b + cc
                one, two = None, None
                for xo, xi in planes:
                    first = 32 * cc + 16 * xo
                    lanes = slice(32 * b + 16 * xi, 32 * b + 16 * xi + 16)
                    part = fpart[first : first + 16, lanes]
                    one = part if one is None else one + part
                    first = 96 + 32 * b + 16 * xi
                    lanes = slice(32 * cc + 16 * xo, 32 * cc + 16 * xo + 16)
                    part = fpart[first : first + 16, lanes]
                    two = part if two is None else two + part
                g_gf[k] = one
                g_gs[26 - k] = two
    for n, (src, mid, dst) in enumerate(((g_gf, t_gf, o_gf), (g_gs, t_gs, o_gs))):
        for o in range(16):
            mid[o] = src[:, o, :].T
        stores.append(pltpu.make_async_copy(mid, dst, ws.at[2 + n]))
        stores[2 + n].start()

    arrived(rs2, zgroup - 1, r2s.at[0], r2r.at[0])
    total = rs2[0].astype(F32)
    for t in range(1, zgroup):
        total = total + rs2[t].astype(F32)
    for o in range(wide_o // ntz):
        g_gc[:, o, :] = total[32 * o : 32 * o + 27, :]
    stores.append(pltpu.make_async_copy(g_gc, o_gc, ws.at[4]))
    stores[4].start()
    for copy in stores:
        copy.wait()


def finish(*refs):
    srcs, dsts, mids, sems = refs[:5], refs[5:10], refs[10:15], refs[15]
    pieces = [(0, pl.ds(8 * q, 8)) for q in range(4)] + [(3, pl.ds(512 * q, 512)) for q in range(2)]
    pieces += [(n, pl.ds(0, srcs[n].shape[0])) for n in (1, 2, 4)]
    into, out = [], []
    for q, (n, rows) in enumerate(pieces):
        into.append(pltpu.make_async_copy(srcs[n].at[rows], mids[n].at[rows], sems.at[0, q]))
        out.append(pltpu.make_async_copy(mids[n].at[rows], dsts[n].at[rows], sems.at[1, q]))
        into[q].start()
    for q in range(len(pieces)):
        into[q].wait()
        out[q].start()
    for copy in out:
        copy.wait()


def solution(mesh):
    sizes = tuple(mesh.shape[a] for a in ("dp", "ty", "tz"))
    ndp, nty, ntz = sizes
    zgroup = ndp * ntz
    wide_o, nx = 128 // nty, nty // 2
    slab = 192 // nty

    def per_device(fine_input, fine_cotangent, first_weight, second_weight, coarse_input, coarse_cotangent, coarse_weight):
        def by_offset(w):
            return w.transpose(1, 2, 0).reshape(256, 27)

        dma = pltpu.SemaphoreType.DMA
        scratch = [
            pltpu.VMEM((32, 64, 128), BF),
            pltpu.VMEM((32, 64, 128), BF),
            pltpu.VMEM((256, 27), BF),
            pltpu.VMEM((256, 27), BF),
            pltpu.VMEM((1024, 128), BF),
            pltpu.VMEM((1024, 128), BF),
            pltpu.VMEM((3456, 128), BF),
            pltpu.VMEM((512, 512), BF),
            pltpu.VMEM((128, 256), BF),
            pltpu.VMEM((3, ROWS, 256), BF),
            pltpu.VMEM((3, ROWS, 256), BF),
            pltpu.VMEM((3, ROWS, 256), BF),
            pltpu.VMEM((1024, 256), BF),
            pltpu.VMEM((3, 3, 128, 256), BF),
            pltpu.VMEM((2, 64, 128), BF),
            pltpu.VMEM((2, 64, 128), BF),
            pltpu.VMEM((2, 32, 128), BF),
            pltpu.VMEM((2, 32, 128), BF),
            pltpu.VMEM((2, 2, 32, 128), BF),
            pltpu.VMEM((2, 128, 128), BF),
            pltpu.VMEM((2, 128, 128), BF),
            pltpu.VMEM((2, 128, 128), BF),
            pltpu.VMEM((2, 128, 128), BF),
            pltpu.VMEM((2, 2, 16, 128), BF),
            pltpu.VMEM((2, 2, 16, 128), BF),
            pltpu.VMEM((2, 32, 128), BF),
            pltpu.VMEM((2, 32, 128), BF),
            pltpu.VMEM((2, 16, 128), BF),
            pltpu.VMEM((2, 16, 128), BF),
            pltpu.VMEM((2, 2, 16, 128), BF),
            pltpu.VMEM((1280, 128), F32),
            pltpu.VMEM((1280, 128), F32),
            pltpu.VMEM((1280, 128), F32),
            pltpu.VMEM((18, 64, 1152), BF),
            pltpu.VMEM((1152, 384), BF),
            pltpu.VMEM((27, nx, 2, wide_o, 128), BF),
            pltpu.VMEM((27, nx, wide_o, 128), BF),
            pltpu.VMEM((27, nx, wide_o, 128), BF),
            pltpu.VMEM((nx, 27, wide_o, 128), BF),
            pltpu.VMEM((32 * wide_o, 128), F32),
            pltpu.VMEM((32 * wide_o, 128), BF),
            pltpu.VMEM((zgroup, 32 * wide_o // ntz, 128), BF),
            pltpu.VMEM((1024, 128), BF),
            pltpu.VMEM((32, 64, 128), BF),
            pltpu.VMEM((27, 16, 16), F32),
            pltpu.VMEM((27, 16, 16), F32),
            pltpu.VMEM((16, 16, 27), F32),
            pltpu.VMEM((16, 16, 27), F32),
            pltpu.VMEM((27, wide_o // ntz, 128), F32),
            pltpu.VMEM((3, 128, 256), F32),
            pltpu.VMEM((3, 192, 128), F32),
            pltpu.VMEM((192, 128), F32),
            pltpu.VMEM((nty, slab, 128), F32),
            pltpu.VMEM((slab, 128), F32),
            pltpu.VMEM((zgroup, slab, 128), F32),
            pltpu.VMEM((slab, 128), F32),
            pltpu.VMEM((nty, slab, 128), F32),
            dma((7,)),
            dma((8,)),
            dma((8,)),
            dma((8,)),
            dma((8,)),
            dma((3,)),
            dma((3,)),
            dma((8,)),
            dma((8,)),
            dma((1,)),
            dma((1,)),
            dma((1,)),
            dma((1,)),
            dma((1,)),
            dma((1,)),
            dma((1,)),
            dma((1,)),
            dma((1,)),
            dma((1,)),
            dma((5,)),
        ]
        outs = pl.pallas_call(
            functools.partial(kernel, sizes),
            out_shape=(
                jax.ShapeDtypeStruct((32, 64, 128), BF),
                jax.ShapeDtypeStruct((16, 16, 27), F32),
                jax.ShapeDtypeStruct((16, 16, 27), F32),
                jax.ShapeDtypeStruct((1024, 128), BF),
                jax.ShapeDtypeStruct((27, wide_o // ntz, 128), F32),
            ),
            in_specs=[pl.BlockSpec(memory_space=pl.ANY)] * 7,
            out_specs=(pl.BlockSpec(memory_space=pl.ANY),) * 5,
            scratch_shapes=scratch,
            compiler_params=pltpu.CompilerParams(
                collective_id=0, has_side_effects=True, vmem_limit_bytes=60 * 1024 * 1024
            ),
        )(
            fine_input.reshape(32, 64, 128),
            fine_cotangent.reshape(32, 64, 128),
            by_offset(first_weight),
            by_offset(second_weight),
            coarse_input.reshape(1024, 128),
            coarse_cotangent.reshape(1024, 128),
            coarse_weight.reshape(3456, 128),
        )
        far = pl.BlockSpec(memory_space=pl.ANY)
        outs = pl.pallas_call(
            finish,
            out_shape=(
                jax.ShapeDtypeStruct((32, 64, 128), BF),
                jax.ShapeDtypeStruct((16, 16, 27), F32),
                jax.ShapeDtypeStruct((16, 16, 27), F32),
                jax.ShapeDtypeStruct((1024, 128), BF),
                jax.ShapeDtypeStruct((27, wide_o // ntz, 128), F32),
            ),
            in_specs=[far] * 5,
            out_specs=(far,) * 5,
            scratch_shapes=[
                pltpu.VMEM((32, 64, 128), BF),
                pltpu.VMEM((16, 16, 27), F32),
                pltpu.VMEM((16, 16, 27), F32),
                pltpu.VMEM((1024, 128), BF),
                pltpu.VMEM((27, wide_o // ntz, 128), F32),
                dma((2, 9)),
            ],
            compiler_params=pltpu.CompilerParams(vmem_limit_bytes=60 * 1024 * 1024),
        )(*outs)
        return (
            outs[0].reshape(fine_input.shape),
            outs[1].transpose(2, 0, 1),
            outs[2].transpose(2, 0, 1),
            outs[3].reshape(coarse_input.shape),
            outs[4].transpose(1, 0, 2),
        )

    fine = P("dp", None, None, "ty", "tz")
    wide = P("dp", None, "ty", "tz", None)
    return jax.shard_map(
        per_device,
        mesh=mesh,
        in_specs=(fine, fine, P(), P(), wide, wide, P()),
        out_specs=(fine, P(), P(), wide, P(("ty", "tz"), None, None)),
        check_vma=False,
    )
```
